128 devices in a mesh: slab: 8 (over y, z_lo), shot: 16 (over x, z_hi, core).
Axes of the slice: x: 4, y: 4, z: 4 (z_hi: 2, z_lo: 2; z = z_hi * 2 + z_lo), core: 2. Of those that a mesh axis runs over, the one named last changes fastest.
Arguments:
- forward_state: float32 [16, 9, 5, 5, 5, 2048], P('shot', None, None, None, None, 'slab'), may hold values from -6 to 6
- adjoint_state: float32 [16, 9, 5, 5, 5, 2048], P('shot', None, None, None, None, 'slab'), may hold values from -6 to 6
- materials: float32 [3, 5, 5, 5, 2048], P(None, None, None, None, 'slab'), may hold values from 0.5 to 2
- plane_neighbours: int32 [256, 4], replicated, may hold values from 0 to 255, as said below
- source_element: int32 [16], P('shot'), may hold values from 0 to 2047
- source_pulse: float32 [16, 2, 3], P('shot'), may hold values from -6 to 6
- receiver_elements: int32 [256], replicated, may hold values from 0 to 2047
- receiver_residuals: float32 [16, 2, 3, 256], P('shot'), may hold values from -6 to 6
Outputs:
- gradient: float32 [3, 5, 5, 5, 2048], P(None, None, None, None, ('slab', 'shot'))
- adjoint_end: float32 [16, 9, 5, 5, 5, 2048], P('shot', None, None, None, None, 'slab')
The draws below stay inside these ranges and needn't reach their ends.
Inputs may be any that keep to these rules, and one draw needn't show every extreme that they name: `plane_neighbours`: the plane positions are the cells of a periodic 16 x 16 grid in some numbering; columns 0 and 1 give a position's lower and upper neighbours along y, columns 2 and 3 along z, and the two of a pair are inverse to each other.
All inputs are finite; a program needn't handle non-finite values.
Results may differ from the reference program's by a relative error of at most 0.0003.
Values sent between devices are 32-bit elements; how exact they have to be, the bound alone decides.
No kernel may reach another device: no remote copies, remote signals or barrier semaphores. Data moves between devices by JAX's collectives and lax.ppermute only.
A program may use at most 128 MiB of HBM per device.

```python
import math
import jax
import jax.numpy as jnp
import numpy as np
from jax import lax

NODES = 5
FIELDS = 9
EY = 16
EZ = 16
STEPS = 2
RECEIVERS = 256
LAYERS = 8
PLANE = 256
ELEMS = 2048
SHOTS = 16


def draw_plane_neighbours(key, part):
    numbering = jax.random.permutation(key, EY * EZ)
    cell_index = jnp.arange(EY * EZ)
    row_index = cell_index // EZ
    col_index = cell_index % EZ

    def number_at(row_value, col_value):
        return numbering[row_value % EY * EZ + col_value % EZ]
    columns = jnp.stack([number_at(row_index - 1, col_index), number_at(row_index + 1, col_index), number_at(row_index, col_index - 1), number_at(row_index, col_index + 1)], axis=1).astype(jnp.int32)
    return jnp.zeros((EY * EZ, 4), jnp.int32).at[numbering].set(columns)


def set_ends(entries, stream_key, low, largest):
    index_at = [jax.random.randint(jax.random.fold_in(stream_key, axis), (), 0, length) for axis, length in enumerate(entries.shape)]
    widest = entries.shape.index(max(entries.shape))
    neighbour = index_at[:widest] + [(index_at[widest] + 1) % entries.shape[widest]] + index_at[widest + 1:]
    return entries.at[tuple(index_at)].set(low).at[tuple(neighbour)].set(largest)


def block_scale(key, dims, shards, smallest, largest):
    level = 1.0
    for dim, shards_of in shards:
        heights = jax.random.uniform(jax.random.fold_in(jax.random.fold_in(key, 6), dim), (shards_of,), jnp.float32, smallest / len(shards), largest / len(shards))
        level = level * jnp.repeat(jnp.exp(heights), dims[dim] // shards_of).reshape((-1,) + (1,) * (len(dims) - 1 - dim))
    return level


def normal_values(key, shape, deviation, most, pieces=(), held_as=jnp.bfloat16):
    result = deviation * jax.random.normal(key, shape, jnp.float32)
    if pieces:
        result = result * block_scale(key, shape, pieces, -0.22, 0.18)
    return jnp.clip(result, -most, most).astype(held_as)


def setup_inputs(seed: int = 0) -> dict:
    arg_keys = jax.random.split(jax.random.key(seed), 9)
    return {
        "forward_state": normal_values(arg_keys[0], (SHOTS, FIELDS, NODES, NODES, NODES, ELEMS), 1.0, 6.0, ((0, 16), (5, 8)), jnp.float32),
        "adjoint_state": normal_values(arg_keys[1], (SHOTS, FIELDS, NODES, NODES, NODES, ELEMS), 1.0, 6.0, ((0, 16), (5, 8)), jnp.float32),
        "materials": jnp.clip(jnp.exp(math.log(2.0) - 1.3862944 * jax.random.uniform(arg_keys[2], (3, NODES, NODES, NODES, ELEMS), jnp.float32) ** block_scale(arg_keys[2], (3, NODES, NODES, NODES, ELEMS), ((4, 8),), -0.2, 0.2)), 0.5, 2.0),
        "plane_neighbours": draw_plane_neighbours(jax.random.fold_in(arg_keys[8], 71), 0),
        "source_element": set_ends(jax.random.randint(arg_keys[4], (SHOTS,), 0, ELEMS), jax.random.fold_in(arg_keys[4], 1), 0, ELEMS - 1).astype(jnp.int32),
        "source_pulse": normal_values(arg_keys[5], (SHOTS, STEPS, 3), 1.0, 6.0, ((0, 16),), jnp.float32),
        "receiver_elements": set_ends(jax.random.randint(arg_keys[6], (RECEIVERS,), 0, ELEMS), jax.random.fold_in(arg_keys[6], 1), 0, ELEMS - 1).astype(jnp.int32),
        "receiver_residuals": normal_values(arg_keys[7], (SHOTS, STEPS, 3, RECEIVERS), 1.0, 6.0, ((0, 16),), jnp.float32),
    }


time_step = 0.01
lift_gain = 10.0
stress_columns = ((3, 8, 7), (8, 4, 6), (7, 6, 5))

def gll_tables():
    root = math.sqrt(3.0 / 7.0)
    points = np.array([-1.0, -root, 0.0, root, 1.0])
    legendre = (35.0 * points ** 4 - 30.0 * points ** 2 + 3.0) / 8.0
    matrix = np.zeros((5, 5))
    for row_index in range(5):
        for col_index in range(5):
            if row_index != col_index:
                matrix[row_index, col_index] = legendre[row_index] / (legendre[col_index] * (points[row_index] - points[col_index]))
    matrix[0, 0] = -5.0
    matrix[4, 4] = 5.0
    quadrature = np.array([0.1, 49.0 / 90.0, 32.0 / 45.0, 49.0 / 90.0, 0.1])
    volume = quadrature[:, None, None] * quadrature[None, :, None] * quadrature[None, None, :]
    return (jnp.asarray(matrix, jnp.float32), jnp.asarray(volume, jnp.float32))

def node_derivative(wavefield, direction, derivative_table):
    einsum_forms = ('ia,zkabcuv->zkibcuv', 'ib,zkabcuv->zkaicuv', 'ic,zkabcuv->zkabiuv')
    return jnp.einsum(einsum_forms[direction], derivative_table, wavefield, precision=lax.Precision.HIGHEST)

def face_of(wavefield, direction, position):
    return lax.index_in_dim(wavefield, position, 2 + direction, keepdims=False)

def add_on_face(target, direction, position, addend):
    location = (slice(None),) * (2 + direction) + (position,)
    return target.at[location].add(addend)

def jump_derivative(wavefield, direction, minus_side, plus_side, derivative_table):
    grown = node_derivative(wavefield, direction, derivative_table)
    grown = add_on_face(grown, direction, 0, -0.5 * lift_gain * (minus_side - face_of(wavefield, direction, 0)))
    grown = add_on_face(grown, direction, 4, 0.5 * lift_gain * (plus_side - face_of(wavefield, direction, 4)))
    return grown

def neighbours_along(wavefield, direction, plane_neighbours, x_sides):
    if direction == 0:
        return x_sides(face_of(wavefield, 0, 4), face_of(wavefield, 0, 0))
    lower_column = 2 * direction - 2
    minus_side = jnp.take(face_of(wavefield, direction, 4), plane_neighbours[:, lower_column], axis=-1)
    plus_side = jnp.take(face_of(wavefield, direction, 0), plane_neighbours[:, lower_column + 1], axis=-1)
    return (minus_side, plus_side)

def leap_step(wavefield, shaped, plane_neighbours, inject, derivative_table, x_sides):
    lame_first = shaped[0]
    shear = shaped[1]
    density = shaped[2]
    summed = None
    for direction in range(3):
        subset = wavefield[:, list(stress_columns[direction])]
        minus_side, plus_side = neighbours_along(subset, direction, plane_neighbours, x_sides)
        contribution = jump_derivative(subset, direction, minus_side, plus_side, derivative_table)
        summed = contribution if summed is None else summed + contribution
    acceleration = summed / density
    velocity = wavefield[:, 0:3] + time_step * acceleration
    velocity = velocity.at[:, :, 2, 2, 2].add(inject)
    gradients = []
    for direction in range(3):
        minus_side, plus_side = neighbours_along(velocity, direction, plane_neighbours, x_sides)
        gradients.append(jump_derivative(velocity, direction, minus_side, plus_side, derivative_table))
    divergence = gradients[0][:, 0] + gradients[1][:, 1] + gradients[2][:, 2]
    stress_rates = jnp.stack([lame_first * divergence + 2.0 * shear * gradients[0][:, 0], lame_first * divergence + 2.0 * shear * gradients[1][:, 1], lame_first * divergence + 2.0 * shear * gradients[2][:, 2], shear * (gradients[2][:, 1] + gradients[1][:, 2]), shear * (gradients[2][:, 0] + gradients[0][:, 2]), shear * (gradients[1][:, 0] + gradients[0][:, 1])], axis=1)
    stress = wavefield[:, 3:] + time_step * stress_rates
    return (jnp.concatenate([velocity, stress], axis=1), acceleration)

def image_terms(forward, adjoint, acceleration, derivative_table, volume_weights):
    forward_grad = [node_derivative(forward[:, 0:3], direction, derivative_table) for direction in range(3)]
    adjoint_grad = [node_derivative(adjoint[:, 0:3], direction, derivative_table) for direction in range(3)]
    forward_trace = forward_grad[0][:, 0] + forward_grad[1][:, 1] + forward_grad[2][:, 2]
    adjoint_trace = adjoint_grad[0][:, 0] + adjoint_grad[1][:, 1] + adjoint_grad[2][:, 2]
    strain_product = forward_grad[0][:, 0] * adjoint_grad[0][:, 0]
    strain_product = strain_product + forward_grad[1][:, 1] * adjoint_grad[1][:, 1]
    strain_product = strain_product + forward_grad[2][:, 2] * adjoint_grad[2][:, 2]
    for outer_index, inner_index in ((0, 1), (0, 2), (1, 2)):
        forward_sym = forward_grad[inner_index][:, outer_index] + forward_grad[outer_index][:, inner_index]
        adjoint_sym = adjoint_grad[inner_index][:, outer_index] + adjoint_grad[outer_index][:, inner_index]
        strain_product = strain_product + 0.5 * forward_sym * adjoint_sym
    inertia = acceleration[:, 0] * adjoint[:, 0] + acceleration[:, 1] * adjoint[:, 1] + acceleration[:, 2] * adjoint[:, 2]
    stacked = jnp.stack([forward_trace * adjoint_trace, 2.0 * strain_product, inertia], axis=1)
    return lax.optimization_barrier(jnp.sum(stacked, axis=0)) * volume_weights[:, :, :, None, None]

def reference(forward_state, adjoint_state, materials, plane_neighbours, source_element, source_pulse, receiver_elements, receiver_residuals):
    derivative_table, volume_weights = gll_tables()
    shaped = materials.reshape(3, 5, 5, 5, LAYERS, PLANE)
    element_ids = jnp.arange(ELEMS, dtype=jnp.int32)
    receiver_hits = (receiver_elements[:, None] == element_ids[None, :]).astype(jnp.float32)

    def x_sides(high_face, low_face):
        return (jnp.roll(high_face, 1, axis=-2), jnp.roll(low_face, -1, axis=-2))

    def one_shot(carried, inputs):
        forward_start, adjoint_start, source_index, pulses, residuals = inputs
        source_hits = (element_ids == source_index).astype(jnp.float32)
        forward_now = forward_start.reshape(1, FIELDS, 5, 5, 5, LAYERS, PLANE)
        forward_list = []
        accel_list = []
        for step_index in range(STEPS):
            inject = (pulses[step_index][:, None] * source_hits[None, :]).reshape(1, 3, LAYERS, PLANE)
            forward_now, acceleration = leap_step(forward_now, shaped, plane_neighbours, inject, derivative_table, x_sides)
            forward_list.append(forward_now)
            accel_list.append(acceleration)
        adjoint_now = adjoint_start.reshape(1, FIELDS, 5, 5, 5, LAYERS, PLANE)
        gradient = image_terms(forward_list[STEPS - 1], adjoint_now, accel_list[STEPS - 1], derivative_table, volume_weights)
        for step_index in range(STEPS):
            placed = jnp.dot(residuals[step_index], receiver_hits, precision=lax.Precision.HIGHEST)
            inject = placed.reshape(1, 3, LAYERS, PLANE)
            adjoint_now, unused_accel = leap_step(adjoint_now, shaped, plane_neighbours, inject, derivative_table, x_sides)
            time_index = STEPS - 2 - step_index
            if time_index >= 0:
                gradient = gradient + image_terms(forward_list[time_index], adjoint_now, accel_list[time_index], derivative_table, volume_weights)
        return (carried + gradient, adjoint_now.reshape(FIELDS, 5, 5, 5, ELEMS))
    start = jnp.zeros((3, 5, 5, 5, LAYERS, PLANE), jnp.float32)
    gradient, adjoint_end = lax.scan(one_shot, start, (forward_state, adjoint_state, source_element, source_pulse, receiver_residuals))
    return (gradient.reshape(3, 5, 5, 5, ELEMS), adjoint_end)
```

```python
import math

import jax
import jax.numpy as jnp
import numpy as np
from jax import lax
from jax.experimental import pallas as pl
from jax.experimental.pallas import tpu as pltpu
from jax.sharding import PartitionSpec as P

f32 = jnp.float32
bf16 = jnp.bfloat16

time_step = 0.01
N = 256
STATE = (1, 9, 5, 5, 5, N)


def tables():
    root = math.sqrt(3.0 / 7.0)
    points = np.array([-1.0, -root, 0.0, root, 1.0])
    legendre = (35.0 * points**4 - 30.0 * points**2 + 3.0) / 8.0
    matrix = np.zeros((5, 5))
    for r in range(5):
        for c in range(5):
            if r != c:
                matrix[r, c] = legendre[r] / (legendre[c] * (points[r] - points[c]))
    matrix[0, 0] = -5.0
    matrix[4, 4] = 5.0
    quad = np.array([0.1, 49.0 / 90.0, 32.0 / 45.0, 49.0 / 90.0, 0.1])
    return matrix, quad


D_PLAIN, QUAD = tables()
D_LIFT = D_PLAIN.copy()
D_LIFT[0, 0] += 5.0
D_LIFT[4, 4] -= 5.0


def block_table(matrix):
    small = np.zeros((8, 8))
    small[:5, :5] = matrix
    whole = np.kron(np.eye(25), small).astype(np.float32)
    high = whole.astype(jnp.bfloat16)
    low = (whole - high.astype(np.float32)).astype(jnp.bfloat16)
    return np.stack([high, low])


def split(x):
    high = x.astype(bf16)
    return high, (x - high.astype(f32)).astype(bf16)


def dot(a, b):
    return lax.dot_general(a, b, (((1,), (0,)), ((), ())), preferred_element_type=f32)


def derive_rows(rows, matrix):
    even0, odd0 = rows[0] + rows[4], rows[0] - rows[4]
    even1, odd1 = rows[1] + rows[3], rows[1] - rows[3]
    out = [None] * 5
    for r in (0, 1):
        m = [float(v) for v in matrix[r]]
        p = 0.5 * (m[0] + m[4]) * even0 + 0.5 * (m[1] + m[3]) * even1 + m[2] * rows[2]
        q = 0.5 * (m[0] - m[4]) * odd0 + 0.5 * (m[1] - m[3]) * odd1
        out[r] = q + p
        out[4 - r] = q - p
    out[2] = float(matrix[2, 0]) * odd0 + float(matrix[2, 1]) * odd1
    return out


def derive_x(x, matrix):
    return jnp.stack(derive_rows([x[k] for k in range(5)], matrix), axis=0)


def derive_y(x, matrix):
    return jnp.stack(derive_rows([x[:, k] for k in range(5)], matrix), axis=1)


def derive_z(x, table):
    high, low = split(x.reshape(200, N))
    y = dot(table[0], high) + dot(table[0], low) + dot(table[1], high)
    return y.reshape(5, 5, 8, N)


def fill(dst, k, value):
    dst[k, :, :, 0:5, :] = value


def zero_pads(dst, count, value=0.0):
    for k in range(count):
        dst[k, :, :, 5:8, :] = jnp.full((5, 5, 3, N), value, f32)


def make_perms(nbr, perms):
    lane = lax.broadcasted_iota(jnp.int32, (N, N), 1)
    for k in range(4):
        sign = 5.0 if k % 2 == 0 else -5.0
        hit = nbr[:, k : k + 1] == lane
        perms[k] = jnp.where(hit, sign, 0.0).astype(bf16)


def permuted(face, matrix):
    high, low = split(face)
    return dot(high, matrix) + dot(low, matrix)


def jump_y(x, perms):
    at_low = permuted(x[:, 4].reshape(40, N), perms[1]).reshape(5, 8, N)
    at_high = permuted(x[:, 0].reshape(40, N), perms[0]).reshape(5, 8, N)
    return at_low, at_high


def jump_z(x, perms):
    rows = lax.broadcasted_iota(jnp.int32, (5, 5, 8, N), 2)
    turned = pltpu.roll(x.reshape(25, 8, N), 4, 1).reshape(5, 5, 8, N)
    down = jnp.where(rows == 0, turned, 0.0).reshape(200, N)
    up = jnp.where(rows == 4, turned, 0.0).reshape(200, N)
    return (permuted(down, perms[3]) + permuted(up, perms[2])).reshape(5, 5, 8, N)


def stress_of(i, d):
    return jnp.where(i == d, i, 6 - i - d)


def local_acceleration(stress, rinv, acc, table, perms):
    def one(i, carry):
        sx, sy, sz = stress[stress_of(i, 0)], stress[stress_of(i, 1)], stress[stress_of(i, 2)]
        total = derive_z(sz, table) + jump_z(sz, perms)
        total = total + derive_x(sx, D_LIFT)
        total = total + derive_y(sy, D_LIFT)
        acc[i] = total
        at_low, at_high = jump_y(sy, perms)
        acc[i, :, 0] += at_low
        acc[i, :, 4] += at_high
        acc[i] = acc[i] * rinv[...]
        return carry

    lax.fori_loop(0, 3, one, 0)


def pack_face(dst, k, value):
    for b in range(5):
        dst[k * 25 + 5 * b : k * 25 + 5 * b + 5, :] = value[b, 0:5]


def unpack_face(dst, k, src, j):
    for b in range(5):
        dst[k, b, 0:5, :] = src[j * 25 + 5 * b : j * 25 + 5 * b + 5, :]


def load_stress(state, stress):
    zero_pads(stress, 6)
    for k in range(6):
        fill(stress, k, state[0, 3 + k])


def load_material(mat, dst, k, pad):
    dst[:, :, 5:8, :] = jnp.full((5, 5, 3, N), pad, f32)
    dst[:, :, 0:5, :] = mat[k]


def inject_rows(kind, step, refs, base):
    if kind == "source":
        where_ref, pulse = refs
        lane = lax.broadcasted_iota(jnp.int32, (1, N), 1) + base
        hit = lane == where_ref[0]
        return [jnp.where(hit, pulse[0, step, i], 0.0) for i in range(3)]
    where_ref, residual = refs
    element = lax.broadcasted_iota(jnp.int32, (N, N), 0) + base
    hits = jnp.where(element == where_ref[...], 1.0, 0.0).astype(bf16)
    x = jnp.concatenate([residual[0, step], jnp.zeros((5, N), f32)], axis=0)
    total = None
    for part in range(3):
        high = x.astype(bf16)
        x = x - high.astype(f32)
        term = lax.dot_general(high, hits, (((1,), (1,)), ((), ())), preferred_element_type=f32)
        total = term if total is None else total + term
    return [total[i : i + 1] for i in range(3)]


def pack_sends(stress, acc, velocity, injected, rinv, up, down, first, with_v, with_r):
    for dst, a in ((up, 4), (down, 0)):
        for i in range(3):
            pack_face(dst, first + i, stress[(0, 5, 4)[i], a])
        if with_v:
            for i in range(3):
                pack_face(dst, first + 3 + i, velocity(i, a) + time_step * acc[i, a])
        if with_r:
            pack_face(dst, first + 6, 0.05 * rinv[a])


def start_kernel(fwd, adj, mat, nbr, table, f_up, f_down, a_up, a_down, f_acc, a_acc, stress, rinv, perms, vel):
    make_perms(nbr, perms)
    load_material(mat, rinv, 2, 1.0)
    rinv[...] = 1.0 / rinv[...]
    for state, acc, up, down, with_r in ((fwd, f_acc, f_up, f_down, True), (adj, a_acc, a_up, a_down, False)):
        load_stress(state, stress)
        local_acceleration(stress, rinv, acc, table, perms)
        vel[:, :, :, 5:8, :] = jnp.zeros((3, 2, 5, 3, N), f32)
        for i in range(3):
            vel[i, 0, :, 0:5, :] = state[0, i, 0]
            vel[i, 1, :, 0:5, :] = state[0, i, 4]
        pack_sends(
            stress, acc, lambda i, a: vel[i, a // 4], None, rinv, up, down, 0, True, with_r
        )


def finish_acceleration(acc, stress, rinv, halo, has_v):
    for i in range(3):
        k = (0, 5, 4)[i]
        acc[i, 0] = acc[i, 0] - 5.0 * rinv[0] * halo[0, i]
        acc[i, 4] = acc[i, 4] + 5.0 * rinv[4] * halo[1, i]
        if has_v:
            halo[0, 3 + i] = halo[0, 3 + i] + halo[0, 6] * stress[k, 0]
            halo[1, 3 + i] = halo[1, 3 + i] - halo[1, 6] * stress[k, 4]


def velocities(vel, acc, rows):
    mask = lax.broadcasted_iota(jnp.int32, (8, N), 0) == 2
    for i in range(3):
        vel[i] = vel[i] + time_step * acc[i]
        vel[i, 2, 2] = vel[i, 2, 2] + jnp.where(mask, rows[i], 0.0)


def jump_gradients(vel, halo, grads, table, perms):
    def one(i, carry):
        v = vel[i]
        gx = derive_x(v, D_LIFT)
        grads[i] = gx
        grads[i, 0] += -5.0 * halo[0, 3 + i]
        grads[i, 4] += 5.0 * halo[1, 3 + i]
        at_low, at_high = jump_y(v, perms)
        grads[3 + i] = derive_y(v, D_LIFT)
        grads[3 + i, :, 0] += at_low
        grads[3 + i, :, 4] += at_high
        grads[6 + i] = derive_z(v, table) + jump_z(v, perms)
        return carry

    lax.fori_loop(0, 3, one, 0)


def update_stress(stress, grads, lam, mu):
    def one(a, carry):
        g = lambda j, i: grads[3 * j + i, a]
        l, m = time_step * lam[a], time_step * mu[a]
        both = l * (g(0, 0) + g(1, 1) + g(2, 2))
        for i in range(3):
            stress[i, a] = stress[i, a] + (both + 2.0 * m * g(i, i))
        stress[3, a] = stress[3, a] + m * (g(2, 1) + g(1, 2))
        stress[4, a] = stress[4, a] + m * (g(2, 0) + g(0, 2))
        stress[5, a] = stress[5, a] + m * (g(1, 0) + g(0, 1))
        return carry

    lax.fori_loop(0, 5, one, 0)


def plain_gradients(vel, grads, table):
    def one(i, carry):
        v = vel[i]
        grads[i] = derive_x(v, D_PLAIN)
        grads[3 + i] = derive_y(v, D_PLAIN)
        grads[6 + i] = derive_z(v, table)
        return carry

    lax.fori_loop(0, 3, one, 0)


def load_halo(halo, below, above, plan, r_from):
    halo[:, :, :, 5:8, :] = jnp.zeros((2, 7, 5, 3, N), f32)
    for side, src in ((0, below), (1, above)):
        for slot, face in plan:
            unpack_face(halo.at[side], slot, src, face)
        if r_from is not None:
            unpack_face(halo.at[side], 6, r_from[side], 6)


def first_step_kernel(kind, base, state, mat, nbr, table, where_ref, strength, acc_in, below, above, r_below, r_above,
                      vel_out, stress_out, acc_out, next_acc, up, down,
                      rinv, lam, mu, halo, grads, perms):
    make_perms(nbr, perms)
    load_material(mat, rinv, 2, 1.0)
    rinv[...] = 1.0 / rinv[...]
    load_material(mat, lam, 0, 0.0)
    load_material(mat, mu, 1, 0.0)
    load_halo(halo, below, above, [(k, k) for k in range(6)], (r_below, r_above))
    load_stress(state, stress_out)
    zero_pads(vel_out, 3)
    for i in range(3):
        fill(vel_out, i, state[0, i])
    acc_out[...] = acc_in[...]
    finish_acceleration(acc_out, stress_out, rinv, halo, True)
    offset = base[0]
    velocities(vel_out, acc_out, inject_rows(kind, 0, (where_ref, strength), offset))
    jump_gradients(vel_out, halo, grads, table, perms)
    update_stress(stress_out, grads, lam, mu)
    local_acceleration(stress_out, rinv, next_acc, table, perms)
    adjoint = kind == "receiver"
    pack_sends(stress_out, next_acc, lambda i, a: vel_out[i, a], None, rinv, up, down, 0, adjoint, False)


def last_step_kernel(base, vel_in, stress_in, mat, nbr, table, where_ref, strength, acc_in, below, above, r_below, r_above,
                     out, rinv, lam, mu, halo, grads, perms, vel, stress, acc):
    make_perms(nbr, perms)
    load_material(mat, rinv, 2, 1.0)
    rinv[...] = 1.0 / rinv[...]
    load_material(mat, lam, 0, 0.0)
    load_material(mat, mu, 1, 0.0)
    load_halo(halo, below, above, [(k, k) for k in range(6)], (r_below, r_above))
    acc[...] = acc_in[...]
    vel[...] = vel_in[...]
    stress[...] = stress_in[...]
    finish_acceleration(acc, stress, rinv, halo, True)
    velocities(vel, acc, inject_rows("receiver", 1, (where_ref, strength), base[0]))
    jump_gradients(vel, halo, grads, table, perms)
    update_stress(stress, grads, lam, mu)
    for k in range(3):
        out[0, k] = vel[k, :, :, 0:5, :]
    for k in range(6):
        out[0, 3 + k] = stress[k, :, :, 0:5, :]


def image_kernel(base, adj, f_vel, f_acc, a_vel, mat, plain, where_ref, strength, acc_in, below, above,
                 out, rinv, halo, vel, acc, adj_vel, fg, ag, dense):
    load_material(mat, rinv, 2, 1.0)
    rinv[...] = 1.0 / rinv[...]
    load_halo(halo, below, above, [(k, k) for k in range(3)], None)
    acc[...] = acc_in[...]
    vel[...] = f_vel[...]
    finish_acceleration(acc, None, rinv, halo, False)
    velocities(vel, acc, inject_rows("source", 1, (where_ref, strength), base[0]))
    zero_pads(adj_vel, 3)
    for i in range(3):
        fill(adj_vel, i, adj[0, i])
    row = lax.broadcasted_iota(jnp.int32, (5, 8, N), 1)
    weight_c = jnp.zeros((5, 8, N), f32)
    for c in range(5):
        weight_c = jnp.where(row == c, float(QUAD[c]), weight_c)
    group = lax.broadcasted_iota(jnp.int32, (5, 8, N), 0)
    weight_b = jnp.zeros((5, 8, N), f32)
    for c in range(5):
        weight_b = jnp.where(group == c, float(QUAD[c]), weight_b)
    weight = weight_b * weight_c
    dense[368:384, :] = jnp.zeros((16, N), f32)
    for part in range(2):
        fv, av, fa = ((vel, adj_vel, acc), (f_vel, a_vel, f_acc))[part]
        plain_gradients(fv, fg, plain)
        plain_gradients(av, ag, plain)
        for a in range(5):
            f = lambda j, i: fg[3 * j + i, a]
            g = lambda j, i: ag[3 * j + i, a]
            w = weight * float(QUAD[a])
            f0, f1, f2 = f(0, 0), f(1, 1), f(2, 2)
            g0, g1, g2 = g(0, 0), g(1, 1), g(2, 2)
            first = (f0 + f1 + f2) * (g0 + g1 + g2) * w
            cross = None
            for i, j in ((0, 1), (0, 2), (1, 2)):
                term = (f(j, i) + f(i, j)) * (g(j, i) + g(i, j))
                cross = term if cross is None else cross + term
            second = (2.0 * (f0 * g0 + f1 * g1 + f2 * g2) + cross) * w
            third = (fa[0, a] * av[0, a] + fa[1, a] * av[1, a] + fa[2, a] * av[2, a]) * w
            for t, term in enumerate((first, second, third)):
                for b in range(5):
                    at = t * 125 + a * 25 + b * 5
                    if part == 0:
                        dense[at : at + 5, :] = term[b, 0:5]
                    else:
                        dense[at : at + 5, :] += term[b, 0:5]
    out[...] = dense[...].T


V = pl.BlockSpec(memory_space=pltpu.VMEM)
S = pl.BlockSpec(memory_space=pltpu.SMEM)


def field(count):
    return jax.ShapeDtypeStruct((count, 5, 5, 8, N), f32)


def sends(faces):
    return jax.ShapeDtypeStruct((faces * 25, N), f32)


def call(kernel, specs, outs, scratch, flops, moved):
    return pl.pallas_call(
        kernel,
        out_shape=outs,
        in_specs=specs,
        out_specs=jax.tree.map(lambda _: V, outs),
        scratch_shapes=scratch,
        compiler_params=pltpu.CompilerParams(vmem_limit_bytes=56 * 2**20),
        cost_estimate=pl.CostEstimate(flops=flops, bytes_accessed=moved, transcendentals=0),
    )


def scr(*shape):
    return pltpu.VMEM(shape, f32)


PERMS = pltpu.VMEM((4, N, N), bf16)
ONE = (5, 5, 8, N)


def passed_along(value, axis, steps):
    count = lax.axis_size(axis)
    pairs = [(source, (source + steps) % count) for source in range(count)]
    return lax.ppermute(value, axis, pairs)


def both_ways(up, down):
    return passed_along(up, "slab", 1), passed_along(down, "slab", -1)


def reduce_over_shots(x):
    x = x.reshape(4, 2, 2, 16, 384)
    place = lax.axis_index("shot")
    core, high, line = place % 2, (place // 2) % 2, place // 4
    pick = lambda v, k, axis: lax.dynamic_index_in_dim(v, k, axis, False)
    hop = lambda v, to: lax.ppermute(v, "shot", [(i, to(i)) for i in range(16)])
    x = pick(x, core, 2) + hop(pick(x, 1 - core, 2), lambda i: i ^ 1)
    total = pick(x, line, 0)
    for d in (1, 2, 3):
        total = total + hop(pick(x, (line + d) % 4, 0), lambda i: (i + 4 * d) % 16)
    return pick(total, high, 0) + hop(pick(total, 1 - high, 0), lambda i: i ^ 2)


def body(fwd, adj, materials, nbr, source_element, pulse, receivers, residuals):
    lift = jnp.asarray(block_table(D_LIFT))
    plain = jnp.asarray(block_table(D_PLAIN))
    base = (lax.axis_index("slab") * N).astype(jnp.int32).reshape(1)
    receivers = receivers.reshape(1, N)

    f_up, f_down, a_up, a_down, f_acc, a_acc = call(
        start_kernel,
        [V] * 5,
        (sends(7), sends(7), sends(6), sends(6), field(3), field(3)),
        [scr(6, *ONE), scr(*ONE), PERMS, scr(3, 2, 5, 8, N)],
        10**8, 4 * 10**6,
    )(fwd, adj, materials, nbr, lift)
    f_below, f_above = both_ways(f_up, f_down)
    a_below, a_above = both_ways(a_up, a_down)

    step_scratch = [scr(*ONE), scr(*ONE), scr(*ONE), scr(2, 7, 5, 8, N), scr(9, *ONE), PERMS]

    def first_step(kind, state, where_ref, strength, acc, below, above, faces):
        kernel = lambda base_ref, *refs: first_step_kernel(kind, base_ref, *refs)
        smem = S if kind == "source" else V
        return call(
            kernel,
            [S, V, V, V, V, smem, smem, V, V, V, V, V],
            (field(3), field(6), field(3), field(3), sends(faces), sends(faces)),
            step_scratch, 2 * 10**8, 10**7,
        )(base, state, materials, nbr, lift, where_ref, strength, acc, below, above, f_below, f_above)

    f_vel, _, f_acc1, f_acc2, f_up, f_down = first_step(
        "source", fwd, source_element, pulse, f_acc, f_below, f_above, 3
    )
    f_below2, f_above2 = both_ways(f_up, f_down)
    a_vel, a_stress, _, a_acc2, a_up, a_down = first_step(
        "receiver", adj, receivers, residuals, a_acc, a_below, a_above, 6
    )
    a_below2, a_above2 = both_ways(a_up, a_down)
    partial = call(
        image_kernel,
        [S, V, V, V, V, V, V, S, S, V, V, V],
        jax.ShapeDtypeStruct((N, 384), f32),
        [scr(*ONE), scr(2, 7, 5, 8, N), scr(3, *ONE), scr(3, *ONE), scr(3, *ONE), scr(9, *ONE), scr(9, *ONE), scr(384, N)],
        3 * 10**8, 10**7,
    )(base, adj, f_vel, f_acc1, a_vel, materials, plain, source_element, pulse, f_acc2, f_below2, f_above2)
    gradient = reduce_over_shots(partial)
    adjoint_end = call(
        last_step_kernel,
        [S, V, V, V, V, V, V, V, V, V, V, V, V],
        jax.ShapeDtypeStruct(STATE, f32),
        step_scratch + [scr(3, *ONE), scr(6, *ONE), scr(3, *ONE)],
        10**8, 10**7,
    )(base, a_vel, a_stress, materials, nbr, lift, receivers, residuals, a_acc2, a_below2, a_above2, f_below, f_above)
    return gradient[:, :375].T.reshape(3, 5, 5, 5, 16), adjoint_end


def solution(mesh):
    return jax.shard_map(
        body,
        mesh=mesh,
        in_specs=(
            P("shot", None, None, None, None, "slab"),
            P("shot", None, None, None, None, "slab"),
            P(None, None, None, None, "slab"),
            P(),
            P("shot"),
            P("shot", None, None),
            P(),
            P("shot", None, None, None),
        ),
        out_specs=(
            P(None, None, None, None, ("slab", "shot")),
            P("shot", None, None, None, None, "slab"),
        ),
        check_vma=False,
    )
```

```python
import math

import jax
import jax.numpy as jnp
import numpy as np
from jax import lax
from jax.experimental import pallas as pl
from jax.experimental.pallas import tpu as pltpu
from jax.sharding import PartitionSpec as P

f32 = jnp.float32
bf16 = jnp.bfloat16

time_step = 0.01
N = 256


def tables():
    root = math.sqrt(3.0 / 7.0)
    points = np.array([-1.0, -root, 0.0, root, 1.0])
    legendre = (35.0 * points**4 - 30.0 * points**2 + 3.0) / 8.0
    matrix = np.zeros((5, 5))
    for r in range(5):
        for c in range(5):
            if r != c:
                matrix[r, c] = legendre[r] / (legendre[c] * (points[r] - points[c]))
    matrix[0, 0] = -5.0
    matrix[4, 4] = 5.0
    quad = np.array([0.1, 49.0 / 90.0, 32.0 / 45.0, 49.0 / 90.0, 0.1])
    return matrix, quad


D_PLAIN, QUAD = tables()
D_LIFT = D_PLAIN.copy()
D_LIFT[0, 0] += 5.0
D_LIFT[4, 4] -= 5.0


def split(x):
    high = x.astype(bf16)
    return high, (x - high.astype(f32)).astype(bf16)


def dot(a, b):
    return lax.dot_general(a, b, (((1,), (0,)), ((), ())), preferred_element_type=f32)


def derive_rows(rows, matrix):
    even0, odd0 = rows[0] + rows[4], rows[0] - rows[4]
    even1, odd1 = rows[1] + rows[3], rows[1] - rows[3]
    out = [None] * 5
    for r in (0, 1):
        m = [float(v) for v in matrix[r]]
        p = 0.5 * (m[0] + m[4]) * even0 + 0.5 * (m[1] + m[3]) * even1 + m[2] * rows[2]
        q = 0.5 * (m[0] - m[4]) * odd0 + 0.5 * (m[1] - m[3]) * odd1
        out[r] = q + p
        out[4 - r] = q - p
    out[2] = float(matrix[2, 0]) * odd0 + float(matrix[2, 1]) * odd1
    return out


class Along:
    def __init__(self, matrix):
        row = lax.broadcasted_iota(jnp.int32, (8, 128), 0)
        self.places = [jnp.where(row < 5, lax.rem(row + m, 5), row) for m in range(1, 5)]
        self.factors = []
        for m in range(1, 5):
            self.factors.append(self.by_row(row, [matrix[c, (c + m) % 5] for c in range(5)]))
        own = [matrix[c, c] for c in range(5)]
        self.own = self.by_row(row, own) if any(own) else None

    @staticmethod
    def by_row(row, values):
        out = jnp.zeros((8, 128), f32)
        for c in range(5):
            out = jnp.where(row == c, float(values[c]), out)
        return out

    def __call__(self, tile):
        total = None if self.own is None else tile * self.own
        for place, factor in zip(self.places, self.factors):
            term = jnp.take_along_axis(tile, place, axis=0) * factor
            total = term if total is None else total + term
        return total


def flat(ref, rows):
    return ref.reshape(rows, 128)


def make_perms(nbr, perms):
    source = lax.broadcasted_iota(jnp.int32, (N, N), 0)
    for k in range(4):
        hit = source == nbr[k : k + 1, :]
        perms[k] = jnp.where(hit, -5.0 if k % 2 == 0 else 5.0, 0.0).astype(bf16)


def permuted(face, matrix):
    rows = face.shape[0]
    both = dot(jnp.concatenate(split(face), axis=0), matrix)
    return both[:rows] + both[rows:]


def jumps(field, ys, first_z, perms, yj, zj):
    count = field.shape[1]
    for side, b in ((0, 4), (1, 0)):
        face = jnp.concatenate(
            [
                jnp.concatenate([field[h, k, :, b].reshape(40, 128) for h in range(2)], axis=1)
                for k in ys
            ],
            axis=0,
        )
        got = permuted(face, perms[side])
        for h in range(2):
            for i in range(3):
                part = got[40 * i : 40 * i + 40, 128 * h : 128 * h + 128]
                yj[side, h, i] = part.reshape(5, 8, 128)
    rows = flat(field, 2 * count * 200)
    into = flat(zj, 1200)
    spare = jnp.zeros((5, N), f32)
    for side, c in ((0, 4), (1, 0)):
        face = jnp.concatenate(
            [rows[pl.ds((h * count + first_z) * 200 + c, 75, 8), :] for h in range(2)], axis=1
        )
        got = permuted(jnp.concatenate([face, spare], axis=0), perms[2 + side])
        for h in range(2):
            into[pl.ds(h * 600 + (0, 4)[side], 75, 8), :] = got[:75, 128 * h : 128 * h + 128]


def stress_of(i, d):
    return jnp.where(i == d, i, 6 - i - d)


def halves(count, one):
    def step(t, carry):
        one(lax.div(t, 2), lax.rem(t, 2))
        return carry

    lax.fori_loop(0, 2 * count, step, 0)


def local_acceleration(stress, rinv, acc, perms, yj, zj):
    along = Along(D_LIFT)
    jumps(stress, (5, 1, 3), 2, perms, yj, zj)

    def one(i, h):
        kx, ky, kz = stress_of(i, 0), stress_of(i, 1), stress_of(i, 2)
        for a in range(5):
            ys = derive_rows([stress[h, ky, a, b] for b in range(5)], D_LIFT)
            ys[0] = ys[0] + yj[0, h, i, a]
            ys[4] = ys[4] + yj[1, h, i, a]
            for b in range(5):
                acc[h, i, a, b] = ys[b] + (along(stress[h, kz, a, b]) + zj[h, 2 - i, a, b])
        for b in range(5):
            xs = derive_rows([stress[h, kx, a, b] for a in range(5)], D_LIFT)
            for a in range(5):
                acc[h, i, a, b] = (acc[h, i, a, b] + xs[a]) * rinv[h, a, b]

    halves(3, one)


def load_fields(src, first, dst, count):
    def one(k, carry):
        for g in range(25):
            for h in range(2):
                dst[h, k, g // 5, g % 5, 0:5, :] = src[pl.ds(250 * (first + k) + 10 * g + h, 5, 2), :]
        return carry

    lax.fori_loop(0, count, one, 0)


def pack_face(dst, k, value, h):
    for b in range(5):
        dst[pl.ds(50 * k + 10 * b + h, 5, 2), :] = value[b, 0:5]


def unpack_face(dst, side, k, src, j):
    for h in range(2):
        for b in range(5):
            dst[side, h, k, b, 0:5, :] = src[pl.ds(50 * j + 10 * b + h, 5, 2), :]


def load_halo(halo, below, above, r_below, r_above, count):
    for side, src in ((0, below), (1, above)):
        for k in range(count):
            unpack_face(halo, side, k, src, k)
    if r_below is not None:
        for side, src in ((0, r_below), (1, r_above)):
            unpack_face(halo, side, 6, src, 6)


def finish_acceleration(acc, stress, rinv, halo, has_v):
    for h in range(2):
        for i in range(3):
            k = (0, 5, 4)[i]
            acc[h, i, 0] = acc[h, i, 0] - 5.0 * rinv[h, 0] * halo[0, h, i]
            acc[h, i, 4] = acc[h, i, 4] + 5.0 * rinv[h, 4] * halo[1, h, i]
            if has_v:
                halo[0, h, 3 + i] = halo[0, h, 3 + i] + halo[0, h, 6] * stress[h, k, 0]
                halo[1, h, 3 + i] = halo[1, h, 3 + i] - halo[1, h, 6] * stress[h, k, 4]


def inject_rows(kind, step, where_ref, strength, base):
    if kind == "source":
        lane = lax.broadcasted_iota(jnp.int32, (1, N), 1) + base
        hit = lane == where_ref[0]
        return [jnp.where(hit, strength[0, step, i], 0.0) for i in range(3)]
    element = lax.broadcasted_iota(jnp.int32, (N, N), 0) + base
    hits = jnp.where(element == where_ref[...], 1.0, 0.0).astype(bf16)
    x = jnp.concatenate([strength[i, step : step + 1] for i in range(3)] + [jnp.zeros((13, N), f32)], axis=0)
    total = None
    for part in range(3):
        high = x.astype(bf16)
        x = x - high.astype(f32)
        term = lax.dot_general(high, hits, (((1,), (1,)), ((), ())), preferred_element_type=f32)
        total = term if total is None else total + term
    return [total[i : i + 1] for i in range(3)]


def velocities(vel_in, vel, acc, rows):
    def one(i, h):
        for a in range(5):
            vel[h, i, a] = vel_in[h, i, a] + time_step * acc[h, i, a]

    halves(3, one)
    mask = lax.broadcasted_iota(jnp.int32, (8, 128), 0) == 2
    for i in range(3):
        for h in range(2):
            vel[h, i, 2, 2] += jnp.where(mask, rows[i][:, 128 * h : 128 * h + 128], 0.0)


def jump_gradients(vel, halo, grads, perms, yj, zj):
    along = Along(D_LIFT)
    jumps(vel, (0, 1, 2), 0, perms, yj, zj)

    def one(i, h):
        for a in range(5):
            ys = derive_rows([vel[h, i, a, b] for b in range(5)], D_LIFT)
            ys[0] = ys[0] + yj[0, h, i, a]
            ys[4] = ys[4] + yj[1, h, i, a]
            for b in range(5):
                grads[h, 3 + i, a, b] = ys[b]
                grads[h, 6 + i, a, b] = along(vel[h, i, a, b]) + zj[h, i, a, b]
        for b in range(5):
            xs = derive_rows([vel[h, i, a, b] for a in range(5)], D_LIFT)
            xs[0] = xs[0] - 5.0 * halo[0, h, 3 + i, b]
            xs[4] = xs[4] + 5.0 * halo[1, h, 3 + i, b]
            for a in range(5):
                grads[h, i, a, b] = xs[a]

    halves(3, one)


def update_stress(stress_in, stress, grads, lam, mu):
    def one(a, h):
        g = lambda j, i: grads[h, 3 * j + i, a]
        l, m = lam[h, a], mu[h, a]
        both = l * (g(0, 0) + g(1, 1) + g(2, 2))
        for i in range(3):
            stress[h, i, a] = stress_in[h, i, a] + (both + 2.0 * m * g(i, i))
        stress[h, 3, a] = stress_in[h, 3, a] + m * (g(2, 1) + g(1, 2))
        stress[h, 4, a] = stress_in[h, 4, a] + m * (g(2, 0) + g(0, 2))
        stress[h, 5, a] = stress_in[h, 5, a] + m * (g(1, 0) + g(0, 1))

    halves(5, one)


def plain_gradients(vel, grads):
    along = Along(D_PLAIN)

    def one(i, h):
        for a in range(5):
            ys = derive_rows([vel[h, i, a, b] for b in range(5)], D_PLAIN)
            for b in range(5):
                grads[h, 3 + i, a, b] = ys[b]
                grads[h, 6 + i, a, b] = along(vel[h, i, a, b])
        for b in range(5):
            xs = derive_rows([vel[h, i, a, b] for a in range(5)], D_PLAIN)
            for a in range(5):
                grads[h, i, a, b] = xs[a]

    halves(3, one)


def image(fg, ag, acc, adj_vel, dense, first):
    row = lax.broadcasted_iota(jnp.int32, (8, 128), 0)
    weight = Along.by_row(row, QUAD)

    def one(k, h):
        for a in range(5):
            for b in range(5):
                f = lambda j, i: fg[h, 3 * j + i, a, b]
                g = lambda j, i: ag[h, 3 * j + i, a, b]
                w = weight * float(QUAD[a] * QUAD[b])
                f0, f1, f2 = f(0, 0), f(1, 1), f(2, 2)
                g0, g1, g2 = g(0, 0), g(1, 1), g(2, 2)
                trace = (f0 + f1 + f2) * (g0 + g1 + g2) * w
                cross = None
                for i, j in ((0, 1), (0, 2), (1, 2)):
                    term = (f(j, i) + f(i, j)) * (g(j, i) + g(i, j))
                    cross = term if cross is None else cross + term
                strain = (2.0 * (f0 * g0 + f1 * g1 + f2 * g2) + cross) * w
                inertia = None
                for i in range(3):
                    term = acc[h, i, a, b] * adj_vel[h, i, a, b]
                    inertia = term if inertia is None else inertia + term
                for t, term in enumerate((trace, strain, inertia * w)):
                    at = t * 125 + a * 25 + b * 5
                    if first is None:
                        dense[h, at : at + 5, :] = term[0:5]
                    else:
                        dense[h, at : at + 5, :] = first[h, at : at + 5, :] + term[0:5]

    halves(1, one)


def start_common(state, rinv, perms, acc, vel, stress, up, down, yj, zj, with_r):
    src = flat(state, 2250)
    up, down = (flat(r, r.shape[0] * 2) for r in (up, down))
    load_fields(src, 0, vel, 3)
    load_fields(src, 3, stress, 6)
    local_acceleration(stress, rinv, acc, perms, yj, zj)
    for dst, a in ((up, 4), (down, 0)):
        for i in range(3):
            dst[50 * i : 50 * i + 50, :] = src[250 * (3, 8, 7)[i] + 50 * a : 250 * (3, 8, 7)[i] + 50 * a + 50, :]
            for h in range(2):
                pack_face(dst, 3 + i, vel[h, i, a] + time_step * acc[h, i, a], h)
        if with_r:
            for h in range(2):
                pack_face(dst, 6, 0.05 * rinv[h, a], h)


def load_material(mat, k, dst):
    for g in range(25):
        for h in range(2):
            dst[h, g // 5, g % 5, 0:5, :] = mat[5 * g : 5 * g + 5, k, 128 * h : 128 * h + 128]


def forward_start_kernel(state, mat, nbr, up, down, acc, vel, stress, rinv, perms, yj, zj):
    make_perms(nbr, perms)
    load_material(mat, 2, rinv)
    for h in range(2):
        for a in range(5):
            rinv[h, a] = 1.0 / rinv[h, a]
    zj[...] = jnp.zeros(zj.shape, f32)
    start_common(state, rinv, perms, acc, vel, stress, up, down, yj, zj, True)


def adjoint_start_kernel(state, mat, rinv, perms, up, down, acc, vel, stress, lam, mu, yj, zj):
    zj[...] = jnp.zeros(zj.shape, f32)
    start_common(state, rinv, perms, acc, vel, stress, up, down, yj, zj, False)
    for k, dst in ((0, lam), (1, mu)):
        load_material(mat, k, dst)
        for h in range(2):
            for a in range(5):
                dst[h, a] = time_step * dst[h, a]


def finish_step(kind, step, base, vel_in, stress_in, lam, mu, rinv, perms, where_ref, strength,
                vel, stress, acc, halo, grads, yj, zj):
    finish_acceleration(acc, stress_in, rinv, halo, True)
    velocities(vel_in, vel, acc, inject_rows(kind, step, where_ref, strength, base))
    jump_gradients(vel, halo, grads, perms, yj, zj)
    update_stress(stress_in, stress, grads, lam, mu)


def middle_kernel(kind, base, vel_in, stress_in, acc_in, lam, mu, rinv, perms, where_ref, strength,
                  below, above, r_below, r_above, up, down, vel, stress, acc, next_acc, halo, grads, yj, zj):
    zj[...] = jnp.zeros(zj.shape, f32)
    load_halo(halo, *(flat(r, r.shape[0] * 2) for r in (below, above, r_below, r_above)), 6)
    acc[...] = acc_in[...]
    finish_step(kind, 0, base[0], vel_in, stress_in, lam, mu, rinv, perms, where_ref, strength,
                vel, stress, acc, halo, grads, yj, zj)
    local_acceleration(stress, rinv, next_acc, perms, yj, zj)
    for dst, a in ((up, 4), (down, 0)):
        dst = flat(dst, dst.shape[0] * 2)
        for i in range(3):
            for h in range(2):
                pack_face(dst, i, stress[h, (0, 5, 4)[i], a], h)
                if kind == "receiver":
                    pack_face(dst, 3 + i, vel[h, i, a] + time_step * next_acc[h, i, a], h)


def last_kernel(base, vel_in, stress_in, acc_in, lam, mu, rinv, perms, where_ref, strength,
                below, above, r_below, r_above, out, vel, stress, acc, halo, grads, yj, zj):
    zj[...] = jnp.zeros(zj.shape, f32)
    load_halo(halo, *(flat(r, r.shape[0] * 2) for r in (below, above, r_below, r_above)), 6)
    acc[...] = acc_in[...]
    finish_step("receiver", 1, base[0], vel_in, stress_in, lam, mu, rinv, perms, where_ref, strength,
                vel, stress, acc, halo, grads, yj, zj)
    dst = flat(out, 2250)
    for first, field, count in ((0, vel, 3), (3, stress, 6)):

        def one(k, carry):
            for g in range(25):
                for h in range(2):
                    dst[pl.ds(250 * (first + k) + 10 * g + h, 5, 2), :] = field[h, k, g // 5, g % 5, 0:5, :]
            return carry

        lax.fori_loop(0, count, one, 0)


def first_image_kernel(adj_vel_end, f_vel, f_acc, a_vel, dense, end_grads, fg, ag):
    plain_gradients(f_vel, fg)
    plain_gradients(a_vel, ag)
    image(fg, ag, f_acc, a_vel, dense, None)
    plain_gradients(adj_vel_end, end_grads)


def last_image_kernel(base, f_vel, acc_in, adj_vel, end_grads, first, rinv, where_ref, strength, below, above,
                      keep, send, halo, vel, acc, fg, dense):
    load_halo(halo, flat(below, 150), flat(above, 150), None, None, 3)
    acc[...] = acc_in[...]
    finish_acceleration(acc, None, rinv, halo, False)
    velocities(f_vel, vel, acc, inject_rows("source", 1, where_ref, strength, base[0]))
    plain_gradients(vel, fg)
    for h in range(2):
        dense[h, 368:384, :] = jnp.zeros((16, 128), f32)
    image(fg, end_grads, acc, adj_vel, dense, first)
    core = base[1]
    turned = [dense[h].T for h in range(2)]
    for parity, (mine, other) in ((0, (keep, send)), (1, (send, keep))):

        @pl.when(core == parity)
        def _():
            for s in range(16):
                piece = turned[s // 8][16 * (s % 8) : 16 * (s % 8) + 16]
                (mine if s % 2 == 0 else other)[s // 2] = piece


V = pl.BlockSpec(memory_space=pltpu.VMEM)
S = pl.BlockSpec(memory_space=pltpu.SMEM)


def shape(*dims):
    return jax.ShapeDtypeStruct(dims, f32)


def field(count):
    return shape(2, count, 5, 5, 8, 128)


ONE = shape(2, 5, 5, 8, 128)
PERMS = jax.ShapeDtypeStruct((4, N, N), bf16)


def sends(faces):
    return shape(faces * 25, 2, 128)


def scr(s):
    return pltpu.VMEM(s.shape, s.dtype)


JUMPS = [pltpu.VMEM((2, 2, 3, 5, 8, 128), f32), pltpu.VMEM((2, 3, 5, 5, 8, 128), f32)]
HALO = pltpu.VMEM((2, 2, 7, 5, 8, 128), f32)


def call(kernel, specs, outs, scratch, flops, moved):
    return pl.pallas_call(
        kernel,
        out_shape=outs,
        in_specs=specs,
        out_specs=jax.tree.map(lambda _: V, outs),
        scratch_shapes=scratch,
        compiler_params=pltpu.CompilerParams(vmem_limit_bytes=20 * 2**20),
        cost_estimate=pl.CostEstimate(flops=flops, bytes_accessed=moved, transcendentals=0),
    )


def passed_along(value, axis, steps):
    count = lax.axis_size(axis)
    pairs = [(source, (source + steps) % count) for source in range(count)]
    return lax.ppermute(value, axis, pairs)


def both_ways(up, down):
    return passed_along(up, "slab", 1), passed_along(down, "slab", -1)


def reduce_over_shots(keep, send):
    place = lax.axis_index("shot")
    high, line = (place // 2) % 2, place // 4
    pick = lambda v, k, axis: lax.dynamic_index_in_dim(v, k, axis, False)
    hop = lambda v, to: lax.ppermute(v, "shot", [(i, to(i)) for i in range(16)])
    x = (keep + hop(send, lambda i: i ^ 1)).reshape(4, 2, 16, 384)
    total = pick(x, line, 0)
    for d in (1, 2, 3):
        total = total + hop(pick(x, (line + d) % 4, 0), lambda i: (i + 4 * d) % 16)
    return pick(total, high, 0) + hop(pick(total, 1 - high, 0), lambda i: i ^ 2)


def body(fwd, adj, materials, nbr, source_element, pulse, receivers, residuals):
    base = jnp.stack([lax.axis_index("slab") * N, lax.axis_index("shot") % 2]).astype(jnp.int32)
    receivers = receivers.reshape(1, N)
    fwd, adj = (x.reshape(1125, 2, 128) for x in (fwd, adj))
    mat = materials.transpose(1, 2, 3, 0, 4).reshape(125, 3, N)
    nbr = nbr.T
    residuals = residuals.transpose(0, 2, 1, 3).reshape(3, 2, N)

    f_up, f_down, f_acc, f_vel, f_stress, rinv, perms = call(
        forward_start_kernel,
        [V] * 3,
        (sends(7), sends(7), field(3), field(3), field(6), ONE, PERMS),
        JUMPS,
        10**8, 4 * 10**6,
    )(fwd, mat, nbr)
    f_below, f_above = both_ways(f_up, f_down)
    a_up, a_down, a_acc, a_vel, a_stress, lam, mu = call(
        adjoint_start_kernel,
        [V] * 4,
        (sends(6), sends(6), field(3), field(3), field(6), ONE, ONE),
        JUMPS,
        10**8, 4 * 10**6,
    )(adj, mat, rinv, perms)
    a_below, a_above = both_ways(a_up, a_down)
    adj_vel_end = a_vel

    def middle(kind, vel, stress, acc, where_ref, strength, below, above, faces):
        kernel = lambda base_ref, *refs: middle_kernel(kind, base_ref, *refs)
        held = S if kind == "source" else V
        return call(
            kernel,
            [S] + [V] * 7 + [held] * 2 + [V] * 4,
            (sends(faces), sends(faces), field(3), field(6), field(3), field(3)),
            [HALO, scr(field(9))] + JUMPS,
            2 * 10**8, 8 * 10**6,
        )(base, vel, stress, acc, lam, mu, rinv, perms, where_ref, strength, below, above, f_below, f_above)

    f_up, f_down, f_vel1, _, f_acc1, f_acc2 = middle(
        "source", f_vel, f_stress, f_acc, source_element, pulse, f_below, f_above, 3
    )
    f_below2, f_above2 = both_ways(f_up, f_down)
    a_up, a_down, a_vel1, a_stress1, _, a_acc2 = middle(
        "receiver", a_vel, a_stress, a_acc, receivers, residuals, a_below, a_above, 6
    )
    a_below2, a_above2 = both_ways(a_up, a_down)
    first, end_grads = call(
        first_image_kernel,
        [V] * 4,
        (shape(2, 384, 128), field(9)),
        [scr(field(9)), scr(field(9))],
        10**8, 8 * 10**6,
    )(adj_vel_end, f_vel1, f_acc1, a_vel1)
    keep, send = call(
        last_image_kernel,
        [S] + [V] * 6 + [S] * 2 + [V] * 2,
        (shape(8, 16, 384), shape(8, 16, 384)),
        [HALO, scr(field(3)), scr(field(3)), scr(field(9)), scr(shape(2, 384, 128))],
        10**8, 8 * 10**6,
    )(base, f_vel1, f_acc2, adj_vel_end, end_grads, first, rinv, source_element, pulse, f_below2, f_above2)
    gradient = reduce_over_shots(keep, send)
    adjoint_end = call(
        last_kernel,
        [S] + [V] * 13,
        shape(1125, 2, 128),
        [scr(field(3)), scr(field(6)), scr(field(3)), HALO, scr(field(9))] + JUMPS,
        10**8, 8 * 10**6,
    )(base, a_vel1, a_stress1, a_acc2, lam, mu, rinv, perms, receivers, residuals, a_below2, a_above2, f_below, f_above)
    return gradient[:, :375].T.reshape(3, 5, 5, 5, 16), adjoint_end.reshape(1, 9, 5, 5, 5, N)


def solution(mesh):
    return jax.shard_map(
        body,
        mesh=mesh,
        in_specs=(
            P("shot", None, None, None, None, "slab"),
            P("shot", None, None, None, None, "slab"),
            P(None, None, None, None, "slab"),
            P(),
            P("shot"),
            P("shot", None, None),
            P(),
            P("shot", None, None, None),
        ),
        out_specs=(
            P(None, None, None, None, ("slab", "shot")),
            P("shot", None, None, None, None, "slab"),
        ),
        check_vma=False,
    )
```

```python
import math

import jax
import jax.numpy as jnp
import numpy as np
from jax import lax
from jax.experimental import pallas as pl
from jax.experimental.pallas import tpu as pltpu
from jax.sharding import PartitionSpec as P

f32 = jnp.float32
bf16 = jnp.bfloat16

time_step = 0.01
N = 256


def tables():
    root = math.sqrt(3.0 / 7.0)
    points = np.array([-1.0, -root, 0.0, root, 1.0])
    legendre = (35.0 * points**4 - 30.0 * points**2 + 3.0) / 8.0
    matrix = np.zeros((5, 5))
    for r in range(5):
        for c in range(5):
            if r != c:
                matrix[r, c] = legendre[r] / (legendre[c] * (points[r] - points[c]))
    matrix[0, 0] = -5.0
    matrix[4, 4] = 5.0
    quad = np.array([0.1, 49.0 / 90.0, 32.0 / 45.0, 49.0 / 90.0, 0.1])
    return matrix, quad


D_PLAIN, QUAD = tables()
D_LIFT = D_PLAIN.copy()
D_LIFT[0, 0] += 5.0
D_LIFT[4, 4] -= 5.0


def split(x):
    high = x.astype(bf16)
    return high, (x - high.astype(f32)).astype(bf16)


def dot(a, b):
    return lax.dot_general(a, b, (((1,), (0,)), ((), ())), preferred_element_type=f32)


def derive_rows(rows, matrix):
    even0, odd0 = rows[0] + rows[4], rows[0] - rows[4]
    even1, odd1 = rows[1] + rows[3], rows[1] - rows[3]
    out = [None] * 5
    for r in (0, 1):
        m = [float(v) for v in matrix[r]]
        p = 0.5 * (m[0] + m[4]) * even0 + 0.5 * (m[1] + m[3]) * even1 + m[2] * rows[2]
        q = 0.5 * (m[0] - m[4]) * odd0 + 0.5 * (m[1] - m[3]) * odd1
        out[r] = q + p
        out[4 - r] = q - p
    out[2] = float(matrix[2, 0]) * odd0 + float(matrix[2, 1]) * odd1
    return out


class Along:
    def __init__(self, matrix):
        row = lax.broadcasted_iota(jnp.int32, (8, 128), 0)
        self.places = [jnp.where(row < 5, lax.rem(row + m, 5), row) for m in range(1, 5)]
        self.factors = []
        for m in range(1, 5):
            self.factors.append(self.by_row(row, [matrix[c, (c + m) % 5] for c in range(5)]))
        own = [matrix[c, c] for c in range(5)]
        self.own = self.by_row(row, own) if any(own) else None

    @staticmethod
    def by_row(row, values):
        out = jnp.zeros((8, 128), f32)
        for c in range(5):
            out = jnp.where(row == c, float(values[c]), out)
        return out

    def __call__(self, tile):
        total = None if self.own is None else tile * self.own
        for place, factor in zip(self.places, self.factors):
            term = jnp.take_along_axis(tile, place, axis=0) * factor
            total = term if total is None else total + term
        return total


def flat(ref, rows):
    return ref.reshape(rows, 128)


def make_perms(nbr, perms):
    source = lax.broadcasted_iota(jnp.int32, (N, N), 0)
    for k in range(4):
        hit = source == nbr[k : k + 1, :]
        perms[k] = jnp.where(hit, -5.0 if k % 2 == 0 else 5.0, 0.0).astype(bf16)


def permuted(face, matrix):
    rows = face.shape[0]
    both = dot(jnp.concatenate(split(face), axis=0), matrix)
    return both[:rows] + both[rows:]


def jumps(field, ys, first_z, perms, yj, zj):
    count = field.shape[1]
    for side, b in ((0, 4), (1, 0)):
        face = jnp.concatenate(
            [
                jnp.concatenate([field[h, k, :, b].reshape(40, 128) for h in range(2)], axis=1)
                for k in ys
            ],
            axis=0,
        )
        got = permuted(face, perms[side])
        for h in range(2):
            for i in range(3):
                part = got[40 * i : 40 * i + 40, 128 * h : 128 * h + 128]
                yj[side, h, i] = part.reshape(5, 8, 128)
    rows = flat(field, 2 * count * 200)
    into = flat(zj, 1200)
    spare = jnp.zeros((5, N), f32)
    for side, c in ((0, 4), (1, 0)):
        face = jnp.concatenate(
            [rows[pl.ds((h * count + first_z) * 200 + c, 75, 8), :] for h in range(2)], axis=1
        )
        got = permuted(jnp.concatenate([face, spare], axis=0), perms[2 + side])
        for h in range(2):
            into[pl.ds(h * 600 + (0, 4)[side], 75, 8), :] = got[:75, 128 * h : 128 * h + 128]


def stress_of(i, d):
    return jnp.where(i == d, i, 6 - i - d)


def halves(count, one):
    def step(t, carry):
        one(lax.div(t, 2), lax.rem(t, 2))
        return carry

    lax.fori_loop(0, 2 * count, step, 0)


def local_acceleration(stress, rinv, acc, perms, yj, zj):
    along = Along(D_LIFT)
    jumps(stress, (5, 1, 3), 2, perms, yj, zj)

    def one(i, h):
        kx, ky, kz = stress_of(i, 0), stress_of(i, 1), stress_of(i, 2)
        for a in range(5):
            ys = derive_rows([stress[h, ky, a, b] for b in range(5)], D_LIFT)
            ys[0] = ys[0] + yj[0, h, i, a]
            ys[4] = ys[4] + yj[1, h, i, a]
            for b in range(5):
                acc[h, i, a, b] = ys[b] + (along(stress[h, kz, a, b]) + zj[h, 2 - i, a, b])
        for b in range(5):
            xs = derive_rows([stress[h, kx, a, b] for a in range(5)], D_LIFT)
            for a in range(5):
                acc[h, i, a, b] = (acc[h, i, a, b] + xs[a]) * rinv[h, a, b]

    halves(3, one)


def load_fields(src, first, dst, count):
    def one(k, carry):
        for g in range(25):
            for h in range(2):
                dst[h, k, g // 5, g % 5, 0:5, :] = src[pl.ds(250 * (first + k) + 10 * g + h, 5, 2), :]
        return carry

    lax.fori_loop(0, count, one, 0)


def pack_face(dst, k, value, h):
    for b in range(5):
        dst[pl.ds(50 * k + 10 * b + h, 5, 2), :] = value[b, 0:5]


def unpack_face(dst, side, k, src, j):
    for h in range(2):
        for b in range(5):
            dst[side, h, k, b, 0:5, :] = src[pl.ds(50 * j + 10 * b + h, 5, 2), :]


def load_halo(halo, below, above, r_below, r_above, count):
    for side, src in ((0, below), (1, above)):
        for k in range(count):
            unpack_face(halo, side, k, src, k)
    if r_below is not None:
        for side, src in ((0, r_below), (1, r_above)):
            unpack_face(halo, side, 6, src, 6)


def finish_acceleration(acc, stress, rinv, halo, has_v):
    for h in range(2):
        for i in range(3):
            k = (0, 5, 4)[i]
            acc[h, i, 0] = acc[h, i, 0] - 5.0 * rinv[h, 0] * halo[0, h, i]
            acc[h, i, 4] = acc[h, i, 4] + 5.0 * rinv[h, 4] * halo[1, h, i]
            if has_v:
                halo[0, h, 3 + i] = halo[0, h, 3 + i] + halo[0, h, 6] * stress[h, k, 0]
                halo[1, h, 3 + i] = halo[1, h, 3 + i] - halo[1, h, 6] * stress[h, k, 4]


def inject_rows(kind, step, where_ref, strength, base):
    if kind == "source":
        lane = lax.broadcasted_iota(jnp.int32, (1, N), 1) + base
        hit = lane == where_ref[0]
        return [jnp.where(hit, strength[0, step, i], 0.0) for i in range(3)]
    element = lax.broadcasted_iota(jnp.int32, (N, N), 0) + base
    hits = jnp.where(element == where_ref[...], 1.0, 0.0).astype(bf16)
    x = jnp.concatenate([strength[i, step : step + 1] for i in range(3)] + [jnp.zeros((13, N), f32)], axis=0)
    total = None
    for part in range(3):
        high = x.astype(bf16)
        x = x - high.astype(f32)
        term = lax.dot_general(high, hits, (((1,), (1,)), ((), ())), preferred_element_type=f32)
        total = term if total is None else total + term
    return [total[i : i + 1] for i in range(3)]


def slab_base():
    return lax.axis_index("slab") * N


def velocities(vel_in, vel, acc, rows):
    def one(i, h):
        for a in range(5):
            vel[h, i, a] = vel_in[h, i, a] + time_step * acc[h, i, a]

    halves(3, one)
    mask = lax.broadcasted_iota(jnp.int32, (8, 128), 0) == 2
    for i in range(3):
        for h in range(2):
            vel[h, i, 2, 2] += jnp.where(mask, rows[i][:, 128 * h : 128 * h + 128], 0.0)


def jump_gradients(vel, halo, grads, perms, yj, zj):
    along = Along(D_LIFT)
    jumps(vel, (0, 1, 2), 0, perms, yj, zj)

    def one(i, h):
        for a in range(5):
            ys = derive_rows([vel[h, i, a, b] for b in range(5)], D_LIFT)
            ys[0] = ys[0] + yj[0, h, i, a]
            ys[4] = ys[4] + yj[1, h, i, a]
            for b in range(5):
                grads[h, 3 + i, a, b] = ys[b]
                grads[h, 6 + i, a, b] = along(vel[h, i, a, b]) + zj[h, i, a, b]
        for b in range(5):
            xs = derive_rows([vel[h, i, a, b] for a in range(5)], D_LIFT)
            xs[0] = xs[0] - 5.0 * halo[0, h, 3 + i, b]
            xs[4] = xs[4] + 5.0 * halo[1, h, 3 + i, b]
            for a in range(5):
                grads[h, i, a, b] = xs[a]

    halves(3, one)


def update_stress(stress_in, stress, grads, lam, mu):
    def one(a, h):
        g = lambda j, i: grads[h, 3 * j + i, a]
        l, m = lam[h, a], mu[h, a]
        both = l * (g(0, 0) + g(1, 1) + g(2, 2))
        for i in range(3):
            stress[h, i, a] = stress_in[h, i, a] + (both + 2.0 * m * g(i, i))
        stress[h, 3, a] = stress_in[h, 3, a] + m * (g(2, 1) + g(1, 2))
        stress[h, 4, a] = stress_in[h, 4, a] + m * (g(2, 0) + g(0, 2))
        stress[h, 5, a] = stress_in[h, 5, a] + m * (g(1, 0) + g(0, 1))

    halves(5, one)


def plain_gradients(vel, grads):
    along = Along(D_PLAIN)

    def one(i, h):
        for a in range(5):
            ys = derive_rows([vel[h, i, a, b] for b in range(5)], D_PLAIN)
            for b in range(5):
                grads[h, 3 + i, a, b] = ys[b]
                grads[h, 6 + i, a, b] = along(vel[h, i, a, b])
        for b in range(5):
            xs = derive_rows([vel[h, i, a, b] for a in range(5)], D_PLAIN)
            for a in range(5):
                grads[h, i, a, b] = xs[a]

    halves(3, one)


def image(fg, ag, acc, adj_vel, dense, first):
    row = lax.broadcasted_iota(jnp.int32, (8, 128), 0)
    weight = Along.by_row(row, QUAD)

    def one(k, h):
        for a in range(5):
            for b in range(5):
                f = lambda j, i: fg[h, 3 * j + i, a, b]
                g = lambda j, i: ag[h, 3 * j + i, a, b]
                w = weight * float(QUAD[a] * QUAD[b])
                f0, f1, f2 = f(0, 0), f(1, 1), f(2, 2)
                g0, g1, g2 = g(0, 0), g(1, 1), g(2, 2)
                trace = (f0 + f1 + f2) * (g0 + g1 + g2) * w
                cross = None
                for i, j in ((0, 1), (0, 2), (1, 2)):
                    term = (f(j, i) + f(i, j)) * (g(j, i) + g(i, j))
                    cross = term if cross is None else cross + term
                strain = (2.0 * (f0 * g0 + f1 * g1 + f2 * g2) + cross) * w
                inertia = None
                for i in range(3):
                    term = acc[h, i, a, b] * adj_vel[h, i, a, b]
                    inertia = term if inertia is None else inertia + term
                for t, term in enumerate((trace, strain, inertia * w)):
                    at = t * 125 + a * 25 + b * 5
                    if first is None:
                        dense[h, at : at + 5, :] = term[0:5]
                    else:
                        dense[h, at : at + 5, :] = first[h, at : at + 5, :] + term[0:5]

    halves(1, one)


def fetch(src, dst, sem):
    copy = pltpu.make_async_copy(src, dst, sem)
    copy.start()
    return copy


def start_common(src, rinv, perms, acc, vel, stress, up, down, yj, zj, with_r):
    src = flat(src, 2250)
    up, down = (flat(r, r.shape[0] * 2) for r in (up, down))
    load_fields(src, 0, vel, 3)
    load_fields(src, 3, stress, 6)
    local_acceleration(stress, rinv, acc, perms, yj, zj)
    for dst, a in ((up, 4), (down, 0)):
        for i in range(3):
            dst[50 * i : 50 * i + 50, :] = src[250 * (3, 8, 7)[i] + 50 * a : 250 * (3, 8, 7)[i] + 50 * a + 50, :]
            for h in range(2):
                pack_face(dst, 3 + i, vel[h, i, a] + time_step * acc[h, i, a], h)
        if with_r:
            for h in range(2):
                pack_face(dst, 6, 0.05 * rinv[h, a], h)


def load_material(mat, k, dst):
    for g in range(25):
        for h in range(2):
            dst[h, g // 5, g % 5, 0:5, :] = mat[5 * g : 5 * g + 5, k, 128 * h : 128 * h + 128]


def forward_start_kernel(state_hbm, mat_hbm, nbr_hbm, up, down, acc, vel, stress, rinv, perms, yj, zj, state, mat, nbr, sems):
    first = fetch(nbr_hbm, nbr, sems.at[0])
    second = fetch(mat_hbm, mat, sems.at[1])
    third = fetch(state_hbm, state, sems.at[2])
    first.wait()
    make_perms(nbr, perms)
    second.wait()
    load_material(mat, 2, rinv)
    for h in range(2):
        for a in range(5):
            rinv[h, a] = 1.0 / rinv[h, a]
    zj[...] = jnp.zeros(zj.shape, f32)
    third.wait()
    start_common(state, rinv, perms, acc, vel, stress, up, down, yj, zj, True)


def adjoint_start_kernel(state, mat, rinv, perms, up, down, acc, vel, stress, lam, mu, yj, zj):
    zj[...] = jnp.zeros(zj.shape, f32)
    start_common(state, rinv, perms, acc, vel, stress, up, down, yj, zj, False)
    for k, dst in ((0, lam), (1, mu)):
        load_material(mat, k, dst)
        for h in range(2):
            for a in range(5):
                dst[h, a] = time_step * dst[h, a]


def finish_step(kind, step, base, vel_in, stress_in, lam, mu, rinv, perms, where_ref, strength,
                vel, stress, acc, halo, grads, yj, zj):
    finish_acceleration(acc, stress_in, rinv, halo, True)
    velocities(vel_in, vel, acc, inject_rows(kind, step, where_ref, strength, base))
    jump_gradients(vel, halo, grads, perms, yj, zj)
    update_stress(stress_in, stress, grads, lam, mu)


def middle_kernel(kind, vel_in, stress_in, acc_in, lam, mu, rinv, perms, where_ref, strength,
                  below, above, r_below, r_above, up, down, vel, stress, acc, *rest):
    next_acc, (halo, grads, yj, zj) = (rest[0], rest[1:]) if kind == "receiver" else (None, rest)
    zj[...] = jnp.zeros(zj.shape, f32)
    load_halo(halo, *(flat(r, r.shape[0] * 2) for r in (below, above, r_below, r_above)), 6)
    acc[...] = acc_in[...]
    finish_step(kind, 0, slab_base(), vel_in, stress_in, lam, mu, rinv, perms, where_ref, strength,
                vel, stress, acc, halo, grads, yj, zj)
    if kind == "receiver":
        local_acceleration(stress, rinv, next_acc, perms, yj, zj)
    for dst, a in ((up, 4), (down, 0)):
        dst = flat(dst, dst.shape[0] * 2)
        for i in range(3):
            for h in range(2):
                pack_face(dst, i, stress[h, (0, 5, 4)[i], a], h)
                if kind == "receiver":
                    pack_face(dst, 3 + i, vel[h, i, a] + time_step * next_acc[h, i, a], h)


def last_kernel(vel_in, stress_in, acc_in, lam, mu, rinv, perms, where_ref, strength,
                below, above, r_below, r_above, out, vel, stress, acc, halo, grads, yj, zj):
    zj[...] = jnp.zeros(zj.shape, f32)
    load_halo(halo, *(flat(r, r.shape[0] * 2) for r in (below, above, r_below, r_above)), 6)
    acc[...] = acc_in[...]
    finish_step("receiver", 1, slab_base(), vel_in, stress_in, lam, mu, rinv, perms, where_ref, strength,
                vel, stress, acc, halo, grads, yj, zj)
    dst = flat(out, 2250)
    for first, field, count in ((0, vel, 3), (3, stress, 6)):

        def one(k, carry):
            for g in range(25):
                for h in range(2):
                    dst[pl.ds(250 * (first + k) + 10 * g + h, 5, 2), :] = field[h, k, g // 5, g % 5, 0:5, :]
            return carry

        lax.fori_loop(0, count, one, 0)


def first_image_kernel(adj_vel_end, f_vel, f_acc, a_vel, f_stress, rinv, perms, dense, end_grads, next_acc, fg, ag, yj, zj):
    zj[...] = jnp.zeros(zj.shape, f32)
    local_acceleration(f_stress, rinv, next_acc, perms, yj, zj)
    plain_gradients(f_vel, fg)
    plain_gradients(a_vel, ag)
    image(fg, ag, f_acc, a_vel, dense, None)
    plain_gradients(adj_vel_end, end_grads)


def last_image_kernel(f_vel, acc_in, adj_vel, end_grads, first, rinv, where_ref, strength, below, above,
                      keep, send, halo, vel, acc, fg, dense):
    load_halo(halo, flat(below, 150), flat(above, 150), None, None, 3)
    acc[...] = acc_in[...]
    finish_acceleration(acc, None, rinv, halo, False)
    velocities(f_vel, vel, acc, inject_rows("source", 1, where_ref, strength, slab_base()))
    plain_gradients(vel, fg)
    for h in range(2):
        dense[h, 368:384, :] = jnp.zeros((16, 128), f32)
    image(fg, end_grads, acc, adj_vel, dense, first)
    core = lax.rem(lax.axis_index("shot"), 2)
    turned = [dense[h].T for h in range(2)]
    for parity, (mine, other) in ((0, (keep, send)), (1, (send, keep))):

        @pl.when(core == parity)
        def _():
            for s in range(16):
                piece = turned[s // 8][16 * (s % 8) : 16 * (s % 8) + 16]
                (mine if s % 2 == 0 else other)[s // 2] = piece


V = pl.BlockSpec(memory_space=pltpu.VMEM)
S = pl.BlockSpec(memory_space=pltpu.SMEM)


def shape(*dims):
    return jax.ShapeDtypeStruct(dims, f32)


def field(count):
    return shape(2, count, 5, 5, 8, 128)


ONE = shape(2, 5, 5, 8, 128)
PERMS = jax.ShapeDtypeStruct((4, N, N), bf16)


def sends(faces):
    return shape(faces * 25, 2, 128)


def scr(s):
    return pltpu.VMEM(s.shape, s.dtype)


JUMPS = [pltpu.VMEM((2, 2, 3, 5, 8, 128), f32), pltpu.VMEM((2, 3, 5, 5, 8, 128), f32)]
HALO = pltpu.VMEM((2, 2, 7, 5, 8, 128), f32)


def call(kernel, specs, outs, scratch, flops, moved):
    return pl.pallas_call(
        kernel,
        out_shape=outs,
        in_specs=specs,
        out_specs=jax.tree.map(lambda _: V, outs),
        scratch_shapes=scratch,
        compiler_params=pltpu.CompilerParams(vmem_limit_bytes=8 * 2**20),
        cost_estimate=pl.CostEstimate(flops=flops, bytes_accessed=moved, transcendentals=0),
    )


def passed_along(value, axis, steps):
    count = lax.axis_size(axis)
    pairs = [(source, (source + steps) % count) for source in range(count)]
    return lax.ppermute(value, axis, pairs)


def both_ways(up, down):
    return passed_along(up, "slab", 1), passed_along(down, "slab", -1)


def reduce_over_shots(keep, send):
    place = lax.axis_index("shot")
    high, line = (place // 2) % 2, place // 4
    pick = lambda v, k, axis: lax.dynamic_index_in_dim(v, k, axis, False)
    hop = lambda v, to: lax.ppermute(v, "shot", [(i, to(i)) for i in range(16)])
    x = (keep + hop(send, lambda i: i ^ 1)).reshape(4, 2, 16, 384)
    total = pick(x, line, 0)
    for d in (1, 2, 3):
        total = total + hop(pick(x, (line + d) % 4, 0), lambda i: (i + 4 * d) % 16)
    return pick(total, high, 0) + hop(pick(total, 1 - high, 0), lambda i: i ^ 2)


def body(fwd, adj, materials, nbr, source_element, pulse, receivers, residuals):
    receivers = receivers.reshape(1, N)
    fwd, adj = (x.reshape(1125, 2, 128) for x in (fwd, adj))
    mat = materials.transpose(1, 2, 3, 0, 4).reshape(125, 3, N)
    nbr = nbr.T
    residuals = residuals.transpose(0, 2, 1, 3).reshape(3, 2, N)

    f_up, f_down, f_acc, f_vel, f_stress, rinv, perms = call(
        forward_start_kernel,
        [pl.BlockSpec(memory_space=pltpu.HBM)] * 3,
        (sends(7), sends(7), field(3), field(3), field(6), ONE, PERMS),
        JUMPS + [scr(shape(1125, 2, 128)), scr(shape(125, 3, N)), pltpu.VMEM((4, N), jnp.int32), pltpu.SemaphoreType.DMA((3,))],
        10**8, 4 * 10**6,
    )(fwd, mat, nbr)
    f_below, f_above = both_ways(f_up, f_down)
    a_up, a_down, a_acc, a_vel, a_stress, lam, mu = call(
        adjoint_start_kernel,
        [V] * 4,
        (sends(6), sends(6), field(3), field(3), field(6), ONE, ONE),
        JUMPS,
        10**8, 4 * 10**6,
    )(adj, mat, rinv, perms)
    a_below, a_above = both_ways(a_up, a_down)
    adj_vel_end = a_vel

    def middle(kind, vel, stress, acc, where_ref, strength, below, above, faces):
        kernel = lambda *refs: middle_kernel(kind, *refs)
        held = S if kind == "source" else V
        return call(
            kernel,
            [V] * 7 + [held] * 2 + [V] * 4,
            (sends(faces), sends(faces), field(3), field(6), field(3)) + (() if kind == "source" else (field(3),)),
            [HALO, scr(field(9))] + JUMPS,
            2 * 10**8, 8 * 10**6,
        )(vel, stress, acc, lam, mu, rinv, perms, where_ref, strength, below, above, f_below, f_above)

    f_up, f_down, f_vel1, f_stress1, f_acc1 = middle(
        "source", f_vel, f_stress, f_acc, source_element, pulse, f_below, f_above, 3
    )
    f_below2, f_above2 = both_ways(f_up, f_down)
    a_up, a_down, a_vel1, a_stress1, _, a_acc2 = middle(
        "receiver", a_vel, a_stress, a_acc, receivers, residuals, a_below, a_above, 6
    )
    a_below2, a_above2 = both_ways(a_up, a_down)
    first, end_grads, f_acc2 = call(
        first_image_kernel,
        [V] * 7,
        (shape(2, 384, 128), field(9), field(3)),
        [scr(field(9)), scr(field(9))] + JUMPS,
        1000, 1000,
    )(adj_vel_end, f_vel1, f_acc1, a_vel1, f_stress1, rinv, perms)
    keep, send = call(
        last_image_kernel,
        [V] * 6 + [S] * 2 + [V] * 2,
        (shape(8, 16, 384), shape(8, 16, 384)),
        [HALO, scr(field(3)), scr(field(3)), scr(field(9)), scr(shape(2, 384, 128))],
        1000, 1000,
    )(f_vel1, f_acc2, adj_vel_end, end_grads, first, rinv, source_element, pulse, f_below2, f_above2)
    gradient = reduce_over_shots(keep, send)
    adjoint_end = call(
        last_kernel,
        [V] * 13,
        shape(1125, 2, 128),
        [scr(field(3)), scr(field(6)), scr(field(3)), HALO, scr(field(9))] + JUMPS,
        10**8, 8 * 10**6,
    )(a_vel1, a_stress1, a_acc2, lam, mu, rinv, perms, receivers, residuals, a_below2, a_above2, f_below, f_above)
    return gradient[:, :375].T.reshape(3, 5, 5, 5, 16), adjoint_end.reshape(1, 9, 5, 5, 5, N)


def solution(mesh):
    return jax.shard_map(
        body,
        mesh=mesh,
        in_specs=(
            P("shot", None, None, None, None, "slab"),
            P("shot", None, None, None, None, "slab"),
            P(None, None, None, None, "slab"),
            P(),
            P("shot"),
            P("shot", None, None),
            P(),
            P("shot", None, None, None),
        ),
        out_specs=(
            P(None, None, None, None, ("slab", "shot")),
            P("shot", None, None, None, None, "slab"),
        ),
        check_vma=False,
    )
```

```python
import math

import jax
import jax.numpy as jnp
import numpy as np
from jax import lax
from jax.experimental import pallas as pl
from jax.experimental.pallas import tpu as pltpu
from jax.sharding import PartitionSpec as P

f32 = jnp.float32
bf16 = jnp.bfloat16

time_step = 0.01
N = 256


def tables():
    root = math.sqrt(3.0 / 7.0)
    points = np.array([-1.0, -root, 0.0, root, 1.0])
    legendre = (35.0 * points**4 - 30.0 * points**2 + 3.0) / 8.0
    matrix = np.zeros((5, 5))
    for r in range(5):
        for c in range(5):
            if r != c:
                matrix[r, c] = legendre[r] / (legendre[c] * (points[r] - points[c]))
    matrix[0, 0] = -5.0
    matrix[4, 4] = 5.0
    quad = np.array([0.1, 49.0 / 90.0, 32.0 / 45.0, 49.0 / 90.0, 0.1])
    return matrix, quad


D_PLAIN, QUAD = tables()
D_LIFT = D_PLAIN.copy()
D_LIFT[0, 0] += 5.0
D_LIFT[4, 4] -= 5.0


def split(x):
    high = x.astype(bf16)
    return high, (x - high.astype(f32)).astype(bf16)


def dot(a, b):
    return lax.dot_general(a, b, (((1,), (0,)), ((), ())), preferred_element_type=f32)


def derive_rows(rows, matrix):
    even0, odd0 = rows[0] + rows[4], rows[0] - rows[4]
    even1, odd1 = rows[1] + rows[3], rows[1] - rows[3]
    out = [None] * 5
    for r in (0, 1):
        m = [float(v) for v in matrix[r]]
        p = 0.5 * (m[0] + m[4]) * even0 + 0.5 * (m[1] + m[3]) * even1 + m[2] * rows[2]
        q = 0.5 * (m[0] - m[4]) * odd0 + 0.5 * (m[1] - m[3]) * odd1
        out[r] = q + p
        out[4 - r] = q - p
    out[2] = float(matrix[2, 0]) * odd0 + float(matrix[2, 1]) * odd1
    return out


class Along:
    def __init__(self, matrix):
        row = lax.broadcasted_iota(jnp.int32, (8, 128), 0)
        self.places = [jnp.where(row < 5, lax.rem(row + m, 5), row) for m in range(1, 5)]
        self.factors = []
        for m in range(1, 5):
            self.factors.append(self.by_row(row, [matrix[c, (c + m) % 5] for c in range(5)]))
        own = [matrix[c, c] for c in range(5)]
        self.own = self.by_row(row, own) if any(own) else None

    @staticmethod
    def by_row(row, values):
        out = jnp.zeros((8, 128), f32)
        for c in range(5):
            out = jnp.where(row == c, float(values[c]), out)
        return out

    def __call__(self, tile):
        total = None if self.own is None else tile * self.own
        for place, factor in zip(self.places, self.factors):
            term = jnp.take_along_axis(tile, place, axis=0) * factor
            total = term if total is None else total + term
        return total


def flat(ref, rows):
    return ref.reshape(rows, 128)


def make_perms(nbr, perms):
    source = lax.broadcasted_iota(jnp.int32, (N, N), 0)
    for k in range(4):
        hit = source == nbr[k : k + 1, :]
        perms[k] = jnp.where(hit, -5.0 if k % 2 == 0 else 5.0, 0.0).astype(bf16)


def permuted(face, matrix):
    rows = face.shape[0]
    both = dot(jnp.concatenate(split(face), axis=0), matrix)
    return both[:rows] + both[rows:]


def jumps(field, ys, first_z, perms, yj, zj):
    count = field.shape[1]
    for side, b in ((0, 4), (1, 0)):
        face = jnp.concatenate(
            [
                jnp.concatenate([field[h, k, :, b].reshape(40, 128) for h in range(2)], axis=1)
                for k in ys
            ],
            axis=0,
        )
        got = permuted(face, perms[side])
        for h in range(2):
            for i in range(3):
                part = got[40 * i : 40 * i + 40, 128 * h : 128 * h + 128]
                yj[side, h, i] = part.reshape(5, 8, 128)
    rows = flat(field, 2 * count * 200)
    into = flat(zj, 1200)
    spare = jnp.zeros((5, N), f32)
    for side, c in ((0, 4), (1, 0)):
        face = jnp.concatenate(
            [rows[pl.ds((h * count + first_z) * 200 + c, 75, 8), :] for h in range(2)], axis=1
        )
        got = permuted(jnp.concatenate([face, spare], axis=0), perms[2 + side])
        for h in range(2):
            into[pl.ds(h * 600 + (0, 4)[side], 75, 8), :] = got[:75, 128 * h : 128 * h + 128]


def stress_of(i, d):
    return jnp.where(i == d, i, 6 - i - d)


def halves(count, one):
    def step(t, carry):
        one(lax.div(t, 2), lax.rem(t, 2))
        return carry

    lax.fori_loop(0, 2 * count, step, 0)


def local_acceleration(stress, rinv, acc, perms, yj, zj):
    along = Along(D_LIFT)
    jumps(stress, (5, 1, 3), 2, perms, yj, zj)

    def one(i, h):
        kx, ky, kz = stress_of(i, 0), stress_of(i, 1), stress_of(i, 2)
        for a in range(5):
            ys = derive_rows([stress[h, ky, a, b] for b in range(5)], D_LIFT)
            ys[0] = ys[0] + yj[0, h, i, a]
            ys[4] = ys[4] + yj[1, h, i, a]
            for b in range(5):
                acc[h, i, a, b] = ys[b] + (along(stress[h, kz, a, b]) + zj[h, 2 - i, a, b])
        for b in range(5):
            xs = derive_rows([stress[h, kx, a, b] for a in range(5)], D_LIFT)
            for a in range(5):
                acc[h, i, a, b] = (acc[h, i, a, b] + xs[a]) * rinv[h, a, b]

    halves(3, one)


def load_fields(src, first, dst, count):
    def one(k, carry):
        for g in range(25):
            for h in range(2):
                dst[h, k, g // 5, g % 5, 0:5, :] = src[pl.ds(250 * (first + k) + 10 * g + h, 5, 2), :]
        return carry

    lax.fori_loop(0, count, one, 0)


def pack_face(dst, k, value, h):
    for b in range(5):
        dst[pl.ds(50 * k + 10 * b + h, 5, 2), :] = value[b, 0:5]


def unpack_face(dst, side, k, src, j):
    for h in range(2):
        for b in range(5):
            dst[side, h, k, b, 0:5, :] = src[pl.ds(50 * j + 10 * b + h, 5, 2), :]


def load_halo(halo, below, above, r_below, r_above, count):
    for side, src in ((0, below), (1, above)):
        for k in range(count):
            unpack_face(halo, side, k, src, k)
    if r_below is not None:
        for side, src in ((0, r_below), (1, r_above)):
            unpack_face(halo, side, 6, src, 6)


def finish_acceleration(acc, stress, rinv, halo, has_v):
    for h in range(2):
        for i in range(3):
            k = (0, 5, 4)[i]
            acc[h, i, 0] = acc[h, i, 0] - 5.0 * rinv[h, 0] * halo[0, h, i]
            acc[h, i, 4] = acc[h, i, 4] + 5.0 * rinv[h, 4] * halo[1, h, i]
            if has_v:
                halo[0, h, 3 + i] = halo[0, h, 3 + i] + halo[0, h, 6] * stress[h, k, 0]
                halo[1, h, 3 + i] = halo[1, h, 3 + i] - halo[1, h, 6] * stress[h, k, 4]


def source_rows(step, where_ref, pulse):
    lane = lax.broadcasted_iota(jnp.int32, (1, N), 1) + slab_base()
    hit = lane == where_ref[0]
    return [jnp.where(hit, pulse[0, step, i], 0.0) for i in range(3)]


def receiver_rows(where_ref, residual):
    element = lax.broadcasted_iota(jnp.int32, (N, N), 0) + slab_base()
    hits = jnp.where(element == where_ref[...], 1.0, 0.0).astype(bf16)
    spare = jnp.zeros((5, N), f32)
    x = jnp.concatenate([r for step in range(2) for r in [residual[i, step : step + 1] for i in range(3)] + [spare]], axis=0)
    total = None
    for part in range(3):
        high = x.astype(bf16)
        x = x - high.astype(f32)
        term = lax.dot_general(high, hits, (((1,), (1,)), ((), ())), preferred_element_type=f32)
        total = term if total is None else total + term
    return total


def slab_base():
    return lax.axis_index("slab") * N


def velocities(vel_in, vel, acc, rows):
    def one(i, h):
        for a in range(5):
            vel[h, i, a] = vel_in[h, i, a] + time_step * acc[h, i, a]

    halves(3, one)
    mask = lax.broadcasted_iota(jnp.int32, (8, 128), 0) == 2
    for i in range(3):
        for h in range(2):
            vel[h, i, 2, 2] += jnp.where(mask, rows[i][:, 128 * h : 128 * h + 128], 0.0)


def jump_gradients(vel, halo, grads, perms, yj, zj):
    along = Along(D_LIFT)
    jumps(vel, (0, 1, 2), 0, perms, yj, zj)

    def one(i, h):
        for a in range(5):
            ys = derive_rows([vel[h, i, a, b] for b in range(5)], D_LIFT)
            ys[0] = ys[0] + yj[0, h, i, a]
            ys[4] = ys[4] + yj[1, h, i, a]
            for b in range(5):
                grads[h, 3 + i, a, b] = ys[b]
                grads[h, 6 + i, a, b] = along(vel[h, i, a, b]) + zj[h, i, a, b]
        for b in range(5):
            xs = derive_rows([vel[h, i, a, b] for a in range(5)], D_LIFT)
            xs[0] = xs[0] - 5.0 * halo[0, h, 3 + i, b]
            xs[4] = xs[4] + 5.0 * halo[1, h, 3 + i, b]
            for a in range(5):
                grads[h, i, a, b] = xs[a]

    halves(3, one)


def update_stress(stress_in, stress, grads, lam, mu):
    def one(a, h):
        g = lambda j, i: grads[h, 3 * j + i, a]
        l, m = lam[h, a], mu[h, a]
        both = l * (g(0, 0) + g(1, 1) + g(2, 2))
        for i in range(3):
            stress[h, i, a] = stress_in[h, i, a] + (both + 2.0 * m * g(i, i))
        stress[h, 3, a] = stress_in[h, 3, a] + m * (g(2, 1) + g(1, 2))
        stress[h, 4, a] = stress_in[h, 4, a] + m * (g(2, 0) + g(0, 2))
        stress[h, 5, a] = stress_in[h, 5, a] + m * (g(1, 0) + g(0, 1))

    halves(5, one)


def plain_gradients(vel, grads):
    along = Along(D_PLAIN)

    def one(i, h):
        for a in range(5):
            ys = derive_rows([vel[h, i, a, b] for b in range(5)], D_PLAIN)
            for b in range(5):
                grads[h, 3 + i, a, b] = ys[b]
                grads[h, 6 + i, a, b] = along(vel[h, i, a, b])
        for b in range(5):
            xs = derive_rows([vel[h, i, a, b] for a in range(5)], D_PLAIN)
            for a in range(5):
                grads[h, i, a, b] = xs[a]

    halves(3, one)


def image(fg, ag, acc, adj_vel, dense, first):
    row = lax.broadcasted_iota(jnp.int32, (8, 128), 0)
    weight = Along.by_row(row, QUAD)

    def one(k, h):
        for a in range(5):
            for b in range(5):
                f = lambda j, i: fg[h, 3 * j + i, a, b]
                g = lambda j, i: ag[h, 3 * j + i, a, b]
                w = weight * float(QUAD[a] * QUAD[b])
                f0, f1, f2 = f(0, 0), f(1, 1), f(2, 2)
                g0, g1, g2 = g(0, 0), g(1, 1), g(2, 2)
                trace = (f0 + f1 + f2) * (g0 + g1 + g2) * w
                cross = None
                for i, j in ((0, 1), (0, 2), (1, 2)):
                    term = (f(j, i) + f(i, j)) * (g(j, i) + g(i, j))
                    cross = term if cross is None else cross + term
                strain = (2.0 * (f0 * g0 + f1 * g1 + f2 * g2) + cross) * w
                inertia = None
                for i in range(3):
                    term = acc[h, i, a, b] * adj_vel[h, i, a, b]
                    inertia = term if inertia is None else inertia + term
                for t, term in enumerate((trace, strain, inertia * w)):
                    at = t * 125 + a * 25 + b * 5
                    if first is None:
                        dense[h, at : at + 5, :] = term[0:5]
                    else:
                        dense[h, at : at + 5, :] = first[h, at : at + 5, :] + term[0:5]

    halves(1, one)


def fetch(src, dst, sem):
    copy = pltpu.make_async_copy(src, dst, sem)
    copy.start()
    return copy


def start_common(src, rinv, perms, acc, vel, stress, up, down, yj, zj, with_r):
    src = flat(src, 2250)
    up, down = (flat(r, r.shape[0] * 2) for r in (up, down))
    load_fields(src, 0, vel, 3)
    load_fields(src, 3, stress, 6)
    local_acceleration(stress, rinv, acc, perms, yj, zj)
    for dst, a in ((up, 4), (down, 0)):
        for i in range(3):
            dst[50 * i : 50 * i + 50, :] = src[250 * (3, 8, 7)[i] + 50 * a : 250 * (3, 8, 7)[i] + 50 * a + 50, :]
            for h in range(2):
                pack_face(dst, 3 + i, vel[h, i, a] + time_step * acc[h, i, a], h)
        if with_r:
            for h in range(2):
                pack_face(dst, 6, 0.05 * rinv[h, a], h)


def load_material(mat, k, dst):
    for g in range(25):
        for h in range(2):
            dst[h, g // 5, g % 5, 0:5, :] = mat[5 * g : 5 * g + 5, k, 128 * h : 128 * h + 128]


def forward_start_kernel(state_hbm, mat_hbm, nbr_hbm, up, down, acc, vel, stress, rinv, perms, yj, zj, state, mat, nbr, sems):
    first = fetch(nbr_hbm, nbr, sems.at[0])
    second = fetch(mat_hbm, mat, sems.at[1])
    third = fetch(state_hbm, state, sems.at[2])
    first.wait()
    make_perms(nbr, perms)
    second.wait()
    load_material(mat, 2, rinv)
    for h in range(2):
        for a in range(5):
            rinv[h, a] = 1.0 / rinv[h, a]
    zj[...] = jnp.zeros(zj.shape, f32)
    third.wait()
    start_common(state, rinv, perms, acc, vel, stress, up, down, yj, zj, True)


def adjoint_start_kernel(state, mat, rinv, perms, receivers, residuals, up, down, acc, vel, stress, lam, mu,
                         end_grads, injected, yj, zj):
    zj[...] = jnp.zeros(zj.shape, f32)
    injected[...] = receiver_rows(receivers, residuals)
    start_common(state, rinv, perms, acc, vel, stress, up, down, yj, zj, False)
    for k, dst in ((0, lam), (1, mu)):
        load_material(mat, k, dst)
        for h in range(2):
            for a in range(5):
                dst[h, a] = time_step * dst[h, a]
    plain_gradients(vel, end_grads)


def finish_step(rows, vel_in, stress_in, lam, mu, rinv, perms, vel, stress, acc, halo, grads, yj, zj):
    finish_acceleration(acc, stress_in, rinv, halo, True)
    velocities(vel_in, vel, acc, rows)
    jump_gradients(vel, halo, grads, perms, yj, zj)
    update_stress(stress_in, stress, grads, lam, mu)


def middle_kernel(kind, vel_in, stress_in, acc_in, lam, mu, rinv, perms, inject,
                  below, above, r_below, r_above, up, down, vel, stress, acc, *rest):
    next_acc, (halo, grads, yj, zj) = (rest[0], rest[1:]) if kind == "receiver" else (None, rest)
    rows = [inject[i : i + 1] for i in range(3)] if kind == "receiver" else source_rows(0, *inject)
    zj[...] = jnp.zeros(zj.shape, f32)
    load_halo(halo, *(flat(r, r.shape[0] * 2) for r in (below, above, r_below, r_above)), 6)
    acc[...] = acc_in[...]
    finish_step(rows, vel_in, stress_in, lam, mu, rinv, perms, vel, stress, acc, halo, grads, yj, zj)
    if kind == "receiver":
        local_acceleration(stress, rinv, next_acc, perms, yj, zj)
    for dst, a in ((up, 4), (down, 0)):
        dst = flat(dst, dst.shape[0] * 2)
        for i in range(3):
            for h in range(2):
                pack_face(dst, i, stress[h, (0, 5, 4)[i], a], h)
                if kind == "receiver":
                    pack_face(dst, 3 + i, vel[h, i, a] + time_step * next_acc[h, i, a], h)


def last_kernel(vel_in, stress_in, acc_in, lam, mu, rinv, perms, inject,
                below, above, r_below, r_above, out, vel, stress, acc, halo, grads, yj, zj):
    zj[...] = jnp.zeros(zj.shape, f32)
    load_halo(halo, *(flat(r, r.shape[0] * 2) for r in (below, above, r_below, r_above)), 6)
    acc[...] = acc_in[...]
    rows = [inject[8 + i : 9 + i] for i in range(3)]
    finish_step(rows, vel_in, stress_in, lam, mu, rinv, perms, vel, stress, acc, halo, grads, yj, zj)
    dst = flat(out, 2250)
    for first, field, count in ((0, vel, 3), (3, stress, 6)):

        def one(k, carry):
            for g in range(25):
                for h in range(2):
                    dst[pl.ds(250 * (first + k) + 10 * g + h, 5, 2), :] = field[h, k, g // 5, g % 5, 0:5, :]
            return carry

        lax.fori_loop(0, count, one, 0)


def first_image_kernel(f_vel, f_acc, a_vel, f_stress, rinv, perms, dense, next_acc, fg, ag, yj, zj):
    zj[...] = jnp.zeros(zj.shape, f32)
    local_acceleration(f_stress, rinv, next_acc, perms, yj, zj)
    plain_gradients(f_vel, fg)
    plain_gradients(a_vel, ag)
    image(fg, ag, f_acc, a_vel, dense, None)


def last_image_kernel(f_vel, acc_in, adj_vel, end_grads, first, rinv, where_ref, strength, below, above,
                      keep, send, halo, vel, acc, fg, dense):
    load_halo(halo, flat(below, 150), flat(above, 150), None, None, 3)
    acc[...] = acc_in[...]
    finish_acceleration(acc, None, rinv, halo, False)
    velocities(f_vel, vel, acc, source_rows(1, where_ref, strength))
    plain_gradients(vel, fg)
    for h in range(2):
        dense[h, 368:384, :] = jnp.zeros((16, 128), f32)
    image(fg, end_grads, acc, adj_vel, dense, first)
    core = lax.rem(lax.axis_index("shot"), 2)
    turned = [dense[h].T for h in range(2)]
    for parity, (mine, other) in ((0, (keep, send)), (1, (send, keep))):

        @pl.when(core == parity)
        def _():
            for s in range(16):
                piece = turned[s // 8][16 * (s % 8) : 16 * (s % 8) + 16]
                (mine if s % 2 == 0 else other)[s // 2] = piece


V = pl.BlockSpec(memory_space=pltpu.VMEM)
S = pl.BlockSpec(memory_space=pltpu.SMEM)


def shape(*dims):
    return jax.ShapeDtypeStruct(dims, f32)


def field(count):
    return shape(2, count, 5, 5, 8, 128)


ONE = shape(2, 5, 5, 8, 128)
PERMS = jax.ShapeDtypeStruct((4, N, N), bf16)


def sends(faces):
    return shape(faces * 25, 2, 128)


def scr(s):
    return pltpu.VMEM(s.shape, s.dtype)


JUMPS = [pltpu.VMEM((2, 2, 3, 5, 8, 128), f32), pltpu.VMEM((2, 3, 5, 5, 8, 128), f32)]
HALO = pltpu.VMEM((2, 2, 7, 5, 8, 128), f32)


def call(kernel, specs, outs, scratch, flops, moved):
    return pl.pallas_call(
        kernel,
        out_shape=outs,
        in_specs=specs,
        out_specs=jax.tree.map(lambda _: V, outs),
        scratch_shapes=scratch,
        compiler_params=pltpu.CompilerParams(vmem_limit_bytes=8 * 2**20),
        cost_estimate=pl.CostEstimate(flops=flops, bytes_accessed=moved, transcendentals=0),
    )


def passed_along(value, axis, steps):
    count = lax.axis_size(axis)
    pairs = [(source, (source + steps) % count) for source in range(count)]
    return lax.ppermute(value, axis, pairs)


def both_ways(up, down):
    return passed_along(up, "slab", 1), passed_along(down, "slab", -1)


def core_sum_kernel(keep, got, mine, *others):
    line = lax.div(lax.axis_index("shot"), 4)
    for d, dst in enumerate((mine, *others)):
        to = lax.rem(line + d, 4)
        for high in range(2):
            dst[high] = keep[2 * to + high] + got[2 * to + high]


def line_sum_kernel(mine, one, two, three, keep, send):
    high = lax.rem(lax.div(lax.axis_index("shot"), 2), 2)
    for dst, k in ((keep, high), (send, 1 - high)):
        dst[...] = (mine[k] + one[k]) + (two[k] + three[k])


def last_sum_kernel(keep, got, out):
    turned = (keep[...] + got[...]).T
    for t in range(3):
        out[:, t, :] = turned[125 * t : 125 * t + 125]


def reduce_over_shots(keep, send):
    hop = lambda v, to: lax.ppermute(v, "shot", [(i, to(i)) for i in range(16)])
    pair, chunk = shape(2, 16, 384), shape(16, 384)
    mine, *others = call(core_sum_kernel, [V] * 2, (pair,) * 4, [], 1000, 1000)(keep, hop(send, lambda i: i ^ 1))
    got = [hop(x, lambda i: (i + 4 * d) % 16) for d, x in enumerate(others, 1)]
    keep, send = call(line_sum_kernel, [V] * 4, (chunk,) * 2, [], 1000, 1000)(mine, *got)
    return call(last_sum_kernel, [V] * 2, shape(125, 3, 16), [], 1000, 1000)(keep, hop(send, lambda i: i ^ 2))


def body(fwd, adj, materials, nbr, source_element, pulse, receivers, residuals):
    receivers = receivers.reshape(1, N)
    fwd, adj = (x.reshape(1125, 2, 128) for x in (fwd, adj))
    mat = materials.transpose(1, 2, 3, 0, 4).reshape(125, 3, N)
    nbr = nbr.T
    residuals = residuals.transpose(0, 2, 1, 3).reshape(3, 2, N)

    f_up, f_down, f_acc, f_vel, f_stress, rinv, perms = call(
        forward_start_kernel,
        [pl.BlockSpec(memory_space=pltpu.HBM)] * 3,
        (sends(7), sends(7), field(3), field(3), field(6), ONE, PERMS),
        JUMPS + [scr(shape(1125, 2, 128)), scr(shape(125, 3, N)), pltpu.VMEM((4, N), jnp.int32), pltpu.SemaphoreType.DMA((3,))],
        10**8, 4 * 10**6,
    )(*(pltpu.with_memory_space_constraint(x, pltpu.HBM) for x in (fwd, mat, nbr)))
    f_below, f_above = both_ways(f_up, f_down)
    a_up, a_down, a_acc, a_vel, a_stress, lam, mu, end_grads, injected = call(
        adjoint_start_kernel,
        [V] * 6,
        (sends(6), sends(6), field(3), field(3), field(6), ONE, ONE, field(9), shape(16, N)),
        JUMPS,
        10**8, 4 * 10**6,
    )(adj, mat, rinv, perms, receivers, residuals)
    a_below, a_above = both_ways(a_up, a_down)
    adj_vel_end = a_vel

    def middle(kind, vel, stress, acc, inject, below, above, faces):
        if kind == "source":
            kernel = lambda *refs: middle_kernel(kind, *refs[:7], refs[7:9], *refs[9:])
            held = [S] * 2
        else:
            kernel = lambda *refs: middle_kernel(kind, *refs)
            held = [V]
        return call(
            kernel,
            [V] * 7 + held + [V] * 4,
            (sends(faces), sends(faces), field(3), field(6), field(3)) + (() if kind == "source" else (field(3),)),
            [HALO, scr(field(9))] + JUMPS,
            2 * 10**8, 8 * 10**6,
        )(vel, stress, acc, lam, mu, rinv, perms, *inject, below, above, f_below, f_above)

    f_up, f_down, f_vel1, f_stress1, f_acc1 = middle(
        "source", f_vel, f_stress, f_acc, (source_element, pulse), f_below, f_above, 3
    )
    f_below2, f_above2 = both_ways(f_up, f_down)
    a_up, a_down, a_vel1, a_stress1, _, a_acc2 = middle(
        "receiver", a_vel, a_stress, a_acc, (injected,), a_below, a_above, 6
    )
    a_below2, a_above2 = both_ways(a_up, a_down)
    first, f_acc2 = call(
        first_image_kernel,
        [V] * 6,
        (shape(2, 384, 128), field(3)),
        [scr(field(9)), scr(field(9))] + JUMPS,
        1000, 1000,
    )(f_vel1, f_acc1, a_vel1, f_stress1, rinv, perms)
    keep, send = call(
        last_image_kernel,
        [V] * 6 + [S] * 2 + [V] * 2,
        (shape(8, 16, 384), shape(8, 16, 384)),
        [HALO, scr(field(3)), scr(field(3)), scr(field(9)), scr(shape(2, 384, 128))],
        1000, 1000,
    )(f_vel1, f_acc2, adj_vel_end, end_grads, first, rinv, source_element, pulse, f_below2, f_above2)
    gradient = reduce_over_shots(keep, send)
    adjoint_end = call(
        last_kernel,
        [V] * 12,
        shape(1125, 2, 128),
        [scr(field(3)), scr(field(6)), scr(field(3)), HALO, scr(field(9))] + JUMPS,
        10**8, 8 * 10**6,
    )(a_vel1, a_stress1, a_acc2, lam, mu, rinv, perms, injected, a_below2, a_above2, f_below, f_above)
    return gradient.reshape(5, 5, 5, 3, 16).transpose(3, 0, 1, 2, 4), adjoint_end.reshape(1, 9, 5, 5, 5, N)


def solution(mesh):
    return jax.shard_map(
        body,
        mesh=mesh,
        in_specs=(
            P("shot", None, None, None, None, "slab"),
            P("shot", None, None, None, None, "slab"),
            P(None, None, None, None, "slab"),
            P(),
            P("shot"),
            P("shot", None, None),
            P(),
            P("shot", None, None, None),
        ),
        out_specs=(
            P(None, None, None, None, ("slab", "shot")),
            P("shot", None, None, None, None, "slab"),
        ),
        check_vma=False,
    )
```

```python
import math

import jax
import jax.numpy as jnp
import numpy as np
from jax import lax
from jax.experimental import pallas as pl
from jax.experimental.pallas import tpu as pltpu
from jax.sharding import PartitionSpec as P

f32 = jnp.float32
bf16 = jnp.bfloat16

time_step = 0.01
N = 256


def tables():
    root = math.sqrt(3.0 / 7.0)
    points = np.array([-1.0, -root, 0.0, root, 1.0])
    legendre = (35.0 * points**4 - 30.0 * points**2 + 3.0) / 8.0
    matrix = np.zeros((5, 5))
    for r in range(5):
        for c in range(5):
            if r != c:
                matrix[r, c] = legendre[r] / (legendre[c] * (points[r] - points[c]))
    matrix[0, 0] = -5.0
    matrix[4, 4] = 5.0
    quad = np.array([0.1, 49.0 / 90.0, 32.0 / 45.0, 49.0 / 90.0, 0.1])
    return matrix, quad


D_PLAIN, QUAD = tables()
D_LIFT = D_PLAIN.copy()
D_LIFT[0, 0] += 5.0
D_LIFT[4, 4] -= 5.0


def split(x):
    high = x.astype(bf16)
    return high, (x - high.astype(f32)).astype(bf16)


def dot(a, b):
    return lax.dot_general(a, b, (((1,), (0,)), ((), ())), preferred_element_type=f32)


def derive_rows(rows, matrix):
    even0, odd0 = rows[0] + rows[4], rows[0] - rows[4]
    even1, odd1 = rows[1] + rows[3], rows[1] - rows[3]
    out = [None] * 5
    for r in (0, 1):
        m = [float(v) for v in matrix[r]]
        p = 0.5 * (m[0] + m[4]) * even0 + 0.5 * (m[1] + m[3]) * even1 + m[2] * rows[2]
        q = 0.5 * (m[0] - m[4]) * odd0 + 0.5 * (m[1] - m[3]) * odd1
        out[r] = q + p
        out[4 - r] = q - p
    out[2] = float(matrix[2, 0]) * odd0 + float(matrix[2, 1]) * odd1
    return out


class Along:
    def __init__(self, matrix):
        row = lax.broadcasted_iota(jnp.int32, (8, 128), 0)
        self.places = [jnp.where(row < 5, lax.rem(row + m, 5), row) for m in range(1, 5)]
        self.factors = []
        for m in range(1, 5):
            self.factors.append(self.by_row(row, [matrix[c, (c + m) % 5] for c in range(5)]))
        own = [matrix[c, c] for c in range(5)]
        self.own = self.by_row(row, own) if any(own) else None

    @staticmethod
    def by_row(row, values):
        out = jnp.zeros((8, 128), f32)
        for c in range(5):
            out = jnp.where(row == c, float(values[c]), out)
        return out

    def __call__(self, tile):
        total = None if self.own is None else tile * self.own
        for place, factor in zip(self.places, self.factors):
            term = jnp.take_along_axis(tile, place, axis=0) * factor
            total = term if total is None else total + term
        return total


def flat(ref, rows):
    return ref.reshape(rows, 128)


def make_perms(nbr, perms):
    source = lax.broadcasted_iota(jnp.int32, (N, N), 0)
    for k in range(4):
        hit = source == nbr[k : k + 1, :]
        perms[k] = jnp.where(hit, -5.0 if k % 2 == 0 else 5.0, 0.0).astype(bf16)


def permuted(face, matrix):
    rows = face.shape[0]
    both = dot(jnp.concatenate(split(face), axis=0), matrix)
    return both[:rows] + both[rows:]


def jumps(field, ys, first_z, perms, yj, zj):
    count = field.shape[1]
    for side, b in ((0, 4), (1, 0)):
        face = jnp.concatenate(
            [
                jnp.concatenate([field[h, k, :, b].reshape(40, 128) for h in range(2)], axis=1)
                for k in ys
            ],
            axis=0,
        )
        got = permuted(face, perms[side])
        for h in range(2):
            for i in range(3):
                part = got[40 * i : 40 * i + 40, 128 * h : 128 * h + 128]
                yj[side, h, i] = part.reshape(5, 8, 128)
    rows = flat(field, 2 * count * 200)
    into = flat(zj, 1200)
    spare = jnp.zeros((5, N), f32)
    for side, c in ((0, 4), (1, 0)):
        face = jnp.concatenate(
            [rows[pl.ds((h * count + first_z) * 200 + c, 75, 8), :] for h in range(2)], axis=1
        )
        got = permuted(jnp.concatenate([face, spare], axis=0), perms[2 + side])
        for h in range(2):
            into[pl.ds(h * 600 + (0, 4)[side], 75, 8), :] = got[:75, 128 * h : 128 * h + 128]


def stress_of(i, d):
    return jnp.where(i == d, i, 6 - i - d)


def halves(count, one):
    def step(t, carry):
        one(lax.div(t, 2), lax.rem(t, 2))
        return carry

    lax.fori_loop(0, 2 * count, step, 0)


def local_acceleration(stress, rinv, acc, perms, yj, zj):
    along = Along(D_LIFT)
    jumps(stress, (5, 1, 3), 2, perms, yj, zj)

    def one(i, h):
        kx, ky, kz = stress_of(i, 0), stress_of(i, 1), stress_of(i, 2)
        for a in range(5):
            ys = derive_rows([stress[h, ky, a, b] for b in range(5)], D_LIFT)
            ys[0] = ys[0] + yj[0, h, i, a]
            ys[4] = ys[4] + yj[1, h, i, a]
            for b in range(5):
                acc[h, i, a, b] = ys[b] + (along(stress[h, kz, a, b]) + zj[h, 2 - i, a, b])
        for b in range(5):
            xs = derive_rows([stress[h, kx, a, b] for a in range(5)], D_LIFT)
            for a in range(5):
                acc[h, i, a, b] = (acc[h, i, a, b] + xs[a]) * rinv[h, a, b]

    halves(3, one)


def load_fields(src, first, dst, count):
    def one(k, carry):
        for g in range(25):
            for h in range(2):
                dst[h, k, g // 5, g % 5, 0:5, :] = src[pl.ds(250 * (first + k) + 10 * g + h, 5, 2), :]
        return carry

    lax.fori_loop(0, count, one, 0)


def pack_face(dst, k, value, h):
    for b in range(5):
        dst[pl.ds(50 * k + 10 * b + h, 5, 2), :] = value[b, 0:5]


def unpack_face(dst, side, k, src, j):
    for h in range(2):
        for b in range(5):
            dst[side, h, k, b, 0:5, :] = src[pl.ds(50 * j + 10 * b + h, 5, 2), :]


def load_halo(halo, first, second, r_first, r_second, count):
    odd = lax.rem(lax.axis_index("slab"), 2)
    for side, src in ((1 - odd, first), (odd, second)):
        for k in range(count):
            unpack_face(halo, side, k, src, k)
    if r_first is not None:
        for side, src in ((1 - odd, r_first), (odd, r_second)):
            unpack_face(halo, side, 6, src, 6)


def pack_faces(first, second, values):
    odd = lax.rem(lax.axis_index("slab"), 2)
    for dst, a in ((first, 4 * (1 - odd)), (second, 4 * odd)):
        dst = flat(dst, dst.shape[0] * 2)
        for h in range(2):
            for k, value in enumerate(values(a, h)):
                pack_face(dst, k, value, h)


def finish_acceleration(acc, stress, rinv, halo, has_v):
    for h in range(2):
        for i in range(3):
            k = (0, 5, 4)[i]
            acc[h, i, 0] = acc[h, i, 0] - 5.0 * rinv[h, 0] * halo[0, h, i]
            acc[h, i, 4] = acc[h, i, 4] + 5.0 * rinv[h, 4] * halo[1, h, i]
            if has_v:
                halo[0, h, 3 + i] = halo[0, h, 3 + i] + halo[0, h, 6] * stress[h, k, 0]
                halo[1, h, 3 + i] = halo[1, h, 3 + i] - halo[1, h, 6] * stress[h, k, 4]


def source_rows(step, where_ref, pulse):
    lane = lax.broadcasted_iota(jnp.int32, (1, N), 1) + slab_base()
    hit = lane == where_ref[0]
    return [jnp.where(hit, pulse[0, step, i], 0.0) for i in range(3)]


def receiver_rows(where_ref, residual):
    element = lax.broadcasted_iota(jnp.int32, (N, N), 0) + slab_base()
    hits = jnp.where(element == where_ref[...], 1.0, 0.0).astype(bf16)
    spare = jnp.zeros((5, N), f32)
    x = jnp.concatenate([r for step in range(2) for r in [residual[i, step : step + 1] for i in range(3)] + [spare]], axis=0)
    total = None
    for part in range(3):
        high = x.astype(bf16)
        x = x - high.astype(f32)
        term = lax.dot_general(high, hits, (((1,), (1,)), ((), ())), preferred_element_type=f32)
        total = term if total is None else total + term
    return total


def slab_base():
    return lax.axis_index("slab") * N


def velocities(vel_in, vel, acc, rows):
    def one(i, h):
        for a in range(5):
            vel[h, i, a] = vel_in[h, i, a] + time_step * acc[h, i, a]

    halves(3, one)
    mask = lax.broadcasted_iota(jnp.int32, (8, 128), 0) == 2
    for i in range(3):
        for h in range(2):
            vel[h, i, 2, 2] += jnp.where(mask, rows[i][:, 128 * h : 128 * h + 128], 0.0)


def jump_gradients(vel, halo, grads, perms, yj, zj):
    along = Along(D_LIFT)
    jumps(vel, (0, 1, 2), 0, perms, yj, zj)

    def one(i, h):
        for a in range(5):
            ys = derive_rows([vel[h, i, a, b] for b in range(5)], D_LIFT)
            ys[0] = ys[0] + yj[0, h, i, a]
            ys[4] = ys[4] + yj[1, h, i, a]
            for b in range(5):
                grads[h, 3 + i, a, b] = ys[b]
                grads[h, 6 + i, a, b] = along(vel[h, i, a, b]) + zj[h, i, a, b]
        for b in range(5):
            xs = derive_rows([vel[h, i, a, b] for a in range(5)], D_LIFT)
            xs[0] = xs[0] - 5.0 * halo[0, h, 3 + i, b]
            xs[4] = xs[4] + 5.0 * halo[1, h, 3 + i, b]
            for a in range(5):
                grads[h, i, a, b] = xs[a]

    halves(3, one)


def update_stress(stress_in, stress, grads, lam, mu):
    def one(a, h):
        g = lambda j, i: grads[h, 3 * j + i, a]
        l, m = lam[h, a], mu[h, a]
        both = l * (g(0, 0) + g(1, 1) + g(2, 2))
        for i in range(3):
            stress[h, i, a] = stress_in[h, i, a] + (both + 2.0 * m * g(i, i))
        stress[h, 3, a] = stress_in[h, 3, a] + m * (g(2, 1) + g(1, 2))
        stress[h, 4, a] = stress_in[h, 4, a] + m * (g(2, 0) + g(0, 2))
        stress[h, 5, a] = stress_in[h, 5, a] + m * (g(1, 0) + g(0, 1))

    halves(5, one)


def plain_gradients(vel, grads):
    along = Along(D_PLAIN)

    def one(i, h):
        for a in range(5):
            ys = derive_rows([vel[h, i, a, b] for b in range(5)], D_PLAIN)
            for b in range(5):
                grads[h, 3 + i, a, b] = ys[b]
                grads[h, 6 + i, a, b] = along(vel[h, i, a, b])
        for b in range(5):
            xs = derive_rows([vel[h, i, a, b] for a in range(5)], D_PLAIN)
            for a in range(5):
                grads[h, i, a, b] = xs[a]

    halves(3, one)


def image(fg, ag, acc, adj_vel, dense, first):
    row = lax.broadcasted_iota(jnp.int32, (8, 128), 0)
    weight = Along.by_row(row, QUAD)

    def one(k, h):
        for a in range(5):
            for b in range(5):
                f = lambda j, i: fg[h, 3 * j + i, a, b]
                g = lambda j, i: ag[h, 3 * j + i, a, b]
                w = weight * float(QUAD[a] * QUAD[b])
                f0, f1, f2 = f(0, 0), f(1, 1), f(2, 2)
                g0, g1, g2 = g(0, 0), g(1, 1), g(2, 2)
                trace = (f0 + f1 + f2) * (g0 + g1 + g2) * w
                cross = None
                for i, j in ((0, 1), (0, 2), (1, 2)):
                    term = (f(j, i) + f(i, j)) * (g(j, i) + g(i, j))
                    cross = term if cross is None else cross + term
                strain = (2.0 * (f0 * g0 + f1 * g1 + f2 * g2) + cross) * w
                inertia = None
                for i in range(3):
                    term = acc[h, i, a, b] * adj_vel[h, i, a, b]
                    inertia = term if inertia is None else inertia + term
                for t, term in enumerate((trace, strain, inertia * w)):
                    at = t * 125 + a * 25 + b * 5
                    if first is None:
                        dense[h, at : at + 5, :] = term[0:5]
                    else:
                        dense[h, at : at + 5, :] = first[h, at : at + 5, :] + term[0:5]

    halves(1, one)


def fetch(src, dst, sem):
    copy = pltpu.make_async_copy(src, dst, sem)
    copy.start()
    return copy


def start_common(src, rinv, perms, acc, vel, stress, one, two, yj, zj, with_r):
    src = flat(src, 2250)
    load_fields(src, 0, vel, 3)
    load_fields(src, 3, stress, 6)
    local_acceleration(stress, rinv, acc, perms, yj, zj)

    def values(a, h):
        out = [stress[h, k, a] for k in (0, 5, 4)] + [vel[h, i, a] + time_step * acc[h, i, a] for i in range(3)]
        return out + ([0.05 * rinv[h, a]] if with_r else [])

    pack_faces(one, two, values)


def load_material(mat, k, dst):
    for g in range(25):
        for h in range(2):
            dst[h, g // 5, g % 5, 0:5, :] = mat[5 * g : 5 * g + 5, k, 128 * h : 128 * h + 128]


def forward_start_kernel(state_hbm, mat_hbm, nbr_hbm, one, two, acc, vel, stress, rinv, perms, yj, zj, state, mat, nbr, sems):
    first = fetch(nbr_hbm, nbr, sems.at[0])
    second = fetch(mat_hbm, mat, sems.at[1])
    third = fetch(state_hbm, state, sems.at[2])
    first.wait()
    make_perms(nbr, perms)
    second.wait()
    load_material(mat, 2, rinv)
    for h in range(2):
        for a in range(5):
            rinv[h, a] = 1.0 / rinv[h, a]
    zj[...] = jnp.zeros(zj.shape, f32)
    third.wait()
    start_common(state, rinv, perms, acc, vel, stress, one, two, yj, zj, True)


def adjoint_start_kernel(state, mat, rinv, perms, receivers, residuals, one, two, acc, vel, stress, lam, mu,
                         end_grads, injected, yj, zj):
    zj[...] = jnp.zeros(zj.shape, f32)
    injected[...] = receiver_rows(receivers, residuals)
    start_common(state, rinv, perms, acc, vel, stress, one, two, yj, zj, False)
    for k, dst in ((0, lam), (1, mu)):
        load_material(mat, k, dst)
        for h in range(2):
            for a in range(5):
                dst[h, a] = time_step * dst[h, a]
    plain_gradients(vel, end_grads)


def finish_step(rows, vel_in, stress_in, lam, mu, rinv, perms, vel, stress, acc, halo, grads, yj, zj):
    finish_acceleration(acc, stress_in, rinv, halo, True)
    velocities(vel_in, vel, acc, rows)
    jump_gradients(vel, halo, grads, perms, yj, zj)
    update_stress(stress_in, stress, grads, lam, mu)


def middle_kernel(kind, vel_in, stress_in, acc_in, lam, mu, rinv, perms, inject,
                  near, far, r_near, r_far, one, two, vel, stress, acc, *rest):
    next_acc, (halo, grads, yj, zj) = (rest[0], rest[1:]) if kind == "receiver" else (None, rest)
    rows = [inject[i : i + 1] for i in range(3)] if kind == "receiver" else source_rows(0, *inject)
    zj[...] = jnp.zeros(zj.shape, f32)
    load_halo(halo, *(flat(r, r.shape[0] * 2) for r in (near, far, r_near, r_far)), 6)
    acc[...] = acc_in[...]
    finish_step(rows, vel_in, stress_in, lam, mu, rinv, perms, vel, stress, acc, halo, grads, yj, zj)
    if kind == "receiver":
        local_acceleration(stress, rinv, next_acc, perms, yj, zj)

    def values(a, h):
        out = [stress[h, k, a] for k in (0, 5, 4)]
        if kind == "receiver":
            out += [vel[h, i, a] + time_step * next_acc[h, i, a] for i in range(3)]
        return out

    pack_faces(one, two, values)


def last_kernel(vel_in, stress_in, acc_in, lam, mu, rinv, perms, inject,
                near, far, r_near, r_far, out, vel, stress, acc, halo, grads, yj, zj):
    zj[...] = jnp.zeros(zj.shape, f32)
    load_halo(halo, *(flat(r, r.shape[0] * 2) for r in (near, far, r_near, r_far)), 6)
    acc[...] = acc_in[...]
    rows = [inject[8 + i : 9 + i] for i in range(3)]
    finish_step(rows, vel_in, stress_in, lam, mu, rinv, perms, vel, stress, acc, halo, grads, yj, zj)
    dst = flat(out, 2250)
    for first, field, count in ((0, vel, 3), (3, stress, 6)):

        def one(k, carry):
            for g in range(25):
                for h in range(2):
                    dst[pl.ds(250 * (first + k) + 10 * g + h, 5, 2), :] = field[h, k, g // 5, g % 5, 0:5, :]
            return carry

        lax.fori_loop(0, count, one, 0)


def first_image_kernel(f_vel, f_acc, a_vel, f_stress, rinv, perms, dense, next_acc, fg, ag, yj, zj):
    zj[...] = jnp.zeros(zj.shape, f32)
    local_acceleration(f_stress, rinv, next_acc, perms, yj, zj)
    plain_gradients(f_vel, fg)
    plain_gradients(a_vel, ag)
    image(fg, ag, f_acc, a_vel, dense, None)


def last_image_kernel(f_vel, acc_in, adj_vel, end_grads, first, rinv, where_ref, strength, near, far,
                      keep, send, halo, vel, acc, fg, dense):
    load_halo(halo, flat(near, 150), flat(far, 150), None, None, 3)
    acc[...] = acc_in[...]
    finish_acceleration(acc, None, rinv, halo, False)
    velocities(f_vel, vel, acc, source_rows(1, where_ref, strength))
    plain_gradients(vel, fg)
    for h in range(2):
        dense[h, 368:384, :] = jnp.zeros((16, 128), f32)
    image(fg, end_grads, acc, adj_vel, dense, first)
    core = lax.rem(lax.axis_index("shot"), 2)
    turned = [dense[h].T for h in range(2)]
    for parity, (mine, other) in ((0, (keep, send)), (1, (send, keep))):

        @pl.when(core == parity)
        def _():
            for s in range(16):
                piece = turned[s // 8][16 * (s % 8) : 16 * (s % 8) + 16]
                (mine if s % 2 == 0 else other)[s // 2] = piece


V = pl.BlockSpec(memory_space=pltpu.VMEM)
S = pl.BlockSpec(memory_space=pltpu.SMEM)


def shape(*dims):
    return jax.ShapeDtypeStruct(dims, f32)


def field(count):
    return shape(2, count, 5, 5, 8, 128)


ONE = shape(2, 5, 5, 8, 128)
PERMS = jax.ShapeDtypeStruct((4, N, N), bf16)


def sends(faces):
    return shape(faces * 25, 2, 128)


def scr(s):
    return pltpu.VMEM(s.shape, s.dtype)


JUMPS = [pltpu.VMEM((2, 2, 3, 5, 8, 128), f32), pltpu.VMEM((2, 3, 5, 5, 8, 128), f32)]
HALO = pltpu.VMEM((2, 2, 7, 5, 8, 128), f32)


def call(kernel, specs, outs, scratch, flops, moved):
    return pl.pallas_call(
        kernel,
        out_shape=outs,
        in_specs=specs,
        out_specs=jax.tree.map(lambda _: V, outs),
        scratch_shapes=scratch,
        compiler_params=pltpu.CompilerParams(vmem_limit_bytes=8 * 2**20),
        cost_estimate=pl.CostEstimate(flops=flops, bytes_accessed=moved, transcendentals=0),
    )


def both_ways(first, second):
    count = lax.axis_size("slab")
    near = [(i, i ^ 1) for i in range(count)]
    far = [(i, (i + (1 if i % 2 else -1)) % count) for i in range(count)]
    return lax.ppermute(first, "slab", near), lax.ppermute(second, "slab", far)


def core_sum_kernel(keep, got, mine, *others):
    line = lax.div(lax.axis_index("shot"), 4)
    for d, dst in enumerate((mine, *others)):
        to = lax.rem(line + d, 4)
        for high in range(2):
            dst[high] = keep[2 * to + high] + got[2 * to + high]


def line_sum_kernel(mine, one, two, three, keep, send):
    high = lax.rem(lax.div(lax.axis_index("shot"), 2), 2)
    for dst, k in ((keep, high), (send, 1 - high)):
        dst[...] = (mine[k] + one[k]) + (two[k] + three[k])


def last_sum_kernel(keep, got, out, rows):
    turned = (keep[...] + got[...]).T
    for t in range(3):
        rows[pl.ds(t, 125, 4), 0:16] = turned[125 * t : 125 * t + 125]
    out[...] = rows.reshape(125, 4, 128)[:, 0:3, 0:16]


def reduce_over_shots(keep, send):
    hop = lambda v, to: lax.ppermute(v, "shot", [(i, to(i)) for i in range(16)])
    pair, chunk = shape(2, 16, 384), shape(16, 384)
    mine, *others = call(core_sum_kernel, [V] * 2, (pair,) * 4, [], 1000, 1000)(keep, hop(send, lambda i: i ^ 1))
    got = [hop(x, lambda i: (i + 4 * d) % 16) for d, x in enumerate(others, 1)]
    keep, send = call(line_sum_kernel, [V] * 4, (chunk,) * 2, [], 1000, 1000)(mine, *got)
    return call(last_sum_kernel, [V] * 2, shape(125, 3, 16), [scr(shape(500, 128))], 1000, 1000)(keep, hop(send, lambda i: i ^ 2))


def body(fwd, adj, materials, nbr, source_element, pulse, receivers, residuals):
    receivers = receivers.reshape(1, N)
    fwd, adj = (x.reshape(1125, 2, 128) for x in (fwd, adj))
    mat = materials.transpose(1, 2, 3, 0, 4).reshape(125, 3, N)
    nbr = nbr.T
    residuals = residuals.transpose(0, 2, 1, 3).reshape(3, 2, N)

    f_one, f_two, f_acc, f_vel, f_stress, rinv, perms = call(
        forward_start_kernel,
        [pl.BlockSpec(memory_space=pltpu.HBM)] * 3,
        (sends(7), sends(7), field(3), field(3), field(6), ONE, PERMS),
        JUMPS + [scr(shape(1125, 2, 128)), scr(shape(125, 3, N)), pltpu.VMEM((4, N), jnp.int32), pltpu.SemaphoreType.DMA((3,))],
        10**8, 4 * 10**6,
    )(*(pltpu.with_memory_space_constraint(x, pltpu.HBM) for x in (fwd, mat, nbr)))
    f_near, f_far = both_ways(f_one, f_two)
    a_one, a_two, a_acc, a_vel, a_stress, lam, mu, end_grads, injected = call(
        adjoint_start_kernel,
        [V] * 6,
        (sends(6), sends(6), field(3), field(3), field(6), ONE, ONE, field(9), shape(16, N)),
        JUMPS,
        10**8, 4 * 10**6,
    )(adj, mat, rinv, perms, receivers, residuals)
    a_near, a_far = both_ways(a_one, a_two)
    adj_vel_end = a_vel

    def middle(kind, vel, stress, acc, inject, near, far, faces):
        if kind == "source":
            kernel = lambda *refs: middle_kernel(kind, *refs[:7], refs[7:9], *refs[9:])
            held = [S] * 2
        else:
            kernel = lambda *refs: middle_kernel(kind, *refs)
            held = [V]
        return call(
            kernel,
            [V] * 7 + held + [V] * 4,
            (sends(faces), sends(faces), field(3), field(6), field(3)) + (() if kind == "source" else (field(3),)),
            [HALO, scr(field(9))] + JUMPS,
            2 * 10**8, 8 * 10**6,
        )(vel, stress, acc, lam, mu, rinv, perms, *inject, near, far, f_near, f_far)

    f_one, f_two, f_vel1, f_stress1, f_acc1 = middle(
        "source", f_vel, f_stress, f_acc, (source_element, pulse), f_near, f_far, 3
    )
    f_near2, f_far2 = both_ways(f_one, f_two)
    a_one, a_two, a_vel1, a_stress1, _, a_acc2 = middle(
        "receiver", a_vel, a_stress, a_acc, (injected,), a_near, a_far, 6
    )
    a_near2, a_far2 = both_ways(a_one, a_two)
    first, f_acc2 = call(
        first_image_kernel,
        [V] * 6,
        (shape(2, 384, 128), field(3)),
        [scr(field(9)), scr(field(9))] + JUMPS,
        1000, 1000,
    )(f_vel1, f_acc1, a_vel1, f_stress1, rinv, perms)
    keep, send = call(
        last_image_kernel,
        [V] * 6 + [S] * 2 + [V] * 2,
        (shape(8, 16, 384), shape(8, 16, 384)),
        [HALO, scr(field(3)), scr(field(3)), scr(field(9)), scr(shape(2, 384, 128))],
        1000, 1000,
    )(f_vel1, f_acc2, adj_vel_end, end_grads, first, rinv, source_element, pulse, f_near2, f_far2)
    gradient = reduce_over_shots(keep, send)
    adjoint_end = call(
        last_kernel,
        [V] * 12,
        shape(1125, 2, 128),
        [scr(field(3)), scr(field(6)), scr(field(3)), HALO, scr(field(9))] + JUMPS,
        10**8, 8 * 10**6,
    )(a_vel1, a_stress1, a_acc2, lam, mu, rinv, perms, injected, a_near2, a_far2, f_near, f_far)
    return gradient.reshape(5, 5, 5, 3, 16).transpose(3, 0, 1, 2, 4), adjoint_end.reshape(1, 9, 5, 5, 5, N)


def solution(mesh):
    return jax.shard_map(
        body,
        mesh=mesh,
        in_specs=(
            P("shot", None, None, None, None, "slab"),
            P("shot", None, None, None, None, "slab"),
            P(None, None, None, None, "slab"),
            P(),
            P("shot"),
            P("shot", None, None),
            P(),
            P("shot", None, None, None),
        ),
        out_specs=(
            P(None, None, None, None, ("slab", "shot")),
            P("shot", None, None, None, None, "slab"),
        ),
        check_vma=False,
    )
```

```python
import math

import jax
import jax.numpy as jnp
import numpy as np
from jax import lax
from jax.experimental import pallas as pl
from jax.experimental.pallas import tpu as pltpu
from jax.sharding import PartitionSpec as P

f32 = jnp.float32
bf16 = jnp.bfloat16

time_step = 0.01
N = 256


def tables():
    root = math.sqrt(3.0 / 7.0)
    points = np.array([-1.0, -root, 0.0, root, 1.0])
    legendre = (35.0 * points**4 - 30.0 * points**2 + 3.0) / 8.0
    matrix = np.zeros((5, 5))
    for r in range(5):
        for c in range(5):
            if r != c:
                matrix[r, c] = legendre[r] / (legendre[c] * (points[r] - points[c]))
    matrix[0, 0] = -5.0
    matrix[4, 4] = 5.0
    quad = np.array([0.1, 49.0 / 90.0, 32.0 / 45.0, 49.0 / 90.0, 0.1])
    return matrix, quad


D_PLAIN, QUAD = tables()
D_LIFT = D_PLAIN.copy()
D_LIFT[0, 0] += 5.0
D_LIFT[4, 4] -= 5.0


def split(x):
    high = x.astype(bf16)
    return high, (x - high.astype(f32)).astype(bf16)


def dot(a, b):
    return lax.dot_general(a, b, (((1,), (0,)), ((), ())), preferred_element_type=f32)


def derive_rows(rows, matrix):
    even0, odd0 = rows[0] + rows[4], rows[0] - rows[4]
    even1, odd1 = rows[1] + rows[3], rows[1] - rows[3]
    out = [None] * 5
    for r in (0, 1):
        m = [float(v) for v in matrix[r]]
        p = 0.5 * (m[0] + m[4]) * even0 + 0.5 * (m[1] + m[3]) * even1 + m[2] * rows[2]
        q = 0.5 * (m[0] - m[4]) * odd0 + 0.5 * (m[1] - m[3]) * odd1
        out[r] = q + p
        out[4 - r] = q - p
    out[2] = float(matrix[2, 0]) * odd0 + float(matrix[2, 1]) * odd1
    return out


class Along:
    def __init__(self, matrix):
        row = lax.broadcasted_iota(jnp.int32, (8, 128), 0)
        self.places = [jnp.where(row < 5, lax.rem(row + m, 5), row) for m in range(1, 5)]
        self.factors = []
        for m in range(1, 5):
            self.factors.append(self.by_row(row, [matrix[c, (c + m) % 5] for c in range(5)]))
        own = [matrix[c, c] for c in range(5)]
        self.own = self.by_row(row, own) if any(own) else None

    @staticmethod
    def by_row(row, values):
        out = jnp.zeros((8, 128), f32)
        for c in range(5):
            out = jnp.where(row == c, float(values[c]), out)
        return out

    def __call__(self, tile):
        total = None if self.own is None else tile * self.own
        for place, factor in zip(self.places, self.factors):
            term = jnp.take_along_axis(tile, place, axis=0) * factor
            total = term if total is None else total + term
        return total


def flat(ref, rows):
    return ref.reshape(rows, 128)


def make_perms(nbr, perms):
    source = lax.broadcasted_iota(jnp.int32, (N, N), 0)
    for k in range(4):
        hit = source == nbr[k : k + 1, :]
        perms[k] = jnp.where(hit, -5.0 if k % 2 == 0 else 5.0, 0.0).astype(bf16)


def permuted(face, matrix):
    rows = face.shape[0]
    both = dot(jnp.concatenate(split(face), axis=0), matrix)
    return both[:rows] + both[rows:]


def jumps(field, ys, first_z, perms, yj, zj):
    count = field.shape[1]
    for side, b in ((0, 4), (1, 0)):
        face = jnp.concatenate(
            [
                jnp.concatenate([field[h, k, :, b].reshape(40, 128) for h in range(2)], axis=1)
                for k in ys
            ],
            axis=0,
        )
        got = permuted(face, perms[side])
        for h in range(2):
            for i in range(3):
                part = got[40 * i : 40 * i + 40, 128 * h : 128 * h + 128]
                yj[side, h, i] = part.reshape(5, 8, 128)
    rows = flat(field, 2 * count * 200)
    into = flat(zj, 1200)
    spare = jnp.zeros((5, N), f32)
    for side, c in ((0, 4), (1, 0)):
        face = jnp.concatenate(
            [rows[pl.ds((h * count + first_z) * 200 + c, 75, 8), :] for h in range(2)], axis=1
        )
        got = permuted(jnp.concatenate([face, spare], axis=0), perms[2 + side])
        for h in range(2):
            into[pl.ds(h * 600 + (0, 4)[side], 75, 8), :] = got[:75, 128 * h : 128 * h + 128]


def stress_of(i, d):
    return jnp.where(i == d, i, 6 - i - d)


def halves(count, one):
    def step(t, carry):
        one(lax.div(t, 2), lax.rem(t, 2))
        return carry

    lax.fori_loop(0, 2 * count, step, 0)


def local_acceleration(stress, rinv, acc, perms, yj, zj):
    along = Along(D_LIFT)
    jumps(stress, (5, 1, 3), 2, perms, yj, zj)

    def one(i, h):
        kx, ky, kz = stress_of(i, 0), stress_of(i, 1), stress_of(i, 2)
        for a in range(5):
            ys = derive_rows([stress[h, ky, a, b] for b in range(5)], D_LIFT)
            ys[0] = ys[0] + yj[0, h, i, a]
            ys[4] = ys[4] + yj[1, h, i, a]
            for b in range(5):
                acc[h, i, a, b] = ys[b] + (along(stress[h, kz, a, b]) + zj[h, 2 - i, a, b])
        for b in range(5):
            xs = derive_rows([stress[h, kx, a, b] for a in range(5)], D_LIFT)
            for a in range(5):
                acc[h, i, a, b] = (acc[h, i, a, b] + xs[a]) * rinv[h, a, b]

    halves(3, one)


def load_fields(src, first, dst, count):
    def one(k, carry):
        for g in range(25):
            for h in range(2):
                dst[h, k, g // 5, g % 5, 0:5, :] = src[pl.ds(250 * (first + k) + 10 * g + h, 5, 2), :]
        return carry

    lax.fori_loop(0, count, one, 0)


def pack_face(dst, k, value, h):
    for b in range(5):
        dst[pl.ds(50 * k + 10 * b + h, 5, 2), :] = value[b, 0:5]


def unpack_face(dst, side, k, src, j):
    for h in range(2):
        for b in range(5):
            dst[side, h, k, b, 0:5, :] = src[pl.ds(50 * j + 10 * b + h, 5, 2), :]


def load_halo(halo, first, second, r_first, r_second, count):
    odd = lax.rem(lax.axis_index("slab"), 2)
    for side, src in ((1 - odd, first), (odd, second)):
        for k in range(count):
            unpack_face(halo, side, k, src, k)
    if r_first is not None:
        for side, src in ((1 - odd, r_first), (odd, r_second)):
            unpack_face(halo, side, 6, src, 6)


def pack_faces(first, second, values):
    odd = lax.rem(lax.axis_index("slab"), 2)
    for dst, a in ((first, 4 * (1 - odd)), (second, 4 * odd)):
        dst = flat(dst, dst.shape[0] * 2)
        for h in range(2):
            for k, value in enumerate(values(a, h)):
                pack_face(dst, k, value, h)


def finish_acceleration(acc, stress, rinv, halo, has_v):
    for h in range(2):
        for i in range(3):
            k = (0, 5, 4)[i]
            acc[h, i, 0] = acc[h, i, 0] - 5.0 * rinv[h, 0] * halo[0, h, i]
            acc[h, i, 4] = acc[h, i, 4] + 5.0 * rinv[h, 4] * halo[1, h, i]
            if has_v:
                halo[0, h, 3 + i] = halo[0, h, 3 + i] + halo[0, h, 6] * stress[h, k, 0]
                halo[1, h, 3 + i] = halo[1, h, 3 + i] - halo[1, h, 6] * stress[h, k, 4]


def source_rows(step, where_ref, pulse):
    lane = lax.broadcasted_iota(jnp.int32, (1, N), 1) + slab_base()
    hit = lane == where_ref[0]
    return [jnp.where(hit, pulse[0, step, i], 0.0) for i in range(3)]


def receiver_rows(where_ref, residual):
    element = lax.broadcasted_iota(jnp.int32, (N, N), 0) + slab_base()
    hits = jnp.where(element == where_ref[...], 1.0, 0.0).astype(bf16)
    spare = jnp.zeros((5, N), f32)
    x = jnp.concatenate([r for step in range(2) for r in [residual[i, step : step + 1] for i in range(3)] + [spare]], axis=0)
    total = None
    for part in range(3):
        high = x.astype(bf16)
        x = x - high.astype(f32)
        term = lax.dot_general(high, hits, (((1,), (1,)), ((), ())), preferred_element_type=f32)
        total = term if total is None else total + term
    return total


def slab_base():
    return lax.axis_index("slab") * N


def velocities(vel_in, vel, acc, rows):
    def one(i, h):
        for a in range(5):
            vel[h, i, a] = vel_in[h, i, a] + time_step * acc[h, i, a]

    halves(3, one)
    mask = lax.broadcasted_iota(jnp.int32, (8, 128), 0) == 2
    for i in range(3):
        for h in range(2):
            vel[h, i, 2, 2] += jnp.where(mask, rows[i][:, 128 * h : 128 * h + 128], 0.0)


def jump_gradients(vel, halo, grads, plain, perms, yj, zj):
    along = Along(D_LIFT)
    jumps(vel, (0, 1, 2), 0, perms, yj, zj)
    own = Along.by_row(lax.broadcasted_iota(jnp.int32, (8, 128), 0), [-5.0, 0.0, 0.0, 0.0, 5.0])

    def one(i, h):
        for a in range(5):
            v = [vel[h, i, a, b] for b in range(5)]
            ys = derive_rows(v, D_LIFT)
            zs = [along(v[b]) for b in range(5)]
            if plain is not None:
                for b in range(5):
                    plain[h, 3 + i, a, b] = ys[b] + {0: -5.0, 4: 5.0}[b] * v[b] if b in (0, 4) else ys[b]
                    plain[h, 6 + i, a, b] = zs[b] + own * v[b]
            ys[0] = ys[0] + yj[0, h, i, a]
            ys[4] = ys[4] + yj[1, h, i, a]
            for b in range(5):
                grads[h, 3 + i, a, b] = ys[b]
                grads[h, 6 + i, a, b] = zs[b] + zj[h, i, a, b]
        for b in range(5):
            v = [vel[h, i, a, b] for a in range(5)]
            xs = derive_rows(v, D_LIFT)
            if plain is not None:
                for a in range(5):
                    plain[h, i, a, b] = xs[a] + {0: -5.0, 4: 5.0}[a] * v[a] if a in (0, 4) else xs[a]
            xs[0] = xs[0] - 5.0 * halo[0, h, 3 + i, b]
            xs[4] = xs[4] + 5.0 * halo[1, h, 3 + i, b]
            for a in range(5):
                grads[h, i, a, b] = xs[a]

    halves(3, one)


def update_stress(stress_in, stress, grads, lam, mu):
    def one(a, h):
        g = lambda j, i: grads[h, 3 * j + i, a]
        l, m = lam[h, a], mu[h, a]
        both = l * (g(0, 0) + g(1, 1) + g(2, 2))
        for i in range(3):
            stress[h, i, a] = stress_in[h, i, a] + (both + 2.0 * m * g(i, i))
        stress[h, 3, a] = stress_in[h, 3, a] + m * (g(2, 1) + g(1, 2))
        stress[h, 4, a] = stress_in[h, 4, a] + m * (g(2, 0) + g(0, 2))
        stress[h, 5, a] = stress_in[h, 5, a] + m * (g(1, 0) + g(0, 1))

    halves(5, one)


def plain_gradients(vel, grads):
    along = Along(D_PLAIN)

    def one(i, h):
        for a in range(5):
            ys = derive_rows([vel[h, i, a, b] for b in range(5)], D_PLAIN)
            for b in range(5):
                grads[h, 3 + i, a, b] = ys[b]
                grads[h, 6 + i, a, b] = along(vel[h, i, a, b])
        for b in range(5):
            xs = derive_rows([vel[h, i, a, b] for a in range(5)], D_PLAIN)
            for a in range(5):
                grads[h, i, a, b] = xs[a]

    halves(3, one)


def image(fg, ag, acc, adj_vel, dense, first):
    row = lax.broadcasted_iota(jnp.int32, (8, 128), 0)
    weight = Along.by_row(row, QUAD)

    def one(k, h):
        for a in range(5):
            for b in range(5):
                f = lambda j, i: fg[h, 3 * j + i, a, b]
                g = lambda j, i: ag[h, 3 * j + i, a, b]
                w = weight * float(QUAD[a] * QUAD[b])
                f0, f1, f2 = f(0, 0), f(1, 1), f(2, 2)
                g0, g1, g2 = g(0, 0), g(1, 1), g(2, 2)
                trace = (f0 + f1 + f2) * (g0 + g1 + g2) * w
                cross = None
                for i, j in ((0, 1), (0, 2), (1, 2)):
                    term = (f(j, i) + f(i, j)) * (g(j, i) + g(i, j))
                    cross = term if cross is None else cross + term
                strain = (2.0 * (f0 * g0 + f1 * g1 + f2 * g2) + cross) * w
                inertia = None
                for i in range(3):
                    term = acc[h, i, a, b] * adj_vel[h, i, a, b]
                    inertia = term if inertia is None else inertia + term
                for t, term in enumerate((trace, strain, inertia * w)):
                    at = t * 125 + a * 25 + b * 5
                    if first is None:
                        dense[h, at : at + 5, :] = term[0:5]
                    else:
                        dense[h, at : at + 5, :] = first[h, at : at + 5, :] + term[0:5]

    halves(1, one)


def fetch(src, dst, sem):
    copy = pltpu.make_async_copy(src, dst, sem)
    copy.start()
    return copy


def start_common(src, rinv, perms, acc, vel, stress, one, two, yj, zj, with_r):
    src = flat(src, 2250)
    load_fields(src, 0, vel, 3)
    load_fields(src, 3, stress, 6)
    local_acceleration(stress, rinv, acc, perms, yj, zj)

    def values(a, h):
        out = [stress[h, k, a] for k in (0, 5, 4)] + [vel[h, i, a] + time_step * acc[h, i, a] for i in range(3)]
        return out + ([0.05 * rinv[h, a]] if with_r else [])

    pack_faces(one, two, values)


def load_material(mat, k, dst):
    for g in range(25):
        for h in range(2):
            dst[h, g // 5, g % 5, 0:5, :] = mat[5 * g : 5 * g + 5, k, 128 * h : 128 * h + 128]


def forward_start_kernel(state_hbm, mat_hbm, nbr_hbm, one, two, acc, vel, stress, rinv, perms, yj, zj, state, mat, nbr, sems):
    first = fetch(nbr_hbm, nbr, sems.at[0])
    third = fetch(state_hbm, state, sems.at[2])
    second = fetch(mat_hbm, mat, sems.at[1])
    first.wait()
    make_perms(nbr, perms)
    second.wait()
    load_material(mat, 2, rinv)
    for h in range(2):
        for a in range(5):
            rinv[h, a] = 1.0 / rinv[h, a]
    zj[...] = jnp.zeros(zj.shape, f32)
    third.wait()
    start_common(state, rinv, perms, acc, vel, stress, one, two, yj, zj, True)


def adjoint_start_kernel(state, mat, rinv, perms, receivers, residuals, one, two, acc, vel, stress, lam, mu,
                         end_grads, injected, yj, zj):
    zj[...] = jnp.zeros(zj.shape, f32)
    injected[...] = receiver_rows(receivers, residuals)
    start_common(state, rinv, perms, acc, vel, stress, one, two, yj, zj, False)
    for k, dst in ((0, lam), (1, mu)):
        load_material(mat, k, dst)
        for h in range(2):
            for a in range(5):
                dst[h, a] = time_step * dst[h, a]
    plain_gradients(vel, end_grads)


def complete_step(rows, vel_in, stress_in, lam, mu, rinv, perms, vel, stress, acc, halo, grads, plain, yj, zj):
    finish_acceleration(acc, stress_in, rinv, halo, True)
    velocities(vel_in, vel, acc, rows)
    jump_gradients(vel, halo, grads, plain, perms, yj, zj)
    update_stress(stress_in, stress, grads, lam, mu)


def middle_common(rows, vel_in, stress_in, acc_in, lam, mu, rinv, perms, near, far, r_near, r_far,
                  one, two, vel, stress, acc, next_acc, plain, halo, grads, yj, zj, with_v):
    zj[...] = jnp.zeros(zj.shape, f32)
    load_halo(halo, *(flat(r, r.shape[0] * 2) for r in (near, far, r_near, r_far)), 6)
    acc[...] = acc_in[...]
    complete_step(rows, vel_in, stress_in, lam, mu, rinv, perms, vel, stress, acc, halo, grads, plain, yj, zj)
    local_acceleration(stress, rinv, next_acc, perms, yj, zj)

    def values(a, h):
        out = [stress[h, k, a] for k in (0, 5, 4)]
        if with_v:
            out += [vel[h, i, a] + time_step * next_acc[h, i, a] for i in range(3)]
        return out

    pack_faces(one, two, values)


def forward_middle_kernel(vel_in, stress_in, acc_in, lam, mu, rinv, perms, where_ref, strength, near, far,
                          one, two, vel, acc, next_acc, plain, stress, halo, grads, yj, zj):
    middle_common(source_rows(0, where_ref, strength), vel_in, stress_in, acc_in, lam, mu, rinv, perms, near, far, near, far,
                  one, two, vel, stress, acc, next_acc, plain, halo, grads, yj, zj, False)


def adjoint_middle_kernel(vel_in, stress_in, acc_in, lam, mu, rinv, perms, inject, near, far, r_near, r_far, f_plain, f_acc,
                          one, two, vel, stress, next_acc, dense, acc, plain, halo, grads, yj, zj):
    rows = [inject[i : i + 1] for i in range(3)]
    middle_common(rows, vel_in, stress_in, acc_in, lam, mu, rinv, perms, near, far, r_near, r_far,
                  one, two, vel, stress, acc, next_acc, plain, halo, grads, yj, zj, True)
    image(f_plain, plain, f_acc, vel, dense, None)


def last_kernel(vel_in, stress_in, acc_in, lam, mu, rinv, perms, inject, near, far, r_near, r_far,
                out, vel, stress, acc, halo, grads, yj, zj, rows_out, sems):
    zj[...] = jnp.zeros(zj.shape, f32)
    load_halo(halo, *(flat(r, r.shape[0] * 2) for r in (near, far, r_near, r_far)), 6)
    acc[...] = acc_in[...]
    rows = [inject[8 + i : 9 + i] for i in range(3)]
    finish_acceleration(acc, stress_in, rinv, halo, True)
    velocities(vel_in, vel, acc, rows)
    dst = flat(rows_out, 2250)

    def leave(first, k, field):
        for g in range(25):
            for h in range(2):
                dst[pl.ds(250 * (first + k) + 10 * g + h, 5, 2), :] = field[h, k, g // 5, g % 5, 0:5, :]
        there = pl.ds(125 * (first + k), 125)
        return pltpu.make_async_copy(rows_out.at[there], out.at[there], sems.at[first + k])

    def leave_all(first, count, field):
        def one(k, carry):
            leave(first, k, field).start()
            return carry

        lax.fori_loop(0, count, one, 0)

    leave_all(0, 3, vel)
    jump_gradients(vel, halo, grads, None, perms, yj, zj)
    update_stress(stress_in, stress, grads, lam, mu)
    leave_all(3, 6, stress)
    for k in range(9):
        there = pl.ds(125 * k, 125)
        pltpu.make_async_copy(rows_out.at[there], out.at[there], sems.at[k]).wait()


def last_image_kernel(f_vel, acc_in, adj_vel, end_grads, first, rinv, where_ref, strength, near, far,
                      keep, send, halo, vel, acc, fg, dense):
    load_halo(halo, flat(near, 150), flat(far, 150), None, None, 3)
    acc[...] = acc_in[...]
    finish_acceleration(acc, None, rinv, halo, False)
    velocities(f_vel, vel, acc, source_rows(1, where_ref, strength))
    plain_gradients(vel, fg)
    for h in range(2):
        dense[h, 368:384, :] = jnp.zeros((16, 128), f32)
    image(fg, end_grads, acc, adj_vel, dense, first)
    core = lax.rem(lax.axis_index("shot"), 2)
    turned = [dense[h].T for h in range(2)]
    for parity, (mine, other) in ((0, (keep, send)), (1, (send, keep))):

        @pl.when(core == parity)
        def _():
            for s in range(16):
                piece = turned[s // 8][16 * (s % 8) : 16 * (s % 8) + 16]
                (mine if s % 2 == 0 else other)[s // 2] = piece


V = pl.BlockSpec(memory_space=pltpu.VMEM)
S = pl.BlockSpec(memory_space=pltpu.SMEM)


def shape(*dims):
    return jax.ShapeDtypeStruct(dims, f32)


def field(count):
    return shape(2, count, 5, 5, 8, 128)


ONE = shape(2, 5, 5, 8, 128)
PERMS = jax.ShapeDtypeStruct((4, N, N), bf16)


def sends(faces):
    return shape(faces * 25, 2, 128)


def scr(s):
    return pltpu.VMEM(s.shape, s.dtype)


JUMPS = [pltpu.VMEM((2, 2, 3, 5, 8, 128), f32), pltpu.VMEM((2, 3, 5, 5, 8, 128), f32)]
HALO = pltpu.VMEM((2, 2, 7, 5, 8, 128), f32)


def call(kernel, specs, outs, scratch, flops, moved, where=V):
    return pl.pallas_call(
        kernel,
        out_shape=outs,
        in_specs=specs,
        out_specs=jax.tree.map(lambda _: where, outs),
        scratch_shapes=scratch,
        compiler_params=pltpu.CompilerParams(vmem_limit_bytes=8 * 2**20),
        cost_estimate=pl.CostEstimate(flops=flops, bytes_accessed=moved, transcendentals=0),
    )


def both_ways(first, second):
    count = lax.axis_size("slab")
    near = [(i, i ^ 1) for i in range(count)]
    far = [(i, (i + (1 if i % 2 else -1)) % count) for i in range(count)]
    return lax.ppermute(first, "slab", near), lax.ppermute(second, "slab", far)


def core_sum_kernel(keep, got, mine, *others):
    line = lax.div(lax.axis_index("shot"), 4)
    for d, dst in enumerate((mine, *others)):
        to = lax.rem(line + d, 4)
        for high in range(2):
            dst[high] = keep[2 * to + high] + got[2 * to + high]


def line_sum_kernel(mine, one, two, three, keep, send):
    high = lax.rem(lax.div(lax.axis_index("shot"), 2), 2)
    for dst, k in ((keep, high), (send, 1 - high)):
        dst[...] = (mine[k] + one[k]) + (two[k] + three[k])


def last_sum_kernel(keep, got, out, rows):
    turned = (keep[...] + got[...]).T
    for t in range(3):
        rows[pl.ds(t, 125, 4), 0:16] = turned[125 * t : 125 * t + 125]
    out[...] = rows.reshape(125, 4, 128)[:, 0:3, 0:16]


def reduce_over_shots(keep, send):
    hop = lambda v, to: lax.ppermute(v, "shot", [(i, to(i)) for i in range(16)])
    pair, chunk = shape(2, 16, 384), shape(16, 384)
    mine, *others = call(core_sum_kernel, [V] * 2, (pair,) * 4, [], 1000, 1000)(keep, hop(send, lambda i: i ^ 1))
    got = [hop(x, lambda i: (i + 4 * d) % 16) for d, x in enumerate(others, 1)]
    keep, send = call(line_sum_kernel, [V] * 4, (chunk,) * 2, [], 1000, 1000)(mine, *got)
    return call(last_sum_kernel, [V] * 2, shape(125, 3, 16), [scr(shape(500, 128))], 1000, 1000)(keep, hop(send, lambda i: i ^ 2))


def body(fwd, adj, materials, nbr, source_element, pulse, receivers, residuals):
    receivers = receivers.reshape(1, N)
    fwd, adj = (x.reshape(1125, 2, 128) for x in (fwd, adj))
    mat = materials.transpose(1, 2, 3, 0, 4).reshape(125, 3, N)
    nbr = nbr.T
    residuals = residuals.transpose(0, 2, 1, 3).reshape(3, 2, N)

    f_one, f_two, f_acc, f_vel, f_stress, rinv, perms = call(
        forward_start_kernel,
        [pl.BlockSpec(memory_space=pltpu.HBM)] * 3,
        (sends(7), sends(7), field(3), field(3), field(6), ONE, PERMS),
        JUMPS + [scr(shape(1125, 2, 128)), scr(shape(125, 3, N)), pltpu.VMEM((4, N), jnp.int32), pltpu.SemaphoreType.DMA((3,))],
        10**8, 4 * 10**6,
    )(*(pltpu.with_memory_space_constraint(x, pltpu.HBM) for x in (fwd, mat, nbr)))
    f_near, f_far = both_ways(f_one, f_two)
    a_one, a_two, a_acc, a_vel, a_stress, lam, mu, end_grads, injected = call(
        adjoint_start_kernel,
        [V] * 6,
        (sends(6), sends(6), field(3), field(3), field(6), ONE, ONE, field(9), shape(16, N)),
        JUMPS,
        10**8, 4 * 10**6,
    )(adj, mat, rinv, perms, receivers, residuals)
    a_near, a_far = both_ways(a_one, a_two)
    adj_vel_end = a_vel

    f_one, f_two, f_vel1, f_acc1, f_acc2, f_plain = call(
        forward_middle_kernel,
        [V] * 7 + [S] * 2 + [V] * 2,
        (sends(3), sends(3), field(3), field(3), field(3), field(9)),
        [scr(field(6)), HALO, scr(field(9))] + JUMPS,
        2 * 10**8, 8 * 10**6,
    )(f_vel, f_stress, f_acc, lam, mu, rinv, perms, source_element, pulse, f_near, f_far)
    f_near2, f_far2 = both_ways(f_one, f_two)
    a_one, a_two, a_vel1, a_stress1, a_acc2, first = call(
        adjoint_middle_kernel,
        [V] * 14,
        (sends(6), sends(6), field(3), field(6), field(3), shape(2, 384, 128)),
        [scr(field(3)), scr(field(9)), HALO, scr(field(9))] + JUMPS,
        2 * 10**8, 8 * 10**6,
    )(a_vel, a_stress, a_acc, lam, mu, rinv, perms, injected, a_near, a_far, f_near, f_far, f_plain, f_acc1)
    a_near2, a_far2 = both_ways(a_one, a_two)
    keep, send = call(
        last_image_kernel,
        [V] * 6 + [S] * 2 + [V] * 2,
        (shape(8, 16, 384), shape(8, 16, 384)),
        [HALO, scr(field(3)), scr(field(3)), scr(field(9)), scr(shape(2, 384, 128))],
        1000, 1000,
    )(f_vel1, f_acc2, adj_vel_end, end_grads, first, rinv, source_element, pulse, f_near2, f_far2)
    gradient = reduce_over_shots(keep, send)
    adjoint_end = call(
        last_kernel,
        [V] * 12,
        shape(1125, 2, 128),
        [scr(field(3)), scr(field(6)), scr(field(3)), HALO, scr(field(9))] + JUMPS
        + [scr(shape(1125, 2, 128)), pltpu.SemaphoreType.DMA((9,))],
        10**8, 8 * 10**6,
        pl.BlockSpec(memory_space=pltpu.HBM),
    )(a_vel1, a_stress1, a_acc2, lam, mu, rinv, perms, injected, a_near2, a_far2, f_near, f_far)
    return gradient.reshape(5, 5, 5, 3, 16).transpose(3, 0, 1, 2, 4), adjoint_end.reshape(1, 9, 5, 5, 5, N)


def solution(mesh):
    return jax.shard_map(
        body,
        mesh=mesh,
        in_specs=(
            P("shot", None, None, None, None, "slab"),
            P("shot", None, None, None, None, "slab"),
            P(None, None, None, None, "slab"),
            P(),
            P("shot"),
            P("shot", None, None),
            P(),
            P("shot", None, None, None),
        ),
        out_specs=(
            P(None, None, None, None, ("slab", "shot")),
            P("shot", None, None, None, None, "slab"),
        ),
        check_vma=False,
    )
```

```python
import math

import jax
import jax.numpy as jnp
import numpy as np
from jax import lax
from jax.experimental import pallas as pl
from jax.experimental.pallas import tpu as pltpu
from jax.sharding import PartitionSpec as P

f32 = jnp.float32
bf16 = jnp.bfloat16

time_step = 0.01
N = 256


def tables():
    root = math.sqrt(3.0 / 7.0)
    points = np.array([-1.0, -root, 0.0, root, 1.0])
    legendre = (35.0 * points**4 - 30.0 * points**2 + 3.0) / 8.0
    matrix = np.zeros((5, 5))
    for r in range(5):
        for c in range(5):
            if r != c:
                matrix[r, c] = legendre[r] / (legendre[c] * (points[r] - points[c]))
    matrix[0, 0] = -5.0
    matrix[4, 4] = 5.0
    quad = np.array([0.1, 49.0 / 90.0, 32.0 / 45.0, 49.0 / 90.0, 0.1])
    return matrix, quad


D_PLAIN, QUAD = tables()
D_LIFT = D_PLAIN.copy()
D_LIFT[0, 0] += 5.0
D_LIFT[4, 4] -= 5.0


def split(x):
    high = x.astype(bf16)
    return high, (x - high.astype(f32)).astype(bf16)


def dot(a, b):
    return lax.dot_general(a, b, (((1,), (0,)), ((), ())), preferred_element_type=f32)


def derive_rows(rows, matrix):
    even0, odd0 = rows[0] + rows[4], rows[0] - rows[4]
    even1, odd1 = rows[1] + rows[3], rows[1] - rows[3]
    out = [None] * 5
    for r in (0, 1):
        m = [float(v) for v in matrix[r]]
        p = 0.5 * (m[0] + m[4]) * even0 + 0.5 * (m[1] + m[3]) * even1 + m[2] * rows[2]
        q = 0.5 * (m[0] - m[4]) * odd0 + 0.5 * (m[1] - m[3]) * odd1
        out[r] = q + p
        out[4 - r] = q - p
    out[2] = float(matrix[2, 0]) * odd0 + float(matrix[2, 1]) * odd1
    return out


class Along:
    def __init__(self, matrix):
        row = lax.broadcasted_iota(jnp.int32, (8, 128), 0)
        self.places = [jnp.where(row < 5, lax.rem(row + m, 5), row) for m in range(1, 5)]
        self.factors = []
        for m in range(1, 5):
            self.factors.append(self.by_row(row, [matrix[c, (c + m) % 5] for c in range(5)]))
        own = [matrix[c, c] for c in range(5)]
        self.own = self.by_row(row, own) if any(own) else None

    @staticmethod
    def by_row(row, values):
        out = jnp.zeros((8, 128), f32)
        for c in range(5):
            out = jnp.where(row == c, float(values[c]), out)
        return out

    def __call__(self, tile):
        total = None if self.own is None else tile * self.own
        for place, factor in zip(self.places, self.factors):
            term = jnp.take_along_axis(tile, place, axis=0) * factor
            total = term if total is None else total + term
        return total


def flat(ref, rows):
    return ref.reshape(rows, 128)


def make_perms(nbr, perms):
    source = lax.broadcasted_iota(jnp.int32, (N, N), 0)
    for k in range(4):
        hit = source == nbr[k : k + 1, :]
        perms[k] = jnp.where(hit, -5.0 if k % 2 == 0 else 5.0, 0.0).astype(bf16)


def permuted(face, matrix):
    rows = face.shape[0]
    both = dot(jnp.concatenate(split(face), axis=0), matrix)
    return both[:rows] + both[rows:]


def jumps(field, ys, first_z, perms, yj, zj):
    count = field.shape[1]
    for side, b in ((0, 4), (1, 0)):
        face = jnp.concatenate(
            [
                jnp.concatenate([field[h, k, :, b].reshape(40, 128) for h in range(2)], axis=1)
                for k in ys
            ],
            axis=0,
        )
        got = permuted(face, perms[side])
        for h in range(2):
            for i in range(3):
                part = got[40 * i : 40 * i + 40, 128 * h : 128 * h + 128]
                yj[side, h, i] = part.reshape(5, 8, 128)
    rows = flat(field, 2 * count * 200)
    into = flat(zj, 1200)
    spare = jnp.zeros((5, N), f32)
    for side, c in ((0, 4), (1, 0)):
        face = jnp.concatenate(
            [rows[pl.ds((h * count + first_z) * 200 + c, 75, 8), :] for h in range(2)], axis=1
        )
        got = permuted(jnp.concatenate([face, spare], axis=0), perms[2 + side])
        for h in range(2):
            into[pl.ds(h * 600 + (0, 4)[side], 75, 8), :] = got[:75, 128 * h : 128 * h + 128]


def stress_of(i, d):
    if isinstance(i, int):
        return i if i == d else 6 - i - d
    return jnp.where(i == d, i, 6 - i - d)


def halves(count, one, unrolled=False):
    if unrolled:
        for k in range(count):
            for h in range(2):
                one(k, h)
        return

    def step(t, carry):
        one(lax.div(t, 2), lax.rem(t, 2))
        return carry

    lax.fori_loop(0, 2 * count, step, 0)


def local_acceleration(stress, rinv, acc, perms, yj, zj):
    along = Along(D_LIFT)
    jumps(stress, (5, 1, 3), 2, perms, yj, zj)

    def one(i, h):
        kx, ky, kz = stress_of(i, 0), stress_of(i, 1), stress_of(i, 2)
        for a in range(5):
            ys = derive_rows([stress[h, ky, a, b] for b in range(5)], D_LIFT)
            ys[0] = ys[0] + yj[0, h, i, a]
            ys[4] = ys[4] + yj[1, h, i, a]
            for b in range(5):
                acc[h, i, a, b] = ys[b] + (along(stress[h, kz, a, b]) + zj[h, 2 - i, a, b])
        for b in range(5):
            xs = derive_rows([stress[h, kx, a, b] for a in range(5)], D_LIFT)
            for a in range(5):
                acc[h, i, a, b] = (acc[h, i, a, b] + xs[a]) * rinv[h, a, b]

    halves(3, one, True)


def load_fields(src, first, dst, count):
    def one(k, carry):
        for g in range(25):
            for h in range(2):
                dst[h, k, g // 5, g % 5, 0:5, :] = src[pl.ds(250 * (first + k) + 10 * g + h, 5, 2), :]
        return carry

    lax.fori_loop(0, count, one, 0)


def pack_face(dst, k, value, h):
    for b in range(5):
        dst[pl.ds(50 * k + 10 * b + h, 5, 2), :] = value[b, 0:5]


def unpack_face(dst, side, k, src, j):
    for h in range(2):
        for b in range(5):
            dst[side, h, k, b, 0:5, :] = src[pl.ds(50 * j + 10 * b + h, 5, 2), :]


def load_halo(halo, first, second, r_first, r_second, count):
    odd = lax.rem(lax.axis_index("slab"), 2)
    for side, src in ((1 - odd, first), (odd, second)):
        for k in range(count):
            unpack_face(halo, side, k, src, k)
    if r_first is not None:
        for side, src in ((1 - odd, r_first), (odd, r_second)):
            unpack_face(halo, side, 6, src, 6)


def pack_faces(first, second, values):
    odd = lax.rem(lax.axis_index("slab"), 2)
    for dst, a in ((first, 4 * (1 - odd)), (second, 4 * odd)):
        dst = flat(dst, dst.shape[0] * 2)
        for h in range(2):
            for k, value in enumerate(values(a, h)):
                pack_face(dst, k, value, h)


def finish_acceleration(acc, stress, rinv, halo, has_v):
    for h in range(2):
        for i in range(3):
            k = (0, 5, 4)[i]
            acc[h, i, 0] = acc[h, i, 0] - 5.0 * rinv[h, 0] * halo[0, h, i]
            acc[h, i, 4] = acc[h, i, 4] + 5.0 * rinv[h, 4] * halo[1, h, i]
            if has_v:
                halo[0, h, 3 + i] = halo[0, h, 3 + i] + halo[0, h, 6] * stress[h, k, 0]
                halo[1, h, 3 + i] = halo[1, h, 3 + i] - halo[1, h, 6] * stress[h, k, 4]


def source_rows(step, where_ref, pulse):
    lane = lax.broadcasted_iota(jnp.int32, (1, N), 1) + slab_base()
    hit = lane == where_ref[0]
    return [jnp.where(hit, pulse[0, step, i], 0.0) for i in range(3)]


def receiver_rows(where_ref, residual):
    element = lax.broadcasted_iota(jnp.int32, (N, N), 0) + slab_base()
    hits = jnp.where(element == where_ref[...], 1.0, 0.0).astype(bf16)
    spare = jnp.zeros((5, N), f32)
    x = jnp.concatenate([r for step in range(2) for r in [residual[i, step : step + 1] for i in range(3)] + [spare]], axis=0)
    total = None
    for part in range(3):
        high = x.astype(bf16)
        x = x - high.astype(f32)
        term = lax.dot_general(high, hits, (((1,), (1,)), ((), ())), preferred_element_type=f32)
        total = term if total is None else total + term
    return total


def slab_base():
    return lax.axis_index("slab") * N


def velocities(vel_in, vel, acc, rows):
    def one(i, h):
        for a in range(5):
            vel[h, i, a] = vel_in[h, i, a] + time_step * acc[h, i, a]

    halves(3, one, True)
    mask = lax.broadcasted_iota(jnp.int32, (8, 128), 0) == 2
    for i in range(3):
        for h in range(2):
            vel[h, i, 2, 2] += jnp.where(mask, rows[i][:, 128 * h : 128 * h + 128], 0.0)


def jump_gradients(vel, halo, grads, plain, perms, yj, zj):
    along = Along(D_LIFT)
    jumps(vel, (0, 1, 2), 0, perms, yj, zj)
    own = Along.by_row(lax.broadcasted_iota(jnp.int32, (8, 128), 0), [-5.0, 0.0, 0.0, 0.0, 5.0])

    def one(i, h):
        for a in range(5):
            v = [vel[h, i, a, b] for b in range(5)]
            ys = derive_rows(v, D_LIFT)
            zs = [along(v[b]) for b in range(5)]
            if plain is not None:
                for b in range(5):
                    plain[h, 3 + i, a, b] = ys[b] + {0: -5.0, 4: 5.0}[b] * v[b] if b in (0, 4) else ys[b]
                    plain[h, 6 + i, a, b] = zs[b] + own * v[b]
            ys[0] = ys[0] + yj[0, h, i, a]
            ys[4] = ys[4] + yj[1, h, i, a]
            for b in range(5):
                grads[h, 3 + i, a, b] = ys[b]
                grads[h, 6 + i, a, b] = zs[b] + zj[h, i, a, b]
        for b in range(5):
            v = [vel[h, i, a, b] for a in range(5)]
            xs = derive_rows(v, D_LIFT)
            if plain is not None:
                for a in range(5):
                    plain[h, i, a, b] = xs[a] + {0: -5.0, 4: 5.0}[a] * v[a] if a in (0, 4) else xs[a]
            xs[0] = xs[0] - 5.0 * halo[0, h, 3 + i, b]
            xs[4] = xs[4] + 5.0 * halo[1, h, 3 + i, b]
            for a in range(5):
                grads[h, i, a, b] = xs[a]

    halves(3, one, True)


def update_stress(stress_in, stress, grads, lam, mu):
    def one(a, h):
        g = lambda j, i: grads[h, 3 * j + i, a]
        l, m = lam[h, a], mu[h, a]
        both = l * (g(0, 0) + g(1, 1) + g(2, 2))
        for i in range(3):
            stress[h, i, a] = stress_in[h, i, a] + (both + 2.0 * m * g(i, i))
        stress[h, 3, a] = stress_in[h, 3, a] + m * (g(2, 1) + g(1, 2))
        stress[h, 4, a] = stress_in[h, 4, a] + m * (g(2, 0) + g(0, 2))
        stress[h, 5, a] = stress_in[h, 5, a] + m * (g(1, 0) + g(0, 1))

    halves(5, one, True)


def plain_gradients(vel, grads):
    along = Along(D_PLAIN)

    def one(i, h):
        for a in range(5):
            ys = derive_rows([vel[h, i, a, b] for b in range(5)], D_PLAIN)
            for b in range(5):
                grads[h, 3 + i, a, b] = ys[b]
                grads[h, 6 + i, a, b] = along(vel[h, i, a, b])
        for b in range(5):
            xs = derive_rows([vel[h, i, a, b] for a in range(5)], D_PLAIN)
            for a in range(5):
                grads[h, i, a, b] = xs[a]

    halves(3, one, True)


def image(fg, ag, acc, adj_vel, dense, first):
    row = lax.broadcasted_iota(jnp.int32, (8, 128), 0)
    weight = Along.by_row(row, QUAD)

    def one(k, h):
        for a in range(5):
            for b in range(5):
                f = lambda j, i: fg[h, 3 * j + i, a, b]
                g = lambda j, i: ag[h, 3 * j + i, a, b]
                w = weight * float(QUAD[a] * QUAD[b])
                f0, f1, f2 = f(0, 0), f(1, 1), f(2, 2)
                g0, g1, g2 = g(0, 0), g(1, 1), g(2, 2)
                trace = (f0 + f1 + f2) * (g0 + g1 + g2) * w
                cross = None
                for i, j in ((0, 1), (0, 2), (1, 2)):
                    term = (f(j, i) + f(i, j)) * (g(j, i) + g(i, j))
                    cross = term if cross is None else cross + term
                strain = (2.0 * (f0 * g0 + f1 * g1 + f2 * g2) + cross) * w
                inertia = None
                for i in range(3):
                    term = acc[h, i, a, b] * adj_vel[h, i, a, b]
                    inertia = term if inertia is None else inertia + term
                for t, term in enumerate((trace, strain, inertia * w)):
                    at = t * 125 + a * 25 + b * 5
                    if first is None:
                        dense[h, at : at + 5, :] = term[0:5]
                    else:
                        dense[h, at : at + 5, :] = first[h, at : at + 5, :] + term[0:5]

    halves(1, one)


def fetch(src, dst, sem):
    copy = pltpu.make_async_copy(src, dst, sem)
    copy.start()
    return copy


def start_common(src, rinv, perms, acc, vel, stress, one, two, yj, zj, with_r):
    src = flat(src, 2250)
    load_fields(src, 0, vel, 3)
    load_fields(src, 3, stress, 6)
    local_acceleration(stress, rinv, acc, perms, yj, zj)

    def values(a, h):
        out = [stress[h, k, a] for k in (0, 5, 4)] + [vel[h, i, a] + time_step * acc[h, i, a] for i in range(3)]
        return out + ([0.05 * rinv[h, a]] if with_r else [])

    pack_faces(one, two, values)


def load_material(mat, k, dst):
    for g in range(25):
        for h in range(2):
            dst[h, g // 5, g % 5, 0:5, :] = mat[5 * g : 5 * g + 5, k, 128 * h : 128 * h + 128]


def forward_start_kernel(state_hbm, mat_hbm, nbr_hbm, one, two, acc, vel, stress, rinv, perms, yj, zj, state, mat, nbr, sems):
    first = fetch(nbr_hbm, nbr, sems.at[0])
    third = fetch(state_hbm, state, sems.at[2])
    second = fetch(mat_hbm, mat, sems.at[1])
    first.wait()
    make_perms(nbr, perms)
    second.wait()
    load_material(mat, 2, rinv)
    for h in range(2):
        for a in range(5):
            rinv[h, a] = 1.0 / rinv[h, a]
    zj[...] = jnp.zeros(zj.shape, f32)
    third.wait()
    start_common(state, rinv, perms, acc, vel, stress, one, two, yj, zj, True)


def adjoint_start_kernel(state, mat, rinv, perms, receivers, residuals, one, two, acc, vel, stress, lam, mu,
                         end_grads, injected, yj, zj):
    zj[...] = jnp.zeros(zj.shape, f32)
    injected[...] = receiver_rows(receivers, residuals)
    start_common(state, rinv, perms, acc, vel, stress, one, two, yj, zj, False)
    for k, dst in ((0, lam), (1, mu)):
        load_material(mat, k, dst)
        for h in range(2):
            for a in range(5):
                dst[h, a] = time_step * dst[h, a]
    plain_gradients(vel, end_grads)


def complete_step(rows, vel_in, stress_in, lam, mu, rinv, perms, vel, stress, acc, halo, grads, plain, yj, zj):
    finish_acceleration(acc, stress_in, rinv, halo, True)
    velocities(vel_in, vel, acc, rows)
    jump_gradients(vel, halo, grads, plain, perms, yj, zj)
    update_stress(stress_in, stress, grads, lam, mu)


def middle_common(rows, vel_in, stress_in, acc_in, lam, mu, rinv, perms, near, far, r_near, r_far,
                  one, two, vel, stress, acc, next_acc, plain, halo, grads, yj, zj):
    zj[...] = jnp.zeros(zj.shape, f32)
    load_halo(halo, *(flat(r, r.shape[0] * 2) for r in (near, far, r_near, r_far)), 6)
    acc[...] = acc_in[...]
    complete_step(rows, vel_in, stress_in, lam, mu, rinv, perms, vel, stress, acc, halo, grads, plain, yj, zj)
    if next_acc is not None:
        local_acceleration(stress, rinv, next_acc, perms, yj, zj)

    def values(a, h):
        out = [stress[h, k, a] for k in (0, 5, 4)]
        if next_acc is not None:
            out += [vel[h, i, a] + time_step * next_acc[h, i, a] for i in range(3)]
        return out

    pack_faces(one, two, values)


def forward_middle_kernel(vel_in, stress_in, acc_in, lam, mu, rinv, perms, where_ref, strength, near, far,
                          one, two, vel, acc, plain, stress, halo, grads, yj, zj):
    middle_common(source_rows(0, where_ref, strength), vel_in, stress_in, acc_in, lam, mu, rinv, perms, near, far, near, far,
                  one, two, vel, stress, acc, None, plain, halo, grads, yj, zj)


def adjoint_middle_kernel(vel_in, stress_in, acc_in, lam, mu, rinv, perms, inject, near, far, r_near, r_far, f_plain, f_acc, f_stress,
                          one, two, vel, stress, next_acc, dense, f_next_acc, acc, plain, halo, grads, yj, zj):
    rows = [inject[i : i + 1] for i in range(3)]
    middle_common(rows, vel_in, stress_in, acc_in, lam, mu, rinv, perms, near, far, r_near, r_far,
                  one, two, vel, stress, acc, next_acc, plain, halo, grads, yj, zj)
    image(f_plain, plain, f_acc, vel, dense, None)
    local_acceleration(f_stress, rinv, f_next_acc, perms, yj, zj)


def last_kernel(vel_in, stress_in, acc_in, lam, mu, rinv, perms, inject, near, far, r_near, r_far,
                out, vel, stress, acc, halo, grads, yj, zj, rows_out, sems):
    zj[...] = jnp.zeros(zj.shape, f32)
    load_halo(halo, *(flat(r, r.shape[0] * 2) for r in (near, far, r_near, r_far)), 6)
    acc[...] = acc_in[...]
    rows = [inject[8 + i : 9 + i] for i in range(3)]
    finish_acceleration(acc, stress_in, rinv, halo, True)
    velocities(vel_in, vel, acc, rows)
    dst = flat(rows_out, 2250)

    def leave(first, k, field):
        for g in range(25):
            for h in range(2):
                dst[pl.ds(250 * (first + k) + 10 * g + h, 5, 2), :] = field[h, k, g // 5, g % 5, 0:5, :]
        there = pl.ds(125 * (first + k), 125)
        return pltpu.make_async_copy(rows_out.at[there], out.at[there], sems.at[first + k])

    def leave_all(first, count, field):
        def one(k, carry):
            leave(first, k, field).start()
            return carry

        lax.fori_loop(0, count, one, 0)

    leave_all(0, 3, vel)
    jump_gradients(vel, halo, grads, None, perms, yj, zj)
    update_stress(stress_in, stress, grads, lam, mu)
    leave_all(3, 6, stress)
    for k in range(9):
        there = pl.ds(125 * k, 125)
        pltpu.make_async_copy(rows_out.at[there], out.at[there], sems.at[k]).wait()


def last_image_kernel(f_vel, acc_in, adj_vel, end_grads, first, rinv, where_ref, strength, near, far,
                      keep, send, halo, vel, acc, fg, dense):
    load_halo(halo, flat(near, 150), flat(far, 150), None, None, 3)
    acc[...] = acc_in[...]
    finish_acceleration(acc, None, rinv, halo, False)
    velocities(f_vel, vel, acc, source_rows(1, where_ref, strength))
    plain_gradients(vel, fg)
    for h in range(2):
        dense[h, 368:384, :] = jnp.zeros((16, 128), f32)
    image(fg, end_grads, acc, adj_vel, dense, first)
    core = lax.rem(lax.axis_index("shot"), 2)
    turned = [dense[h].T for h in range(2)]
    for parity, (mine, other) in ((0, (keep, send)), (1, (send, keep))):

        @pl.when(core == parity)
        def _():
            for s in range(16):
                piece = turned[s // 8][16 * (s % 8) : 16 * (s % 8) + 16]
                (mine if s % 2 == 0 else other)[s // 2] = piece


V = pl.BlockSpec(memory_space=pltpu.VMEM)
S = pl.BlockSpec(memory_space=pltpu.SMEM)


def shape(*dims):
    return jax.ShapeDtypeStruct(dims, f32)


def field(count):
    return shape(2, count, 5, 5, 8, 128)


ONE = shape(2, 5, 5, 8, 128)
PERMS = jax.ShapeDtypeStruct((4, N, N), bf16)


def sends(faces):
    return shape(faces * 25, 2, 128)


def scr(s):
    return pltpu.VMEM(s.shape, s.dtype)


JUMPS = [pltpu.VMEM((2, 2, 3, 5, 8, 128), f32), pltpu.VMEM((2, 3, 5, 5, 8, 128), f32)]
HALO = pltpu.VMEM((2, 2, 7, 5, 8, 128), f32)


def call(kernel, specs, outs, scratch, flops, moved, where=V):
    return pl.pallas_call(
        kernel,
        out_shape=outs,
        in_specs=specs,
        out_specs=jax.tree.map(lambda _: where, outs),
        scratch_shapes=scratch,
        compiler_params=pltpu.CompilerParams(vmem_limit_bytes=8 * 2**20),
        cost_estimate=pl.CostEstimate(flops=flops, bytes_accessed=moved, transcendentals=0),
    )


def both_ways(first, second):
    count = lax.axis_size("slab")
    near = [(i, i ^ 1) for i in range(count)]
    far = [(i, (i + (1 if i % 2 else -1)) % count) for i in range(count)]
    return lax.ppermute(first, "slab", near), lax.ppermute(second, "slab", far)


def core_sum_kernel(keep, got, mine, *others):
    line = lax.div(lax.axis_index("shot"), 4)
    for d, dst in enumerate((mine, *others)):
        to = lax.rem(line + d, 4)
        for high in range(2):
            dst[high] = keep[2 * to + high] + got[2 * to + high]


def line_sum_kernel(mine, one, two, three, keep, send):
    high = lax.rem(lax.div(lax.axis_index("shot"), 2), 2)
    for dst, k in ((keep, high), (send, 1 - high)):
        dst[...] = (mine[k] + one[k]) + (two[k] + three[k])


def last_sum_kernel(keep, got, out, rows):
    turned = (keep[...] + got[...]).T
    for t in range(3):
        rows[pl.ds(t, 125, 4), 0:16] = turned[125 * t : 125 * t + 125]
    out[...] = rows.reshape(125, 4, 128)[:, 0:3, 0:16]


def reduce_over_shots(keep, send):
    hop = lambda v, to: lax.ppermute(v, "shot", [(i, to(i)) for i in range(16)])
    pair, chunk = shape(2, 16, 384), shape(16, 384)
    mine, *others = call(core_sum_kernel, [V] * 2, (pair,) * 4, [], 1000, 1000)(keep, hop(send, lambda i: i ^ 1))
    got = [hop(x, lambda i: (i + 4 * d) % 16) for d, x in enumerate(others, 1)]
    keep, send = call(line_sum_kernel, [V] * 4, (chunk,) * 2, [], 1000, 1000)(mine, *got)
    return call(last_sum_kernel, [V] * 2, shape(125, 3, 16), [scr(shape(500, 128))], 1000, 1000)(keep, hop(send, lambda i: i ^ 2))


def body(fwd, adj, materials, nbr, source_element, pulse, receivers, residuals):
    receivers = receivers.reshape(1, N)
    fwd, adj = (x.reshape(1125, 2, 128) for x in (fwd, adj))
    mat = materials.transpose(1, 2, 3, 0, 4).reshape(125, 3, N)
    nbr = nbr.T
    residuals = residuals.transpose(0, 2, 1, 3).reshape(3, 2, N)

    f_one, f_two, f_acc, f_vel, f_stress, rinv, perms = call(
        forward_start_kernel,
        [pl.BlockSpec(memory_space=pltpu.HBM)] * 3,
        (sends(7), sends(7), field(3), field(3), field(6), ONE, PERMS),
        JUMPS + [scr(shape(1125, 2, 128)), scr(shape(125, 3, N)), pltpu.VMEM((4, N), jnp.int32), pltpu.SemaphoreType.DMA((3,))],
        10**8, 4 * 10**6,
    )(*(pltpu.with_memory_space_constraint(x, pltpu.HBM) for x in (fwd, mat, nbr)))
    f_near, f_far = both_ways(f_one, f_two)
    a_one, a_two, a_acc, a_vel, a_stress, lam, mu, end_grads, injected = call(
        adjoint_start_kernel,
        [V] * 6,
        (sends(6), sends(6), field(3), field(3), field(6), ONE, ONE, field(9), shape(16, N)),
        JUMPS,
        10**8, 4 * 10**6,
    )(adj, mat, rinv, perms, receivers, residuals)
    a_near, a_far = both_ways(a_one, a_two)
    adj_vel_end = a_vel

    f_one, f_two, f_vel1, f_acc1, f_plain, f_stress1 = call(
        forward_middle_kernel,
        [V] * 7 + [S] * 2 + [V] * 2,
        (sends(3), sends(3), field(3), field(3), field(9), field(6)),
        [HALO, scr(field(9))] + JUMPS,
        2 * 10**8, 8 * 10**6,
    )(f_vel, f_stress, f_acc, lam, mu, rinv, perms, source_element, pulse, f_near, f_far)
    f_near2, f_far2 = both_ways(f_one, f_two)
    a_one, a_two, a_vel1, a_stress1, a_acc2, first, f_acc2 = call(
        adjoint_middle_kernel,
        [V] * 15,
        (sends(6), sends(6), field(3), field(6), field(3), shape(2, 384, 128), field(3)),
        [scr(field(3)), scr(field(9)), HALO, scr(field(9))] + JUMPS,
        2 * 10**8, 8 * 10**6,
    )(a_vel, a_stress, a_acc, lam, mu, rinv, perms, injected, a_near, a_far, f_near, f_far, f_plain, f_acc1, f_stress1)
    a_near2, a_far2 = both_ways(a_one, a_two)
    keep, send = call(
        last_image_kernel,
        [V] * 6 + [S] * 2 + [V] * 2,
        (shape(8, 16, 384), shape(8, 16, 384)),
        [HALO, scr(field(3)), scr(field(3)), scr(field(9)), scr(shape(2, 384, 128))],
        1000, 1000,
    )(f_vel1, f_acc2, adj_vel_end, end_grads, first, rinv, source_element, pulse, f_near2, f_far2)
    gradient = reduce_over_shots(keep, send)
    adjoint_end = call(
        last_kernel,
        [V] * 12,
        shape(1125, 2, 128),
        [scr(field(3)), scr(field(6)), scr(field(3)), HALO, scr(field(9))] + JUMPS
        + [scr(shape(1125, 2, 128)), pltpu.SemaphoreType.DMA((9,))],
        10**8, 8 * 10**6,
        pl.BlockSpec(memory_space=pltpu.HBM),
    )(a_vel1, a_stress1, a_acc2, lam, mu, rinv, perms, injected, a_near2, a_far2, f_near, f_far)
    return gradient.reshape(5, 5, 5, 3, 16).transpose(3, 0, 1, 2, 4), adjoint_end.reshape(1, 9, 5, 5, 5, N)


def solution(mesh):
    return jax.shard_map(
        body,
        mesh=mesh,
        in_specs=(
            P("shot", None, None, None, None, "slab"),
            P("shot", None, None, None, None, "slab"),
            P(None, None, None, None, "slab"),
            P(),
            P("shot"),
            P("shot", None, None),
            P(),
            P("shot", None, None, None),
        ),
        out_specs=(
            P(None, None, None, None, ("slab", "shot")),
            P("shot", None, None, None, None, "slab"),
        ),
        check_vma=False,
    )
```

```python
import math

import jax
import jax.numpy as jnp
import numpy as np
from jax import lax
from jax.experimental import pallas as pl
from jax.experimental.pallas import tpu as pltpu
from jax.sharding import PartitionSpec as P

f32 = jnp.float32
bf16 = jnp.bfloat16

time_step = 0.01
N = 256


def tables():
    root = math.sqrt(3.0 / 7.0)
    points = np.array([-1.0, -root, 0.0, root, 1.0])
    legendre = (35.0 * points**4 - 30.0 * points**2 + 3.0) / 8.0
    matrix = np.zeros((5, 5))
    for r in range(5):
        for c in range(5):
            if r != c:
                matrix[r, c] = legendre[r] / (legendre[c] * (points[r] - points[c]))
    matrix[0, 0] = -5.0
    matrix[4, 4] = 5.0
    quad = np.array([0.1, 49.0 / 90.0, 32.0 / 45.0, 49.0 / 90.0, 0.1])
    return matrix, quad


D_PLAIN, QUAD = tables()
D_LIFT = D_PLAIN.copy()
D_LIFT[0, 0] += 5.0
D_LIFT[4, 4] -= 5.0


def split(x):
    high = x.astype(bf16)
    return high, (x - high.astype(f32)).astype(bf16)


def dot(a, b):
    return lax.dot_general(a, b, (((1,), (0,)), ((), ())), preferred_element_type=f32)


def derive_rows(rows, matrix):
    even0, odd0 = rows[0] + rows[4], rows[0] - rows[4]
    even1, odd1 = rows[1] + rows[3], rows[1] - rows[3]
    out = [None] * 5
    for r in (0, 1):
        m = [float(v) for v in matrix[r]]
        p = 0.5 * (m[0] + m[4]) * even0 + 0.5 * (m[1] + m[3]) * even1 + m[2] * rows[2]
        q = 0.5 * (m[0] - m[4]) * odd0 + 0.5 * (m[1] - m[3]) * odd1
        out[r] = q + p
        out[4 - r] = q - p
    out[2] = float(matrix[2, 0]) * odd0 + float(matrix[2, 1]) * odd1
    return out


class Along:
    def __init__(self, matrix):
        row = lax.broadcasted_iota(jnp.int32, (8, 128), 0)
        self.places = [jnp.where(row < 5, lax.rem(row + m, 5), row) for m in range(1, 5)]
        self.factors = []
        for m in range(1, 5):
            self.factors.append(self.by_row(row, [matrix[c, (c + m) % 5] for c in range(5)]))
        own = [matrix[c, c] for c in range(5)]
        self.own = self.by_row(row, own) if any(own) else None

    @staticmethod
    def by_row(row, values):
        out = jnp.zeros((8, 128), f32)
        for c in range(5):
            out = jnp.where(row == c, float(values[c]), out)
        return out

    def __call__(self, tile):
        total = None if self.own is None else tile * self.own
        for place, factor in zip(self.places, self.factors):
            term = jnp.take_along_axis(tile, place, axis=0) * factor
            total = term if total is None else total + term
        return total


def flat(ref, rows):
    return ref.reshape(rows, 128)


def make_perms(nbr, perms):
    source = lax.broadcasted_iota(jnp.int32, (N, N), 0)
    for k in range(4):
        hit = source == nbr[k : k + 1, :]
        perms[k] = jnp.where(hit, -5.0 if k % 2 == 0 else 5.0, 0.0).astype(bf16)


def permuted(face, matrix):
    rows = face.shape[0]
    both = dot(jnp.concatenate(split(face), axis=0), matrix)
    return both[:rows] + both[rows:]


def jumps(field, ys, first_z, perms, yj, zj):
    count = field.shape[1]
    for side, b in ((0, 4), (1, 0)):
        face = jnp.concatenate(
            [
                jnp.concatenate([field[h, k, :, b].reshape(40, 128) for h in range(2)], axis=1)
                for k in ys
            ],
            axis=0,
        )
        got = permuted(face, perms[side])
        for h in range(2):
            for i in range(3):
                part = got[40 * i : 40 * i + 40, 128 * h : 128 * h + 128]
                yj[side, h, i] = part.reshape(5, 8, 128)
    rows = flat(field, 2 * count * 200)
    into = flat(zj, 1200)
    spare = jnp.zeros((5, N), f32)
    for side, c in ((0, 4), (1, 0)):
        face = jnp.concatenate(
            [rows[pl.ds((h * count + first_z) * 200 + c, 75, 8), :] for h in range(2)], axis=1
        )
        got = permuted(jnp.concatenate([face, spare], axis=0), perms[2 + side])
        for h in range(2):
            into[pl.ds(h * 600 + (0, 4)[side], 75, 8), :] = got[:75, 128 * h : 128 * h + 128]


def stress_of(i, d):
    if isinstance(i, int):
        return i if i == d else 6 - i - d
    return jnp.where(i == d, i, 6 - i - d)


def halves(count, one, unrolled=False):
    if unrolled:
        for k in range(count):
            for h in range(2):
                one(k, h)
        return

    def step(t, carry):
        one(lax.div(t, 2), lax.rem(t, 2))
        return carry

    lax.fori_loop(0, 2 * count, step, 0)


def local_acceleration(stress, rinv, acc, perms, yj, zj):
    along = Along(D_LIFT)
    jumps(stress, (5, 1, 3), 2, perms, yj, zj)

    def one(i, h):
        kx, ky, kz = stress_of(i, 0), stress_of(i, 1), stress_of(i, 2)
        for a in range(5):
            ys = derive_rows([stress[h, ky, a, b] for b in range(5)], D_LIFT)
            ys[0] = ys[0] + yj[0, h, i, a]
            ys[4] = ys[4] + yj[1, h, i, a]
            for b in range(5):
                acc[h, i, a, b] = ys[b] + (along(stress[h, kz, a, b]) + zj[h, 2 - i, a, b])
        for b in range(5):
            xs = derive_rows([stress[h, kx, a, b] for a in range(5)], D_LIFT)
            for a in range(5):
                acc[h, i, a, b] = (acc[h, i, a, b] + xs[a]) * rinv[h, a, b]

    halves(3, one, True)


def load_fields(src, first, dst, count):
    def one(k, carry):
        for g in range(25):
            for h in range(2):
                dst[h, k, g // 5, g % 5, 0:5, :] = src[pl.ds(250 * (first + k) + 10 * g + h, 5, 2), :]
        return carry

    lax.fori_loop(0, count, one, 0)


def pack_face(dst, k, value, h):
    for b in range(5):
        dst[pl.ds(50 * k + 10 * b + h, 5, 2), :] = value[b, 0:5]


def unpack_face(dst, side, k, src, j):
    for h in range(2):
        for b in range(5):
            dst[side, h, k, b, 0:5, :] = src[pl.ds(50 * j + 10 * b + h, 5, 2), :]


def load_halo(halo, first, second, r_first, r_second, count):
    odd = lax.rem(lax.axis_index("slab"), 2)
    for side, src in ((1 - odd, first), (odd, second)):
        for k in range(count):
            unpack_face(halo, side, k, src, k)
    if r_first is not None:
        for side, src in ((1 - odd, r_first), (odd, r_second)):
            unpack_face(halo, side, 6, src, 6)


def pack_faces(first, second, values):
    odd = lax.rem(lax.axis_index("slab"), 2)
    for dst, a in ((first, 4 * (1 - odd)), (second, 4 * odd)):
        dst = flat(dst, dst.shape[0] * 2)
        for h in range(2):
            for k, value in enumerate(values(a, h)):
                pack_face(dst, k, value, h)


def finish_acceleration(acc, stress, rinv, halo, has_v):
    for h in range(2):
        for i in range(3):
            k = (0, 5, 4)[i]
            acc[h, i, 0] = acc[h, i, 0] - 5.0 * rinv[h, 0] * halo[0, h, i]
            acc[h, i, 4] = acc[h, i, 4] + 5.0 * rinv[h, 4] * halo[1, h, i]
            if has_v:
                halo[0, h, 3 + i] = halo[0, h, 3 + i] + halo[0, h, 6] * stress[h, k, 0]
                halo[1, h, 3 + i] = halo[1, h, 3 + i] - halo[1, h, 6] * stress[h, k, 4]


def source_rows(step, where_ref, pulse):
    lane = lax.broadcasted_iota(jnp.int32, (1, N), 1) + slab_base()
    hit = lane == where_ref[0]
    return [jnp.where(hit, pulse[0, step, i], 0.0) for i in range(3)]


def receiver_rows(where_ref, residual):
    element = lax.broadcasted_iota(jnp.int32, (N, N), 0) + slab_base()
    hits = jnp.where(element == where_ref[...], 1.0, 0.0).astype(bf16)
    spare = jnp.zeros((5, N), f32)
    x = jnp.concatenate([r for step in range(2) for r in [residual[i, step : step + 1] for i in range(3)] + [spare]], axis=0)
    total = None
    for part in range(3):
        high = x.astype(bf16)
        x = x - high.astype(f32)
        term = lax.dot_general(high, hits, (((1,), (1,)), ((), ())), preferred_element_type=f32)
        total = term if total is None else total + term
    return total


def slab_base():
    return lax.axis_index("slab") * N


def velocities(vel_in, vel, acc, rows):
    def one(i, h):
        for a in range(5):
            vel[h, i, a] = vel_in[h, i, a] + time_step * acc[h, i, a]

    halves(3, one, True)
    mask = lax.broadcasted_iota(jnp.int32, (8, 128), 0) == 2
    for i in range(3):
        for h in range(2):
            vel[h, i, 2, 2] += jnp.where(mask, rows[i][:, 128 * h : 128 * h + 128], 0.0)


def jump_gradients(vel, halo, grads, plain, perms, yj, zj):
    along = Along(D_LIFT)
    jumps(vel, (0, 1, 2), 0, perms, yj, zj)
    own = Along.by_row(lax.broadcasted_iota(jnp.int32, (8, 128), 0), [-5.0, 0.0, 0.0, 0.0, 5.0])

    def one(i, h):
        for a in range(5):
            v = [vel[h, i, a, b] for b in range(5)]
            ys = derive_rows(v, D_LIFT)
            zs = [along(v[b]) for b in range(5)]
            if plain is not None:
                for b in range(5):
                    plain[h, 3 + i, a, b] = ys[b] + {0: -5.0, 4: 5.0}[b] * v[b] if b in (0, 4) else ys[b]
                    plain[h, 6 + i, a, b] = zs[b] + own * v[b]
            ys[0] = ys[0] + yj[0, h, i, a]
            ys[4] = ys[4] + yj[1, h, i, a]
            for b in range(5):
                grads[h, 3 + i, a, b] = ys[b]
                grads[h, 6 + i, a, b] = zs[b] + zj[h, i, a, b]
        for b in range(5):
            v = [vel[h, i, a, b] for a in range(5)]
            xs = derive_rows(v, D_LIFT)
            if plain is not None:
                for a in range(5):
                    plain[h, i, a, b] = xs[a] + {0: -5.0, 4: 5.0}[a] * v[a] if a in (0, 4) else xs[a]
            xs[0] = xs[0] - 5.0 * halo[0, h, 3 + i, b]
            xs[4] = xs[4] + 5.0 * halo[1, h, 3 + i, b]
            for a in range(5):
                grads[h, i, a, b] = xs[a]

    halves(3, one, True)


def update_stress(stress_in, stress, grads, lam, mu):
    def one(a, h):
        g = lambda j, i: grads[h, 3 * j + i, a]
        l, m = lam[h, a], mu[h, a]
        both = l * (g(0, 0) + g(1, 1) + g(2, 2))
        for i in range(3):
            stress[h, i, a] = stress_in[h, i, a] + (both + 2.0 * m * g(i, i))
        stress[h, 3, a] = stress_in[h, 3, a] + m * (g(2, 1) + g(1, 2))
        stress[h, 4, a] = stress_in[h, 4, a] + m * (g(2, 0) + g(0, 2))
        stress[h, 5, a] = stress_in[h, 5, a] + m * (g(1, 0) + g(0, 1))

    halves(5, one, True)


def plain_gradients(vel, grads):
    along = Along(D_PLAIN)

    def one(i, h):
        for a in range(5):
            ys = derive_rows([vel[h, i, a, b] for b in range(5)], D_PLAIN)
            for b in range(5):
                grads[h, 3 + i, a, b] = ys[b]
                grads[h, 6 + i, a, b] = along(vel[h, i, a, b])
        for b in range(5):
            xs = derive_rows([vel[h, i, a, b] for a in range(5)], D_PLAIN)
            for a in range(5):
                grads[h, i, a, b] = xs[a]

    halves(3, one, True)


def reader(field, count):
    return lambda h, a, b: [field[h, k, a, b] for k in range(count)]


def image(f_read, g_read, acc_read, adj_vel, dense, first):
    row = lax.broadcasted_iota(jnp.int32, (8, 128), 0)
    weight = Along.by_row(row, QUAD)

    def one(k, h):
        for a in range(5):
            for b in range(5):
                fs, gs, accs = f_read(h, a, b), g_read(h, a, b), acc_read(h, a, b)
                f = lambda j, i: fs[3 * j + i]
                g = lambda j, i: gs[3 * j + i]
                w = weight * float(QUAD[a] * QUAD[b])
                f0, f1, f2 = f(0, 0), f(1, 1), f(2, 2)
                g0, g1, g2 = g(0, 0), g(1, 1), g(2, 2)
                trace = (f0 + f1 + f2) * (g0 + g1 + g2) * w
                cross = None
                for i, j in ((0, 1), (0, 2), (1, 2)):
                    term = (f(j, i) + f(i, j)) * (g(j, i) + g(i, j))
                    cross = term if cross is None else cross + term
                strain = (2.0 * (f0 * g0 + f1 * g1 + f2 * g2) + cross) * w
                inertia = None
                for i in range(3):
                    term = accs[i] * adj_vel[h, i, a, b]
                    inertia = term if inertia is None else inertia + term
                for t, term in enumerate((trace, strain, inertia * w)):
                    at = t * 125 + a * 25 + b * 5
                    if first is None:
                        dense[h, at : at + 5, :] = term[0:5]
                    else:
                        dense[h, at : at + 5, :] = first[h, at : at + 5, :] + term[0:5]

    halves(1, one)


def fetch(src, dst, sem):
    copy = pltpu.make_async_copy(src, dst, sem)
    copy.start()
    return copy


def start_common(src, rinv, perms, acc, vel, stress, one, two, yj, zj, with_r):
    src = flat(src, 2250)
    load_fields(src, 0, vel, 3)
    load_fields(src, 3, stress, 6)
    local_acceleration(stress, rinv, acc, perms, yj, zj)

    def values(a, h):
        out = [stress[h, k, a] for k in (0, 5, 4)] + [vel[h, i, a] + time_step * acc[h, i, a] for i in range(3)]
        return out + ([0.05 * rinv[h, a]] if with_r else [])

    pack_faces(one, two, values)


def load_material(mat, k, dst):
    for g in range(25):
        for h in range(2):
            dst[h, g // 5, g % 5, 0:5, :] = mat[5 * g : 5 * g + 5, k, 128 * h : 128 * h + 128]


def forward_start_kernel(state_hbm, mat_hbm, nbr_hbm, one, two, acc, vel, stress, rinv, perms, yj, zj, state, mat, nbr, sems):
    first = fetch(nbr_hbm, nbr, sems.at[0])
    third = fetch(state_hbm, state, sems.at[2])
    second = fetch(mat_hbm, mat, sems.at[1])
    first.wait()
    make_perms(nbr, perms)
    second.wait()
    load_material(mat, 2, rinv)
    for h in range(2):
        for a in range(5):
            rinv[h, a] = 1.0 / rinv[h, a]
    zj[...] = jnp.zeros(zj.shape, f32)
    third.wait()
    start_common(state, rinv, perms, acc, vel, stress, one, two, yj, zj, True)


def adjoint_start_kernel(state, mat, rinv, perms, receivers, residuals, one, two, acc, vel, stress, lam, mu,
                         end_grads, injected, yj, zj):
    zj[...] = jnp.zeros(zj.shape, f32)
    injected[...] = receiver_rows(receivers, residuals)
    start_common(state, rinv, perms, acc, vel, stress, one, two, yj, zj, False)
    for k, dst in ((0, lam), (1, mu)):
        load_material(mat, k, dst)
        for h in range(2):
            for a in range(5):
                dst[h, a] = time_step * dst[h, a]
    plain_gradients(vel, end_grads)


def complete_step(rows, vel_in, stress_in, lam, mu, rinv, perms, vel, stress, acc, halo, grads, plain, yj, zj):
    finish_acceleration(acc, stress_in, rinv, halo, True)
    velocities(vel_in, vel, acc, rows)
    jump_gradients(vel, halo, grads, plain, perms, yj, zj)
    update_stress(stress_in, stress, grads, lam, mu)


def middle_common(rows, vel_in, stress_in, acc_in, lam, mu, rinv, perms, near, far, r_near, r_far,
                  one, two, vel, stress, acc, next_acc, plain, halo, grads, yj, zj):
    zj[...] = jnp.zeros(zj.shape, f32)
    load_halo(halo, *(flat(r, r.shape[0] * 2) for r in (near, far, r_near, r_far)), 6)
    acc[...] = acc_in[...]
    complete_step(rows, vel_in, stress_in, lam, mu, rinv, perms, vel, stress, acc, halo, grads, plain, yj, zj)
    if next_acc is not None:
        local_acceleration(stress, rinv, next_acc, perms, yj, zj)

    def values(a, h):
        out = [stress[h, k, a] for k in (0, 5, 4)]
        if next_acc is not None:
            out += [vel[h, i, a] + time_step * next_acc[h, i, a] for i in range(3)]
        return out

    pack_faces(one, two, values)


def forward_middle_kernel(vel_in, stress_in, acc_in, lam, mu, rinv, perms, where_ref, strength, near, far,
                          one, two, vel, acc, plain, stress, halo, grads, yj, zj):
    middle_common(source_rows(0, where_ref, strength), vel_in, stress_in, acc_in, lam, mu, rinv, perms, near, far, near, far,
                  one, two, vel, stress, acc, None, plain, halo, grads, yj, zj)


def adjoint_middle_kernel(vel_in, stress_in, acc_in, lam, mu, rinv, perms, inject, near, far, r_near, r_far, f_plain, f_acc, f_stress,
                          f_vel, where_ref, pulse,
                          one, two, vel, stress, next_acc, dense, f_next_acc, f_early, acc, plain, halo, grads, yj, zj):
    rows = [inject[i : i + 1] for i in range(3)]
    middle_common(rows, vel_in, stress_in, acc_in, lam, mu, rinv, perms, near, far, r_near, r_far,
                  one, two, vel, stress, acc, next_acc, plain, halo, grads, yj, zj)
    image(reader(f_plain, 9), reader(plain, 9), reader(f_acc, 3), vel, dense, None)
    local_acceleration(f_stress, rinv, f_next_acc, perms, yj, zj)
    velocities(f_vel, acc, f_next_acc, source_rows(1, where_ref, pulse))
    plain_gradients(acc, f_early)


def last_kernel(vel_in, stress_in, acc_in, lam, mu, rinv, perms, inject, near, far, r_near, r_far,
                out, vel, stress, acc, halo, grads, yj, zj, rows_out, sems):
    zj[...] = jnp.zeros(zj.shape, f32)
    load_halo(halo, *(flat(r, r.shape[0] * 2) for r in (near, far, r_near, r_far)), 6)
    acc[...] = acc_in[...]
    rows = [inject[8 + i : 9 + i] for i in range(3)]
    finish_acceleration(acc, stress_in, rinv, halo, True)
    velocities(vel_in, vel, acc, rows)
    dst = flat(rows_out, 2250)

    def leave(first, k, field):
        for g in range(25):
            for h in range(2):
                dst[pl.ds(250 * (first + k) + 10 * g + h, 5, 2), :] = field[h, k, g // 5, g % 5, 0:5, :]
        there = pl.ds(125 * (first + k), 125)
        return pltpu.make_async_copy(rows_out.at[there], out.at[there], sems.at[first + k])

    def leave_all(first, count, field):
        def one(k, carry):
            leave(first, k, field).start()
            return carry

        lax.fori_loop(0, count, one, 0)

    leave_all(0, 3, vel)
    jump_gradients(vel, halo, grads, None, perms, yj, zj)
    update_stress(stress_in, stress, grads, lam, mu)
    leave_all(3, 6, stress)
    for k in range(9):
        there = pl.ds(125 * k, 125)
        pltpu.make_async_copy(rows_out.at[there], out.at[there], sems.at[k]).wait()


def last_image_kernel(acc, early, adj_vel, end_grads, first, rinv, near, far, keep, send, halo, change, turn, dense):
    load_halo(halo, flat(near, 150), flat(far, 150), None, None, 3)
    along = Along(D_PLAIN)
    for h in range(2):
        for i in range(3):
            for side, a in ((0, 0), (1, 4)):
                d = (5.0 if side else -5.0) * rinv[h, a] * halo[side, h, i]
                change[side, h, i] = d
                ys = derive_rows([time_step * d[b] for b in range(5)], D_PLAIN)
                for b in range(5):
                    turn[side, h, i, b] = ys[b]
                    turn[side, h, 3 + i, b] = along(time_step * d[b])

    def f_read(h, a, b):
        out = [early[h, k, a, b] for k in range(9)]
        low, high = float(time_step * D_PLAIN[a, 0]), float(time_step * D_PLAIN[a, 4])
        for i in range(3):
            out[i] = out[i] + (low * change[0, h, i, b] + high * change[1, h, i, b])
        if a in (0, 4):
            for k in range(6):
                out[3 + k] = out[3 + k] + turn[a // 4, h, k, b]
        return out

    def acc_read(h, a, b):
        if a in (0, 4):
            return [acc[h, i, a, b] + change[a // 4, h, i, b] for i in range(3)]
        return [acc[h, i, a, b] for i in range(3)]

    for h in range(2):
        dense[h, 368:384, :] = jnp.zeros((16, 128), f32)
    image(f_read, reader(end_grads, 9), acc_read, adj_vel, dense, first)
    core = lax.rem(lax.axis_index("shot"), 2)
    turned = [dense[h].T for h in range(2)]
    for parity, (mine, other) in ((0, (keep, send)), (1, (send, keep))):

        @pl.when(core == parity)
        def _():
            for s in range(16):
                piece = turned[s // 8][16 * (s % 8) : 16 * (s % 8) + 16]
                (mine if s % 2 == 0 else other)[s // 2] = piece


V = pl.BlockSpec(memory_space=pltpu.VMEM)
S = pl.BlockSpec(memory_space=pltpu.SMEM)


def shape(*dims):
    return jax.ShapeDtypeStruct(dims, f32)


def field(count):
    return shape(2, count, 5, 5, 8, 128)


ONE = shape(2, 5, 5, 8, 128)
PERMS = jax.ShapeDtypeStruct((4, N, N), bf16)


def sends(faces):
    return shape(faces * 25, 2, 128)


def scr(s):
    return pltpu.VMEM(s.shape, s.dtype)


JUMPS = [pltpu.VMEM((2, 2, 3, 5, 8, 128), f32), pltpu.VMEM((2, 3, 5, 5, 8, 128), f32)]
HALO = pltpu.VMEM((2, 2, 7, 5, 8, 128), f32)


def call(kernel, specs, outs, scratch, flops, moved, where=V):
    return pl.pallas_call(
        kernel,
        out_shape=outs,
        in_specs=specs,
        out_specs=jax.tree.map(lambda _: where, outs),
        scratch_shapes=scratch,
        compiler_params=pltpu.CompilerParams(vmem_limit_bytes=8 * 2**20),
        cost_estimate=pl.CostEstimate(flops=flops, bytes_accessed=moved, transcendentals=0),
    )


def both_ways(first, second):
    count = lax.axis_size("slab")
    near = [(i, i ^ 1) for i in range(count)]
    far = [(i, (i + (1 if i % 2 else -1)) % count) for i in range(count)]
    return lax.ppermute(first, "slab", near), lax.ppermute(second, "slab", far)


def core_sum_kernel(keep, got, mine, *others):
    line = lax.div(lax.axis_index("shot"), 4)
    for d, dst in enumerate((mine, *others)):
        to = lax.rem(line + d, 4)
        for high in range(2):
            dst[high] = keep[2 * to + high] + got[2 * to + high]


def line_sum_kernel(mine, one, two, three, keep, send):
    high = lax.rem(lax.div(lax.axis_index("shot"), 2), 2)
    for dst, k in ((keep, high), (send, 1 - high)):
        dst[...] = (mine[k] + one[k]) + (two[k] + three[k])


def last_sum_kernel(keep, got, out, rows):
    turned = (keep[...] + got[...]).T
    for t in range(3):
        rows[pl.ds(t, 125, 4), 0:16] = turned[125 * t : 125 * t + 125]
    out[...] = rows.reshape(125, 4, 128)[:, 0:3, 0:16]


def reduce_over_shots(keep, send):
    hop = lambda v, to: lax.ppermute(v, "shot", [(i, to(i)) for i in range(16)])
    pair, chunk = shape(2, 16, 384), shape(16, 384)
    mine, *others = call(core_sum_kernel, [V] * 2, (pair,) * 4, [], 1000, 1000)(keep, hop(send, lambda i: i ^ 1))
    got = [hop(x, lambda i: (i + 4 * d) % 16) for d, x in enumerate(others, 1)]
    keep, send = call(line_sum_kernel, [V] * 4, (chunk,) * 2, [], 1000, 1000)(mine, *got)
    return call(last_sum_kernel, [V] * 2, shape(125, 3, 16), [scr(shape(500, 128))], 1000, 1000)(keep, hop(send, lambda i: i ^ 2))


def body(fwd, adj, materials, nbr, source_element, pulse, receivers, residuals):
    receivers = receivers.reshape(1, N)
    fwd, adj = (x.reshape(1125, 2, 128) for x in (fwd, adj))
    mat = materials.transpose(1, 2, 3, 0, 4).reshape(125, 3, N)
    nbr = nbr.T
    residuals = residuals.transpose(0, 2, 1, 3).reshape(3, 2, N)

    f_one, f_two, f_acc, f_vel, f_stress, rinv, perms = call(
        forward_start_kernel,
        [pl.BlockSpec(memory_space=pltpu.HBM)] * 3,
        (sends(7), sends(7), field(3), field(3), field(6), ONE, PERMS),
        JUMPS + [scr(shape(1125, 2, 128)), scr(shape(125, 3, N)), pltpu.VMEM((4, N), jnp.int32), pltpu.SemaphoreType.DMA((3,))],
        10**8, 4 * 10**6,
    )(*(pltpu.with_memory_space_constraint(x, pltpu.HBM) for x in (fwd, mat, nbr)))
    f_near, f_far = both_ways(f_one, f_two)
    a_one, a_two, a_acc, a_vel, a_stress, lam, mu, end_grads, injected = call(
        adjoint_start_kernel,
        [V] * 6,
        (sends(6), sends(6), field(3), field(3), field(6), ONE, ONE, field(9), shape(16, N)),
        JUMPS,
        10**8, 4 * 10**6,
    )(adj, mat, rinv, perms, receivers, residuals)
    a_near, a_far = both_ways(a_one, a_two)
    adj_vel_end = a_vel

    f_one, f_two, f_vel1, f_acc1, f_plain, f_stress1 = call(
        forward_middle_kernel,
        [V] * 7 + [S] * 2 + [V] * 2,
        (sends(3), sends(3), field(3), field(3), field(9), field(6)),
        [HALO, scr(field(9))] + JUMPS,
        2 * 10**8, 8 * 10**6,
    )(f_vel, f_stress, f_acc, lam, mu, rinv, perms, source_element, pulse, f_near, f_far)
    f_near2, f_far2 = both_ways(f_one, f_two)
    a_one, a_two, a_vel1, a_stress1, a_acc2, first, f_acc2, f_early = call(
        adjoint_middle_kernel,
        [V] * 16 + [S] * 2,
        (sends(6), sends(6), field(3), field(6), field(3), shape(2, 384, 128), field(3), field(9)),
        [scr(field(3)), scr(field(9)), HALO, scr(field(9))] + JUMPS,
        2 * 10**8, 8 * 10**6,
    )(a_vel, a_stress, a_acc, lam, mu, rinv, perms, injected, a_near, a_far, f_near, f_far, f_plain, f_acc1, f_stress1, f_vel1, source_element, pulse)
    a_near2, a_far2 = both_ways(a_one, a_two)
    keep, send = call(
        last_image_kernel,
        [V] * 8,
        (shape(8, 16, 384), shape(8, 16, 384)),
        [HALO, pltpu.VMEM((2, 2, 3, 5, 8, 128), f32), pltpu.VMEM((2, 2, 6, 5, 8, 128), f32), scr(shape(2, 384, 128))],
        1000, 1000,
    )(f_acc2, f_early, adj_vel_end, end_grads, first, rinv, f_near2, f_far2)
    gradient = reduce_over_shots(keep, send)
    adjoint_end = call(
        last_kernel,
        [V] * 12,
        shape(1125, 2, 128),
        [scr(field(3)), scr(field(6)), scr(field(3)), HALO, scr(field(9))] + JUMPS
        + [scr(shape(1125, 2, 128)), pltpu.SemaphoreType.DMA((9,))],
        10**8, 8 * 10**6,
        pl.BlockSpec(memory_space=pltpu.HBM),
    )(a_vel1, a_stress1, a_acc2, lam, mu, rinv, perms, injected, a_near2, a_far2, f_near, f_far)
    return gradient.reshape(5, 5, 5, 3, 16).transpose(3, 0, 1, 2, 4), adjoint_end.reshape(1, 9, 5, 5, 5, N)


def solution(mesh):
    return jax.shard_map(
        body,
        mesh=mesh,
        in_specs=(
            P("shot", None, None, None, None, "slab"),
            P("shot", None, None, None, None, "slab"),
            P(None, None, None, None, "slab"),
            P(),
            P("shot"),
            P("shot", None, None),
            P(),
            P("shot", None, None, None),
        ),
        out_specs=(
            P(None, None, None, None, ("slab", "shot")),
            P("shot", None, None, None, None, "slab"),
        ),
        check_vma=False,
    )
```

```python
import math

import jax
import jax.numpy as jnp
import numpy as np
from jax import lax
from jax.experimental import pallas as pl
from jax.experimental.pallas import tpu as pltpu
from jax.sharding import PartitionSpec as P

f32 = jnp.float32
bf16 = jnp.bfloat16

time_step = 0.01
N = 256


def tables():
    root = math.sqrt(3.0 / 7.0)
    points = np.array([-1.0, -root, 0.0, root, 1.0])
    legendre = (35.0 * points**4 - 30.0 * points**2 + 3.0) / 8.0
    matrix = np.zeros((5, 5))
    for r in range(5):
        for c in range(5):
            if r != c:
                matrix[r, c] = legendre[r] / (legendre[c] * (points[r] - points[c]))
    matrix[0, 0] = -5.0
    matrix[4, 4] = 5.0
    quad = np.array([0.1, 49.0 / 90.0, 32.0 / 45.0, 49.0 / 90.0, 0.1])
    return matrix, quad


D_PLAIN, QUAD = tables()
D_LIFT = D_PLAIN.copy()
D_LIFT[0, 0] += 5.0
D_LIFT[4, 4] -= 5.0


def split(x):
    high = x.astype(bf16)
    return high, (x - high.astype(f32)).astype(bf16)


def dot(a, b):
    return lax.dot_general(a, b, (((1,), (0,)), ((), ())), preferred_element_type=f32)


def derive_rows(rows, matrix):
    even0, odd0 = rows[0] + rows[4], rows[0] - rows[4]
    even1, odd1 = rows[1] + rows[3], rows[1] - rows[3]
    out = [None] * 5
    for r in (0, 1):
        m = [float(v) for v in matrix[r]]
        p = 0.5 * (m[0] + m[4]) * even0 + 0.5 * (m[1] + m[3]) * even1 + m[2] * rows[2]
        q = 0.5 * (m[0] - m[4]) * odd0 + 0.5 * (m[1] - m[3]) * odd1
        out[r] = q + p
        out[4 - r] = q - p
    out[2] = float(matrix[2, 0]) * odd0 + float(matrix[2, 1]) * odd1
    return out


class Along:
    def __init__(self, matrix):
        row = lax.broadcasted_iota(jnp.int32, (8, 128), 0)
        self.places = [jnp.where(row < 5, lax.rem(row + m, 5), row) for m in range(1, 5)]
        self.factors = []
        for m in range(1, 5):
            self.factors.append(self.by_row(row, [matrix[c, (c + m) % 5] for c in range(5)]))
        own = [matrix[c, c] for c in range(5)]
        self.own = self.by_row(row, own) if any(own) else None

    @staticmethod
    def by_row(row, values):
        out = jnp.zeros((8, 128), f32)
        for c in range(5):
            out = jnp.where(row == c, float(values[c]), out)
        return out

    def __call__(self, tile):
        total = None if self.own is None else tile * self.own
        for place, factor in zip(self.places, self.factors):
            term = jnp.take_along_axis(tile, place, axis=0) * factor
            total = term if total is None else total + term
        return total


def flat(ref, rows):
    return ref.reshape(rows, 128)


def make_perms(nbr, perms):
    source = lax.broadcasted_iota(jnp.int32, (N, N), 0)
    for k in range(4):
        hit = source == nbr[k : k + 1, :]
        perms[k] = jnp.where(hit, -5.0 if k % 2 == 0 else 5.0, 0.0).astype(bf16)


def permuted(face, matrix):
    rows = face.shape[0]
    both = dot(jnp.concatenate(split(face), axis=0), matrix)
    return both[:rows] + both[rows:]


def jumps(field, ys, first_z, perms, yj, zj):
    count = field.shape[1]
    for side, b in ((0, 4), (1, 0)):
        face = jnp.concatenate(
            [
                jnp.concatenate([field[h, k, :, b].reshape(40, 128) for h in range(2)], axis=1)
                for k in ys
            ],
            axis=0,
        )
        got = permuted(face, perms[side])
        for h in range(2):
            for i in range(3):
                part = got[40 * i : 40 * i + 40, 128 * h : 128 * h + 128]
                yj[side, h, i] = part.reshape(5, 8, 128)
    rows = flat(field, 2 * count * 200)
    into = flat(zj, 1200)
    spare = jnp.zeros((5, N), f32)
    for side, c in ((0, 4), (1, 0)):
        face = jnp.concatenate(
            [rows[pl.ds((h * count + first_z) * 200 + c, 75, 8), :] for h in range(2)], axis=1
        )
        got = permuted(jnp.concatenate([face, spare], axis=0), perms[2 + side])
        for h in range(2):
            into[pl.ds(h * 600 + (0, 4)[side], 75, 8), :] = got[:75, 128 * h : 128 * h + 128]


def stress_of(i, d):
    if isinstance(i, int):
        return i if i == d else 6 - i - d
    return jnp.where(i == d, i, 6 - i - d)


def halves(count, one, unrolled=False):
    if unrolled:
        for k in range(count):
            for h in range(2):
                one(k, h)
        return

    def step(t, carry):
        one(lax.div(t, 2), lax.rem(t, 2))
        return carry

    lax.fori_loop(0, 2 * count, step, 0)


def local_acceleration(stress, rinv, acc, perms, yj, zj):
    along = Along(D_LIFT)
    jumps(stress, (5, 1, 3), 2, perms, yj, zj)

    def one(i, h):
        kx, ky, kz = stress_of(i, 0), stress_of(i, 1), stress_of(i, 2)
        for a in range(5):
            ys = derive_rows([stress[h, ky, a, b] for b in range(5)], D_LIFT)
            ys[0] = ys[0] + yj[0, h, i, a]
            ys[4] = ys[4] + yj[1, h, i, a]
            for b in range(5):
                acc[h, i, a, b] = ys[b] + (along(stress[h, kz, a, b]) + zj[h, 2 - i, a, b])
        for b in range(5):
            xs = derive_rows([stress[h, kx, a, b] for a in range(5)], D_LIFT)
            for a in range(5):
                acc[h, i, a, b] = (acc[h, i, a, b] + xs[a]) * rinv[h, a, b]

    halves(3, one, True)


def load_fields(src, first, dst, count):
    def one(k, carry):
        for g in range(25):
            for h in range(2):
                dst[h, k, g // 5, g % 5, 0:5, :] = src[pl.ds(250 * (first + k) + 10 * g + h, 5, 2), :]
        return carry

    lax.fori_loop(0, count, one, 0)


def pack_face(dst, k, value, h):
    for b in range(5):
        dst[pl.ds(50 * k + 10 * b + h, 5, 2), :] = value[b, 0:5]


def unpack_face(dst, side, k, src, j):
    for h in range(2):
        for b in range(5):
            dst[side, h, k, b, 0:5, :] = src[pl.ds(50 * j + 10 * b + h, 5, 2), :]


def load_halo(halo, first, second, r_first, r_second, count):
    odd = lax.rem(lax.axis_index("slab"), 2)
    for side, src in ((1 - odd, first), (odd, second)):
        for k in range(count):
            unpack_face(halo, side, k, src, k)
    if r_first is not None:
        for side, src in ((1 - odd, r_first), (odd, r_second)):
            unpack_face(halo, side, 6, src, 6)


def pack_faces(first, second, values):
    odd = lax.rem(lax.axis_index("slab"), 2)
    for dst, a in ((first, 4 * (1 - odd)), (second, 4 * odd)):
        dst = flat(dst, dst.shape[0] * 2)
        for h in range(2):
            for k, value in enumerate(values(a, h)):
                pack_face(dst, k, value, h)


def finish_acceleration(acc, stress, rinv, halo, has_v):
    for h in range(2):
        for i in range(3):
            k = (0, 5, 4)[i]
            acc[h, i, 0] = acc[h, i, 0] - 5.0 * rinv[h, 0] * halo[0, h, i]
            acc[h, i, 4] = acc[h, i, 4] + 5.0 * rinv[h, 4] * halo[1, h, i]
            if has_v:
                halo[0, h, 3 + i] = halo[0, h, 3 + i] + halo[0, h, 6] * stress[h, k, 0]
                halo[1, h, 3 + i] = halo[1, h, 3 + i] - halo[1, h, 6] * stress[h, k, 4]


def source_rows(step, where_ref, pulse):
    lane = lax.broadcasted_iota(jnp.int32, (1, N), 1) + slab_base()
    hit = lane == where_ref[0]
    return [jnp.where(hit, pulse[0, step, i], 0.0) for i in range(3)]


def receiver_rows(where_ref, residual):
    element = lax.broadcasted_iota(jnp.int32, (N, N), 0) + slab_base()
    hits = jnp.where(element == where_ref[...], 1.0, 0.0).astype(bf16)
    spare = jnp.zeros((5, N), f32)
    x = jnp.concatenate([r for step in range(2) for r in [residual[i, step : step + 1] for i in range(3)] + [spare]], axis=0)
    total = None
    for part in range(3):
        high = x.astype(bf16)
        x = x - high.astype(f32)
        term = lax.dot_general(high, hits, (((1,), (1,)), ((), ())), preferred_element_type=f32)
        total = term if total is None else total + term
    return total


def slab_base():
    return lax.axis_index("slab") * N


def velocities(vel_in, vel, acc, rows):
    def one(i, h):
        for a in range(5):
            vel[h, i, a] = vel_in[h, i, a] + time_step * acc[h, i, a]

    halves(3, one, True)
    mask = lax.broadcasted_iota(jnp.int32, (8, 128), 0) == 2
    for i in range(3):
        for h in range(2):
            vel[h, i, 2, 2] += jnp.where(mask, rows[i][:, 128 * h : 128 * h + 128], 0.0)


def jump_gradients(vel, halo, grads, plain, perms, yj, zj):
    along = Along(D_LIFT)
    jumps(vel, (0, 1, 2), 0, perms, yj, zj)
    own = Along.by_row(lax.broadcasted_iota(jnp.int32, (8, 128), 0), [-5.0, 0.0, 0.0, 0.0, 5.0])

    def one(i, h):
        for a in range(5):
            v = [vel[h, i, a, b] for b in range(5)]
            ys = derive_rows(v, D_LIFT)
            zs = [along(v[b]) for b in range(5)]
            if plain is not None:
                for b in range(5):
                    plain[h, 3 + i, a, b] = ys[b] + {0: -5.0, 4: 5.0}[b] * v[b] if b in (0, 4) else ys[b]
                    plain[h, 6 + i, a, b] = zs[b] + own * v[b]
            ys[0] = ys[0] + yj[0, h, i, a]
            ys[4] = ys[4] + yj[1, h, i, a]
            for b in range(5):
                grads[h, 3 + i, a, b] = ys[b]
                grads[h, 6 + i, a, b] = zs[b] + zj[h, i, a, b]
        for b in range(5):
            v = [vel[h, i, a, b] for a in range(5)]
            xs = derive_rows(v, D_LIFT)
            if plain is not None:
                for a in range(5):
                    plain[h, i, a, b] = xs[a] + {0: -5.0, 4: 5.0}[a] * v[a] if a in (0, 4) else xs[a]
            if halo is not None:
                xs[0] = xs[0] - 5.0 * halo[0, h, 3 + i, b]
                xs[4] = xs[4] + 5.0 * halo[1, h, 3 + i, b]
            for a in range(5):
                grads[h, i, a, b] = xs[a]

    halves(3, one, True)


def update_stress(stress_in, stress, read, lam, mu):
    def one(a, h):
        at = read(h, a)
        g = lambda j, i: at[3 * j + i]
        l, m = lam[h, a], mu[h, a]
        both = l * (g(0, 0) + g(1, 1) + g(2, 2))
        for i in range(3):
            stress[h, i, a] = stress_in[h, i, a] + (both + 2.0 * m * g(i, i))
        stress[h, 3, a] = stress_in[h, 3, a] + m * (g(2, 1) + g(1, 2))
        stress[h, 4, a] = stress_in[h, 4, a] + m * (g(2, 0) + g(0, 2))
        stress[h, 5, a] = stress_in[h, 5, a] + m * (g(1, 0) + g(0, 1))

    halves(5, one, True)


def plain_gradients(vel, grads):
    along = Along(D_PLAIN)

    def one(i, h):
        for a in range(5):
            ys = derive_rows([vel[h, i, a, b] for b in range(5)], D_PLAIN)
            for b in range(5):
                grads[h, 3 + i, a, b] = ys[b]
                grads[h, 6 + i, a, b] = along(vel[h, i, a, b])
        for b in range(5):
            xs = derive_rows([vel[h, i, a, b] for a in range(5)], D_PLAIN)
            for a in range(5):
                grads[h, i, a, b] = xs[a]

    halves(3, one, True)


def reader(field, count):
    return lambda h, a, b: [field[h, k, a, b] for k in range(count)]


def image(f_read, g_read, acc_read, adj_vel, dense, first):
    row = lax.broadcasted_iota(jnp.int32, (8, 128), 0)
    weight = Along.by_row(row, QUAD)

    def one(k, h):
        for a in range(5):
            for b in range(5):
                fs, gs, accs = f_read(h, a, b), g_read(h, a, b), acc_read(h, a, b)
                f = lambda j, i: fs[3 * j + i]
                g = lambda j, i: gs[3 * j + i]
                w = weight * float(QUAD[a] * QUAD[b])
                f0, f1, f2 = f(0, 0), f(1, 1), f(2, 2)
                g0, g1, g2 = g(0, 0), g(1, 1), g(2, 2)
                trace = (f0 + f1 + f2) * (g0 + g1 + g2) * w
                cross = None
                for i, j in ((0, 1), (0, 2), (1, 2)):
                    term = (f(j, i) + f(i, j)) * (g(j, i) + g(i, j))
                    cross = term if cross is None else cross + term
                strain = (2.0 * (f0 * g0 + f1 * g1 + f2 * g2) + cross) * w
                inertia = None
                for i in range(3):
                    term = accs[i] * adj_vel[h, i, a, b]
                    inertia = term if inertia is None else inertia + term
                for t, term in enumerate((trace, strain, inertia * w)):
                    at = t * 125 + a * 25 + b * 5
                    if first is None:
                        dense[h, at : at + 5, :] = term[0:5]
                    else:
                        dense[h, at : at + 5, :] = first[h, at : at + 5, :] + term[0:5]

    halves(1, one)


def fetch(src, dst, sem):
    copy = pltpu.make_async_copy(src, dst, sem)
    copy.start()
    return copy


def start_common(src, rinv, perms, acc, vel, stress, one, two, yj, zj, with_r):
    src = flat(src, 2250)
    load_fields(src, 0, vel, 3)
    load_fields(src, 3, stress, 6)
    local_acceleration(stress, rinv, acc, perms, yj, zj)

    def values(a, h):
        out = [stress[h, k, a] for k in (0, 5, 4)] + [vel[h, i, a] + time_step * acc[h, i, a] for i in range(3)]
        return out + ([0.05 * rinv[h, a]] if with_r else [])

    pack_faces(one, two, values)


def load_material(mat, k, dst):
    for g in range(25):
        for h in range(2):
            dst[h, g // 5, g % 5, 0:5, :] = mat[5 * g : 5 * g + 5, k, 128 * h : 128 * h + 128]


def forward_start_kernel(state_hbm, mat_hbm, nbr_hbm, one, two, acc, vel, stress, rinv, perms, yj, zj, state, mat, nbr, sems):
    first = fetch(nbr_hbm, nbr, sems.at[0])
    third = fetch(state_hbm, state, sems.at[2])
    second = fetch(mat_hbm, mat, sems.at[1])
    first.wait()
    make_perms(nbr, perms)
    second.wait()
    load_material(mat, 2, rinv)
    for h in range(2):
        for a in range(5):
            rinv[h, a] = 1.0 / rinv[h, a]
    zj[...] = jnp.zeros(zj.shape, f32)
    third.wait()
    start_common(state, rinv, perms, acc, vel, stress, one, two, yj, zj, True)


def adjoint_start_kernel(state, mat, rinv, perms, receivers, residuals, one, two, acc, vel, stress, lam, mu,
                         end_grads, injected, yj, zj):
    zj[...] = jnp.zeros(zj.shape, f32)
    injected[...] = receiver_rows(receivers, residuals)
    start_common(state, rinv, perms, acc, vel, stress, one, two, yj, zj, False)
    for k, dst in ((0, lam), (1, mu)):
        load_material(mat, k, dst)
        for h in range(2):
            for a in range(5):
                dst[h, a] = time_step * dst[h, a]
    plain_gradients(vel, end_grads)


def complete_step(rows, vel_in, stress_in, lam, mu, rinv, perms, vel, stress, acc, halo, grads, plain, yj, zj):
    finish_acceleration(acc, stress_in, rinv, halo, True)
    velocities(vel_in, vel, acc, rows)
    jump_gradients(vel, halo, grads, plain, perms, yj, zj)
    update_stress(stress_in, stress, lambda h, a: [grads[h, k, a] for k in range(9)], lam, mu)


def middle_common(rows, vel_in, stress_in, acc_in, lam, mu, rinv, perms, near, far, r_near, r_far,
                  one, two, vel, stress, acc, next_acc, plain, halo, grads, yj, zj):
    zj[...] = jnp.zeros(zj.shape, f32)
    load_halo(halo, *(flat(r, r.shape[0] * 2) for r in (near, far, r_near, r_far)), 6)
    acc[...] = acc_in[...]
    complete_step(rows, vel_in, stress_in, lam, mu, rinv, perms, vel, stress, acc, halo, grads, plain, yj, zj)
    if next_acc is not None:
        local_acceleration(stress, rinv, next_acc, perms, yj, zj)

    def values(a, h):
        out = [stress[h, k, a] for k in (0, 5, 4)]
        if next_acc is not None:
            out += [vel[h, i, a] + time_step * next_acc[h, i, a] for i in range(3)]
        return out

    pack_faces(one, two, values)


def forward_middle_kernel(vel_in, stress_in, acc_in, lam, mu, rinv, perms, where_ref, strength, near, far,
                          one, two, vel, acc, plain, stress, halo, grads, yj, zj):
    middle_common(source_rows(0, where_ref, strength), vel_in, stress_in, acc_in, lam, mu, rinv, perms, near, far, near, far,
                  one, two, vel, stress, acc, None, plain, halo, grads, yj, zj)


def adjoint_middle_kernel(vel_in, stress_in, acc_in, lam, mu, rinv, perms, inject, near, far, r_near, r_far, f_plain, f_acc, f_stress,
                          f_vel, where_ref, pulse,
                          one, two, vel, stress, next_acc, dense, f_next_acc, f_early, acc, plain, halo, grads, yj, zj):
    rows = [inject[i : i + 1] for i in range(3)]
    middle_common(rows, vel_in, stress_in, acc_in, lam, mu, rinv, perms, near, far, r_near, r_far,
                  one, two, vel, stress, acc, next_acc, plain, halo, grads, yj, zj)
    image(reader(f_plain, 9), reader(plain, 9), reader(f_acc, 3), vel, dense, None)
    local_acceleration(f_stress, rinv, f_next_acc, perms, yj, zj)
    velocities(f_vel, acc, f_next_acc, source_rows(1, where_ref, pulse))
    plain_gradients(acc, f_early)


def early_kernel(vel_in, acc, perms, inject, held, vel, grads, yj, zj):
    zj[...] = jnp.zeros(zj.shape, f32)
    velocities(vel_in, vel, acc, [inject[8 + i : 9 + i] for i in range(3)])
    jump_gradients(vel, None, grads, None, perms, yj, zj)


def plane_changes(change, turn, perms, zj):
    along = Along(D_LIFT)
    yj = []
    for side, b in ((0, 4), (1, 0)):
        face = jnp.concatenate(
            [
                jnp.concatenate([change[h, i, p, b] for h in range(2)], axis=1)
                for i in range(3)
                for p in range(2)
            ],
            axis=0,
        )
        yj.append(permuted(face, perms[side]))
    rows, into = flat(change, 480), flat(zj, 480)
    spare = jnp.zeros((2, N), f32)
    for side, c in ((0, 4), (1, 0)):
        face = jnp.concatenate([rows[pl.ds(240 * h + c, 30, 8), :] for h in range(2)], axis=1)
        got = permuted(jnp.concatenate([face, spare], axis=0), perms[2 + side])
        for h in range(2):
            into[pl.ds(240 * h + (0, 4)[side], 30, 8), :] = got[:30, 128 * h : 128 * h + 128]
    for h in range(2):
        for i in range(3):
            for p in range(2):
                d = [change[h, i, p, b] for b in range(5)]
                ys = derive_rows(d, D_LIFT)
                at = 8 * (2 * i + p)
                for b, got in ((0, yj[0]), (4, yj[1])):
                    ys[b] = ys[b] + got[at : at + 8, 128 * h : 128 * h + 128]
                for b in range(5):
                    turn[h, i, p, b] = ys[b]
                    turn[h, 3 + i, p, b] = along(d[b]) + zj[h, i, p, b]


def last_kernel(early_vel, early, stress_in, lam, mu, rinv, perms, near, far, r_near, r_far,
                out, vel, stress, halo, change, turn, zj, rows_out, sems):
    zj[...] = jnp.zeros(zj.shape, f32)
    load_halo(halo, *(flat(r, r.shape[0] * 2) for r in (near, far, r_near, r_far)), 6)
    vel[...] = early_vel[...]
    for h in range(2):
        for i in range(3):
            k = (0, 5, 4)[i]
            for p, a in ((0, 0), (1, 4)):
                d = (5.0 * time_step if p else -5.0 * time_step) * rinv[h, a] * halo[p, h, i]
                change[h, i, p] = d
                vel[h, i, a] = vel[h, i, a] + d
            halo[0, h, 3 + i] = halo[0, h, 3 + i] + halo[0, h, 6] * stress_in[h, k, 0]
            halo[1, h, 3 + i] = halo[1, h, 3 + i] - halo[1, h, 6] * stress_in[h, k, 4]
    dst = flat(rows_out, 2250)

    def leave(first, k, field):
        for g in range(25):
            for h in range(2):
                dst[pl.ds(250 * (first + k) + 10 * g + h, 5, 2), :] = field[h, k, g // 5, g % 5, 0:5, :]
        there = pl.ds(125 * (first + k), 125)
        return pltpu.make_async_copy(rows_out.at[there], out.at[there], sems.at[first + k])

    def leave_all(first, count, field):
        def one(k, carry):
            leave(first, k, field).start()
            return carry

        lax.fori_loop(0, count, one, 0)

    leave_all(0, 3, vel)
    plane_changes(change, turn, perms, zj)

    def read(h, a):
        at = [early[h, k, a] for k in range(9)]
        low, high = float(D_LIFT[a, 0]), float(D_LIFT[a, 4])
        for i in range(3):
            if low:
                at[i] = at[i] + low * change[h, i, 0]
            if high:
                at[i] = at[i] + high * change[h, i, 1]
            if a in (0, 4):
                at[i] = at[i] + (5.0 if a else -5.0) * halo[a // 4, h, 3 + i]
                for k in (3, 6):
                    at[k + i] = at[k + i] + turn[h, k - 3 + i, a // 4]
        return at

    update_stress(stress_in, stress, read, lam, mu)
    leave_all(3, 6, stress)
    for k in range(9):
        there = pl.ds(125 * k, 125)
        pltpu.make_async_copy(rows_out.at[there], out.at[there], sems.at[k]).wait()


def last_image_kernel(acc, early, adj_vel, end_grads, first, rinv, near, far, keep, send, halo, change, turn, dense):
    load_halo(halo, flat(near, 150), flat(far, 150), None, None, 3)
    along = Along(D_PLAIN)
    for h in range(2):
        for i in range(3):
            for side, a in ((0, 0), (1, 4)):
                d = (5.0 if side else -5.0) * rinv[h, a] * halo[side, h, i]
                change[side, h, i] = d
                ys = derive_rows([time_step * d[b] for b in range(5)], D_PLAIN)
                for b in range(5):
                    turn[side, h, i, b] = ys[b]
                    turn[side, h, 3 + i, b] = along(time_step * d[b])

    def f_read(h, a, b):
        out = [early[h, k, a, b] for k in range(9)]
        low, high = float(time_step * D_PLAIN[a, 0]), float(time_step * D_PLAIN[a, 4])
        for i in range(3):
            out[i] = out[i] + (low * change[0, h, i, b] + high * change[1, h, i, b])
        if a in (0, 4):
            for k in range(6):
                out[3 + k] = out[3 + k] + turn[a // 4, h, k, b]
        return out

    def acc_read(h, a, b):
        if a in (0, 4):
            return [acc[h, i, a, b] + change[a // 4, h, i, b] for i in range(3)]
        return [acc[h, i, a, b] for i in range(3)]

    for h in range(2):
        dense[h, 368:384, :] = jnp.zeros((16, 128), f32)
    image(f_read, reader(end_grads, 9), acc_read, adj_vel, dense, first)
    core = lax.rem(lax.axis_index("shot"), 2)
    turned = [dense[h].T for h in range(2)]
    for parity, (mine, other) in ((0, (keep, send)), (1, (send, keep))):

        @pl.when(core == parity)
        def _():
            for s in range(16):
                piece = turned[s // 8][16 * (s % 8) : 16 * (s % 8) + 16]
                (mine if s % 2 == 0 else other)[s // 2] = piece


V = pl.BlockSpec(memory_space=pltpu.VMEM)
S = pl.BlockSpec(memory_space=pltpu.SMEM)


def shape(*dims):
    return jax.ShapeDtypeStruct(dims, f32)


def field(count):
    return shape(2, count, 5, 5, 8, 128)


ONE = shape(2, 5, 5, 8, 128)
PERMS = jax.ShapeDtypeStruct((4, N, N), bf16)


def sends(faces):
    return shape(faces * 25, 2, 128)


def scr(s):
    return pltpu.VMEM(s.shape, s.dtype)


JUMPS = [pltpu.VMEM((2, 2, 3, 5, 8, 128), f32), pltpu.VMEM((2, 3, 5, 5, 8, 128), f32)]
HALO = pltpu.VMEM((2, 2, 7, 5, 8, 128), f32)


def call(kernel, specs, outs, scratch, flops, moved, where=V):
    return pl.pallas_call(
        kernel,
        out_shape=outs,
        in_specs=specs,
        out_specs=jax.tree.map(lambda _: where, outs),
        scratch_shapes=scratch,
        compiler_params=pltpu.CompilerParams(vmem_limit_bytes=8 * 2**20),
        cost_estimate=pl.CostEstimate(flops=flops, bytes_accessed=moved, transcendentals=0),
    )


def both_ways(first, second):
    count = lax.axis_size("slab")
    near = [(i, i ^ 1) for i in range(count)]
    far = [(i, (i + (1 if i % 2 else -1)) % count) for i in range(count)]
    return lax.ppermute(first, "slab", near), lax.ppermute(second, "slab", far)


def core_sum_kernel(keep, got, mine, *others):
    line = lax.div(lax.axis_index("shot"), 4)
    for d, dst in enumerate((mine, *others)):
        to = lax.rem(line + d, 4)
        for high in range(2):
            dst[high] = keep[2 * to + high] + got[2 * to + high]


def line_sum_kernel(mine, one, two, three, held, keep, send):
    high = lax.rem(lax.div(lax.axis_index("shot"), 2), 2)
    for dst, k in ((keep, high), (send, 1 - high)):
        dst[...] = (mine[k] + one[k]) + (two[k] + three[k])


def last_sum_kernel(keep, got, out, rows):
    turned = (keep[...] + got[...]).T
    for t in range(3):
        rows[pl.ds(t, 125, 4), 0:16] = turned[125 * t : 125 * t + 125]
    out[...] = rows.reshape(125, 4, 128)[:, 0:3, 0:16]


def reduce_over_shots(keep, send, beside):
    hop = lambda v, to: lax.ppermute(v, "shot", [(i, to(i)) for i in range(16)])
    pair, chunk, hold = shape(2, 16, 384), shape(16, 384), pl.BlockSpec(memory_space=pl.ANY)
    mine, *others = call(core_sum_kernel, [V] * 2, (pair,) * 4, [], 1000, 1000)(keep, hop(send, lambda i: i ^ 1))
    got = [hop(x, lambda i: (i + 4 * d) % 16) for d, x in enumerate(others, 1)]
    made = beside(mine)
    keep, send = call(line_sum_kernel, [V] * 4 + [hold], (chunk,) * 2, [], 1000, 1000)(mine, *got, made[0])
    result = call(last_sum_kernel, [V] * 2, shape(125, 3, 16), [scr(shape(500, 128))], 1000, 1000)(
        keep, hop(send, lambda i: i ^ 2)
    )
    return result, made


def body(fwd, adj, materials, nbr, source_element, pulse, receivers, residuals):
    receivers = receivers.reshape(1, N)
    fwd, adj = (x.reshape(1125, 2, 128) for x in (fwd, adj))
    mat = materials.transpose(1, 2, 3, 0, 4).reshape(125, 3, N)
    nbr = nbr.T
    residuals = residuals.transpose(0, 2, 1, 3).reshape(3, 2, N)

    f_one, f_two, f_acc, f_vel, f_stress, rinv, perms = call(
        forward_start_kernel,
        [pl.BlockSpec(memory_space=pltpu.HBM)] * 3,
        (sends(7), sends(7), field(3), field(3), field(6), ONE, PERMS),
        JUMPS + [scr(shape(1125, 2, 128)), scr(shape(125, 3, N)), pltpu.VMEM((4, N), jnp.int32), pltpu.SemaphoreType.DMA((3,))],
        10**8, 4 * 10**6,
    )(*(pltpu.with_memory_space_constraint(x, pltpu.HBM) for x in (fwd, mat, nbr)))
    f_near, f_far = both_ways(f_one, f_two)
    a_one, a_two, a_acc, a_vel, a_stress, lam, mu, end_grads, injected = call(
        adjoint_start_kernel,
        [V] * 6,
        (sends(6), sends(6), field(3), field(3), field(6), ONE, ONE, field(9), shape(16, N)),
        JUMPS,
        10**8, 4 * 10**6,
    )(adj, mat, rinv, perms, receivers, residuals)
    a_near, a_far = both_ways(a_one, a_two)
    adj_vel_end = a_vel

    f_one, f_two, f_vel1, f_acc1, f_plain, f_stress1 = call(
        forward_middle_kernel,
        [V] * 7 + [S] * 2 + [V] * 2,
        (sends(3), sends(3), field(3), field(3), field(9), field(6)),
        [HALO, scr(field(9))] + JUMPS,
        2 * 10**8, 8 * 10**6,
    )(f_vel, f_stress, f_acc, lam, mu, rinv, perms, source_element, pulse, f_near, f_far)
    f_near2, f_far2 = both_ways(f_one, f_two)
    a_one, a_two, a_vel1, a_stress1, a_acc2, first, f_acc2, f_early = call(
        adjoint_middle_kernel,
        [V] * 16 + [S] * 2,
        (sends(6), sends(6), field(3), field(6), field(3), shape(2, 384, 128), field(3), field(9)),
        [scr(field(3)), scr(field(9)), HALO, scr(field(9))] + JUMPS,
        2 * 10**8, 8 * 10**6,
    )(a_vel, a_stress, a_acc, lam, mu, rinv, perms, injected, a_near, a_far, f_near, f_far, f_plain, f_acc1, f_stress1, f_vel1, source_element, pulse)
    a_near2, a_far2 = both_ways(a_one, a_two)
    keep, send = call(
        last_image_kernel,
        [V] * 8,
        (shape(8, 16, 384), shape(8, 16, 384)),
        [HALO, pltpu.VMEM((2, 2, 3, 5, 8, 128), f32), pltpu.VMEM((2, 2, 6, 5, 8, 128), f32), scr(shape(2, 384, 128))],
        1000, 1000,
    )(f_acc2, f_early, adj_vel_end, end_grads, first, rinv, f_near2, f_far2)
    early_step = call(
        early_kernel,
        [V] * 4 + [pl.BlockSpec(memory_space=pl.ANY)],
        (field(3), field(9)),
        JUMPS,
        10**8, 8 * 10**6,
    )
    gradient, (early_vel, early) = reduce_over_shots(
        keep, send, lambda held: early_step(a_vel1, a_acc2, perms, injected, held)
    )
    adjoint_end = call(
        last_kernel,
        [V] * 11,
        shape(1125, 2, 128),
        [scr(field(3)), scr(field(6)), HALO]
        + [pltpu.VMEM((2, k, 2, 5, 8, 128), f32) for k in (3, 6, 3)]
        + [scr(shape(1125, 2, 128)), pltpu.SemaphoreType.DMA((9,))],
        10**8, 8 * 10**6,
        pl.BlockSpec(memory_space=pltpu.HBM),
    )(early_vel, early, a_stress1, lam, mu, rinv, perms, a_near2, a_far2, f_near, f_far)
    return gradient.reshape(5, 5, 5, 3, 16).transpose(3, 0, 1, 2, 4), adjoint_end.reshape(1, 9, 5, 5, 5, N)


def solution(mesh):
    return jax.shard_map(
        body,
        mesh=mesh,
        in_specs=(
            P("shot", None, None, None, None, "slab"),
            P("shot", None, None, None, None, "slab"),
            P(None, None, None, None, "slab"),
            P(),
            P("shot"),
            P("shot", None, None),
            P(),
            P("shot", None, None, None),
        ),
        out_specs=(
            P(None, None, None, None, ("slab", "shot")),
            P("shot", None, None, None, None, "slab"),
        ),
        check_vma=False,
    )
```

```python
import math

import jax
import jax.numpy as jnp
import numpy as np
from jax import lax
from jax.experimental import pallas as pl
from jax.experimental.pallas import tpu as pltpu
from jax.sharding import PartitionSpec as P

f32 = jnp.float32
bf16 = jnp.bfloat16

time_step = 0.01
N = 256


def tables():
    root = math.sqrt(3.0 / 7.0)
    points = np.array([-1.0, -root, 0.0, root, 1.0])
    legendre = (35.0 * points**4 - 30.0 * points**2 + 3.0) / 8.0
    matrix = np.zeros((5, 5))
    for r in range(5):
        for c in range(5):
            if r != c:
                matrix[r, c] = legendre[r] / (legendre[c] * (points[r] - points[c]))
    matrix[0, 0] = -5.0
    matrix[4, 4] = 5.0
    quad = np.array([0.1, 49.0 / 90.0, 32.0 / 45.0, 49.0 / 90.0, 0.1])
    return matrix, quad


D_PLAIN, QUAD = tables()
D_LIFT = D_PLAIN.copy()
D_LIFT[0, 0] += 5.0
D_LIFT[4, 4] -= 5.0


def split(x):
    high = x.astype(bf16)
    return high, (x - high.astype(f32)).astype(bf16)


def dot(a, b):
    return lax.dot_general(a, b, (((1,), (0,)), ((), ())), preferred_element_type=f32)


def derive_rows(rows, matrix):
    even0, odd0 = rows[0] + rows[4], rows[0] - rows[4]
    even1, odd1 = rows[1] + rows[3], rows[1] - rows[3]
    out = [None] * 5
    for r in (0, 1):
        m = [float(v) for v in matrix[r]]
        p = 0.5 * (m[0] + m[4]) * even0 + 0.5 * (m[1] + m[3]) * even1 + m[2] * rows[2]
        q = 0.5 * (m[0] - m[4]) * odd0 + 0.5 * (m[1] - m[3]) * odd1
        out[r] = q + p
        out[4 - r] = q - p
    out[2] = float(matrix[2, 0]) * odd0 + float(matrix[2, 1]) * odd1
    return out


class Along:
    def __init__(self, matrix):
        row = lax.broadcasted_iota(jnp.int32, (8, 128), 0)
        self.places = [jnp.where(row < 5, lax.rem(row + m, 5), row) for m in range(1, 5)]
        self.factors = []
        for m in range(1, 5):
            self.factors.append(self.by_row(row, [matrix[c, (c + m) % 5] for c in range(5)]))
        own = [matrix[c, c] for c in range(5)]
        self.own = self.by_row(row, own) if any(own) else None

    @staticmethod
    def by_row(row, values):
        out = jnp.zeros((8, 128), f32)
        for c in range(5):
            out = jnp.where(row == c, float(values[c]), out)
        return out

    def __call__(self, tile):
        total = None if self.own is None else tile * self.own
        for place, factor in zip(self.places, self.factors):
            term = jnp.take_along_axis(tile, place, axis=0) * factor
            total = term if total is None else total + term
        return total


def flat(ref, rows):
    return ref.reshape(rows, 128)


def make_perms(nbr, perms):
    source = lax.broadcasted_iota(jnp.int32, (N, N), 0)
    for k in range(4):
        hit = source == nbr[k : k + 1, :]
        perms[k] = jnp.where(hit, -5.0 if k % 2 == 0 else 5.0, 0.0).astype(bf16)


def permuted(face, matrix):
    rows = face.shape[0]
    both = dot(jnp.concatenate(split(face), axis=0), matrix)
    return both[:rows] + both[rows:]


def jumps(field, ys, first_z, perms, yj, zj):
    count = field.shape[1]
    for side, b in ((0, 4), (1, 0)):
        face = jnp.concatenate(
            [
                jnp.concatenate([field[h, k, :, b].reshape(40, 128) for h in range(2)], axis=1)
                for k in ys
            ],
            axis=0,
        )
        got = permuted(face, perms[side])
        for h in range(2):
            for i in range(3):
                part = got[40 * i : 40 * i + 40, 128 * h : 128 * h + 128]
                yj[side, h, i] = part.reshape(5, 8, 128)
    rows = flat(field, 2 * count * 200)
    into = flat(zj, 1200)
    spare = jnp.zeros((5, N), f32)
    for side, c in ((0, 4), (1, 0)):
        face = jnp.concatenate(
            [rows[pl.ds((h * count + first_z) * 200 + c, 75, 8), :] for h in range(2)], axis=1
        )
        got = permuted(jnp.concatenate([face, spare], axis=0), perms[2 + side])
        for h in range(2):
            into[pl.ds(h * 600 + (0, 4)[side], 75, 8), :] = got[:75, 128 * h : 128 * h + 128]


def stress_of(i, d):
    if isinstance(i, int):
        return i if i == d else 6 - i - d
    return jnp.where(i == d, i, 6 - i - d)


def halves(count, one, unrolled=False):
    if unrolled:
        for k in range(count):
            for h in range(2):
                one(k, h)
        return

    def step(t, carry):
        one(lax.div(t, 2), lax.rem(t, 2))
        return carry

    lax.fori_loop(0, 2 * count, step, 0)


def local_acceleration(stress, rinv, acc, perms, yj, zj):
    along = Along(D_LIFT)
    jumps(stress, (5, 1, 3), 2, perms, yj, zj)

    def one(i, h):
        kx, ky, kz = stress_of(i, 0), stress_of(i, 1), stress_of(i, 2)
        for a in range(5):
            ys = derive_rows([stress[h, ky, a, b] for b in range(5)], D_LIFT)
            ys[0] = ys[0] + yj[0, h, i, a]
            ys[4] = ys[4] + yj[1, h, i, a]
            for b in range(5):
                acc[h, i, a, b] = ys[b] + (along(stress[h, kz, a, b]) + zj[h, 2 - i, a, b])
        for b in range(5):
            xs = derive_rows([stress[h, kx, a, b] for a in range(5)], D_LIFT)
            for a in range(5):
                acc[h, i, a, b] = (acc[h, i, a, b] + xs[a]) * rinv[h, a, b]

    halves(3, one, True)


def load_fields(src, first, dst, count):
    def one(k, carry):
        for g in range(25):
            for h in range(2):
                dst[h, k, g // 5, g % 5, 0:5, :] = src[pl.ds(250 * (first + k) + 10 * g + h, 5, 2), :]
        return carry

    lax.fori_loop(0, count, one, 0)


def pack_face(dst, k, value, h):
    for b in range(5):
        dst[pl.ds(50 * k + 10 * b + h, 5, 2), :] = value[b, 0:5]


def unpack_face(dst, side, k, src, j):
    for h in range(2):
        for b in range(5):
            dst[side, h, k, b, 0:5, :] = src[pl.ds(50 * j + 10 * b + h, 5, 2), :]


def load_halo(halo, first, second, r_first, r_second, count):
    odd = lax.rem(lax.axis_index("slab"), 2)
    for side, src in ((1 - odd, first), (odd, second)):
        for k in range(count):
            unpack_face(halo, side, k, src, k)
    if r_first is not None:
        for side, src in ((1 - odd, r_first), (odd, r_second)):
            unpack_face(halo, side, 6, src, 6)


def pack_faces(first, second, values):
    odd = lax.rem(lax.axis_index("slab"), 2)
    for dst, a in ((first, 4 * (1 - odd)), (second, 4 * odd)):
        dst = flat(dst, dst.shape[0] * 2)
        for h in range(2):
            for k, value in enumerate(values(a, h)):
                pack_face(dst, k, value, h)


def finish_acceleration(acc, stress, rinv, halo, has_v):
    for h in range(2):
        for i in range(3):
            k = (0, 5, 4)[i]
            acc[h, i, 0] = acc[h, i, 0] - 5.0 * rinv[h, 0] * halo[0, h, i]
            acc[h, i, 4] = acc[h, i, 4] + 5.0 * rinv[h, 4] * halo[1, h, i]
            if has_v:
                halo[0, h, 3 + i] = halo[0, h, 3 + i] + halo[0, h, 6] * stress[h, k, 0]
                halo[1, h, 3 + i] = halo[1, h, 3 + i] - halo[1, h, 6] * stress[h, k, 4]


def source_rows(step, where_ref, pulse):
    lane = lax.broadcasted_iota(jnp.int32, (1, N), 1) + slab_base()
    hit = lane == where_ref[0]
    return [jnp.where(hit, pulse[0, step, i], 0.0) for i in range(3)]


def receiver_rows(where_ref, residual):
    element = lax.broadcasted_iota(jnp.int32, (N, N), 0) + slab_base()
    hits = jnp.where(element == where_ref[...], 1.0, 0.0).astype(bf16)
    spare = jnp.zeros((5, N), f32)
    x = jnp.concatenate([r for step in range(2) for r in [residual[i, step : step + 1] for i in range(3)] + [spare]], axis=0)
    total = None
    for part in range(3):
        high = x.astype(bf16)
        x = x - high.astype(f32)
        term = lax.dot_general(high, hits, (((1,), (1,)), ((), ())), preferred_element_type=f32)
        total = term if total is None else total + term
    return total


def slab_base():
    return lax.axis_index("slab") * N


def velocities(vel_in, vel, acc, rows):
    def one(i, h):
        for a in range(5):
            vel[h, i, a] = vel_in[h, i, a] + time_step * acc[h, i, a]

    halves(3, one, True)
    mask = lax.broadcasted_iota(jnp.int32, (8, 128), 0) == 2
    for i in range(3):
        for h in range(2):
            vel[h, i, 2, 2] += jnp.where(mask, rows[i][:, 128 * h : 128 * h + 128], 0.0)


def jump_gradients(vel, halo, grads, plain, perms, yj, zj):
    along = Along(D_LIFT)
    jumps(vel, (0, 1, 2), 0, perms, yj, zj)
    own = Along.by_row(lax.broadcasted_iota(jnp.int32, (8, 128), 0), [-5.0, 0.0, 0.0, 0.0, 5.0])

    def one(i, h):
        for a in range(5):
            v = [vel[h, i, a, b] for b in range(5)]
            ys = derive_rows(v, D_LIFT)
            zs = [along(v[b]) for b in range(5)]
            if plain is not None:
                for b in range(5):
                    plain[h, 3 + i, a, b] = ys[b] + {0: -5.0, 4: 5.0}[b] * v[b] if b in (0, 4) else ys[b]
                    plain[h, 6 + i, a, b] = zs[b] + own * v[b]
            ys[0] = ys[0] + yj[0, h, i, a]
            ys[4] = ys[4] + yj[1, h, i, a]
            for b in range(5):
                grads[h, 3 + i, a, b] = ys[b]
                grads[h, 6 + i, a, b] = zs[b] + zj[h, i, a, b]
        for b in range(5):
            v = [vel[h, i, a, b] for a in range(5)]
            xs = derive_rows(v, D_LIFT)
            if plain is not None:
                for a in range(5):
                    plain[h, i, a, b] = xs[a] + {0: -5.0, 4: 5.0}[a] * v[a] if a in (0, 4) else xs[a]
            if halo is not None:
                xs[0] = xs[0] - 5.0 * halo[0, h, 3 + i, b]
                xs[4] = xs[4] + 5.0 * halo[1, h, 3 + i, b]
            for a in range(5):
                grads[h, i, a, b] = xs[a]

    halves(3, one, True)


def update_stress(stress_in, stress, read, lam, mu):
    def one(a, h):
        at = read(h, a)
        g = lambda j, i: at[3 * j + i]
        l, m = lam[h, a], mu[h, a]
        both = l * (g(0, 0) + g(1, 1) + g(2, 2))
        for i in range(3):
            stress[h, i, a] = stress_in[h, i, a] + (both + 2.0 * m * g(i, i))
        stress[h, 3, a] = stress_in[h, 3, a] + m * (g(2, 1) + g(1, 2))
        stress[h, 4, a] = stress_in[h, 4, a] + m * (g(2, 0) + g(0, 2))
        stress[h, 5, a] = stress_in[h, 5, a] + m * (g(1, 0) + g(0, 1))

    halves(5, one, True)


def plain_gradients(vel, grads):
    along = Along(D_PLAIN)

    def one(i, h):
        for a in range(5):
            ys = derive_rows([vel[h, i, a, b] for b in range(5)], D_PLAIN)
            for b in range(5):
                grads[h, 3 + i, a, b] = ys[b]
                grads[h, 6 + i, a, b] = along(vel[h, i, a, b])
        for b in range(5):
            xs = derive_rows([vel[h, i, a, b] for a in range(5)], D_PLAIN)
            for a in range(5):
                grads[h, i, a, b] = xs[a]

    halves(3, one, True)


def reader(field, count):
    return lambda h, a, b: [field[h, k, a, b] for k in range(count)]


def image(f_read, g_read, acc_read, adj_vel, dense, first):
    row = lax.broadcasted_iota(jnp.int32, (8, 128), 0)
    weight = Along.by_row(row, QUAD)

    def one(k, h):
        for a in range(5):
            for b in range(5):
                fs, gs, accs = f_read(h, a, b), g_read(h, a, b), acc_read(h, a, b)
                f = lambda j, i: fs[3 * j + i]
                g = lambda j, i: gs[3 * j + i]
                w = weight * float(QUAD[a] * QUAD[b])
                f0, f1, f2 = f(0, 0), f(1, 1), f(2, 2)
                g0, g1, g2 = g(0, 0), g(1, 1), g(2, 2)
                trace = (f0 + f1 + f2) * (g0 + g1 + g2) * w
                cross = None
                for i, j in ((0, 1), (0, 2), (1, 2)):
                    term = (f(j, i) + f(i, j)) * (g(j, i) + g(i, j))
                    cross = term if cross is None else cross + term
                strain = (2.0 * (f0 * g0 + f1 * g1 + f2 * g2) + cross) * w
                inertia = None
                for i in range(3):
                    term = accs[i] * adj_vel[h, i, a, b]
                    inertia = term if inertia is None else inertia + term
                for t, term in enumerate((trace, strain, inertia * w)):
                    at = t * 125 + a * 25 + b * 5
                    if first is None:
                        dense[h, at : at + 5, :] = term[0:5]
                    else:
                        dense[h, at : at + 5, :] = first[h, at : at + 5, :] + term[0:5]

    halves(1, one)


def fetch(src, dst, sem):
    copy = pltpu.make_async_copy(src, dst, sem)
    copy.start()
    return copy


def start_common(src, rinv, perms, acc, vel, stress, one, two, yj, zj, with_r):
    src = flat(src, 2250)
    load_fields(src, 0, vel, 3)
    load_fields(src, 3, stress, 6)
    local_acceleration(stress, rinv, acc, perms, yj, zj)

    def values(a, h):
        out = [stress[h, k, a] for k in (0, 5, 4)] + [vel[h, i, a] + time_step * acc[h, i, a] for i in range(3)]
        return out + ([0.05 * rinv[h, a]] if with_r else [])

    pack_faces(one, two, values)


def load_material(mat, k, dst):
    for g in range(25):
        for h in range(2):
            dst[h, g // 5, g % 5, 0:5, :] = mat[5 * g : 5 * g + 5, k, 128 * h : 128 * h + 128]


def forward_start_kernel(state_hbm, mat_hbm, nbr_hbm, one, two, acc, vel, stress, rinv, perms, yj, zj, state, mat, nbr, sems):
    first = fetch(nbr_hbm, nbr, sems.at[0])
    third = fetch(state_hbm, state, sems.at[2])
    second = fetch(mat_hbm, mat, sems.at[1])
    first.wait()
    make_perms(nbr, perms)
    second.wait()
    load_material(mat, 2, rinv)
    for h in range(2):
        for a in range(5):
            rinv[h, a] = 1.0 / rinv[h, a]
    zj[...] = jnp.zeros(zj.shape, f32)
    third.wait()
    start_common(state, rinv, perms, acc, vel, stress, one, two, yj, zj, True)


def adjoint_start_kernel(state, mat, rinv, perms, receivers, residuals, one, two, acc, vel, stress, lam, mu,
                         end_grads, injected, yj, zj):
    zj[...] = jnp.zeros(zj.shape, f32)
    injected[...] = receiver_rows(receivers, residuals)
    start_common(state, rinv, perms, acc, vel, stress, one, two, yj, zj, False)
    for k, dst in ((0, lam), (1, mu)):
        load_material(mat, k, dst)
        for h in range(2):
            for a in range(5):
                dst[h, a] = time_step * dst[h, a]
    plain_gradients(vel, end_grads)


def complete_step(rows, vel_in, stress_in, lam, mu, rinv, perms, vel, stress, acc, halo, grads, plain, yj, zj):
    finish_acceleration(acc, stress_in, rinv, halo, True)
    velocities(vel_in, vel, acc, rows)
    jump_gradients(vel, halo, grads, plain, perms, yj, zj)
    update_stress(stress_in, stress, lambda h, a: [grads[h, k, a] for k in range(9)], lam, mu)


def middle_common(rows, vel_in, stress_in, acc_in, lam, mu, rinv, perms, near, far, r_near, r_far,
                  one, two, vel, stress, acc, next_acc, plain, halo, grads, yj, zj):
    zj[...] = jnp.zeros(zj.shape, f32)
    load_halo(halo, *(flat(r, r.shape[0] * 2) for r in (near, far, r_near, r_far)), 6)
    acc[...] = acc_in[...]
    complete_step(rows, vel_in, stress_in, lam, mu, rinv, perms, vel, stress, acc, halo, grads, plain, yj, zj)
    if next_acc is not None:
        local_acceleration(stress, rinv, next_acc, perms, yj, zj)

    def values(a, h):
        out = [stress[h, k, a] for k in (0, 5, 4)]
        if next_acc is not None:
            out += [vel[h, i, a] + time_step * next_acc[h, i, a] for i in range(3)]
        return out

    pack_faces(one, two, values)


def forward_middle_kernel(vel_in, stress_in, acc_in, lam, mu, rinv, perms, where_ref, strength, near, far,
                          one, two, vel, acc, plain, stress, halo, grads, yj, zj):
    middle_common(source_rows(0, where_ref, strength), vel_in, stress_in, acc_in, lam, mu, rinv, perms, near, far, near, far,
                  one, two, vel, stress, acc, None, plain, halo, grads, yj, zj)


def adjoint_middle_kernel(vel_in, stress_in, acc_in, lam, mu, rinv, perms, inject, near, far, r_near, r_far, f_plain, f_acc, f_stress,
                          f_vel, where_ref, pulse,
                          one, two, vel, stress, next_acc, dense, f_next_acc, f_early, acc, plain, halo, grads, yj, zj):
    rows = [inject[i : i + 1] for i in range(3)]
    middle_common(rows, vel_in, stress_in, acc_in, lam, mu, rinv, perms, near, far, r_near, r_far,
                  one, two, vel, stress, acc, next_acc, plain, halo, grads, yj, zj)
    image(reader(f_plain, 9), reader(plain, 9), reader(f_acc, 3), vel, dense, None)
    local_acceleration(f_stress, rinv, f_next_acc, perms, yj, zj)
    velocities(f_vel, acc, f_next_acc, source_rows(1, where_ref, pulse))
    plain_gradients(acc, f_early)


def early_kernel(vel_in, acc, perms, inject, held, vel, grads, yj, zj):
    zj[...] = jnp.zeros(zj.shape, f32)
    velocities(vel_in, vel, acc, [inject[8 + i : 9 + i] for i in range(3)])
    jump_gradients(vel, None, grads, None, perms, yj, zj)


def plane_changes(change, turn, perms, zj):
    along = Along(D_LIFT)
    yj = []
    for side, b in ((0, 4), (1, 0)):
        face = jnp.concatenate(
            [
                jnp.concatenate([change[h, i, p, b] for h in range(2)], axis=1)
                for i in range(3)
                for p in range(2)
            ],
            axis=0,
        )
        yj.append(permuted(face, perms[side]))
    rows, into = flat(change, 480), flat(zj, 480)
    spare = jnp.zeros((2, N), f32)
    for side, c in ((0, 4), (1, 0)):
        face = jnp.concatenate([rows[pl.ds(240 * h + c, 30, 8), :] for h in range(2)], axis=1)
        got = permuted(jnp.concatenate([face, spare], axis=0), perms[2 + side])
        for h in range(2):
            into[pl.ds(240 * h + (0, 4)[side], 30, 8), :] = got[:30, 128 * h : 128 * h + 128]
    for h in range(2):
        for i in range(3):
            for p in range(2):
                d = [change[h, i, p, b] for b in range(5)]
                ys = derive_rows(d, D_LIFT)
                at = 8 * (2 * i + p)
                for b, got in ((0, yj[0]), (4, yj[1])):
                    ys[b] = ys[b] + got[at : at + 8, 128 * h : 128 * h + 128]
                for b in range(5):
                    turn[h, i, p, b] = ys[b]
                    turn[h, 3 + i, p, b] = along(d[b]) + zj[h, i, p, b]


def last_kernel(early_vel, early, stress_in, lam, mu, rinv, perms, near, far, r_near, r_far,
                out, vel, stress, halo, change, turn, zj, rows_out, sems):
    zj[...] = jnp.zeros(zj.shape, f32)
    load_halo(halo, *(flat(r, r.shape[0] * 2) for r in (near, far, r_near, r_far)), 6)
    vel[...] = early_vel[...]
    for h in range(2):
        for i in range(3):
            k = (0, 5, 4)[i]
            for p, a in ((0, 0), (1, 4)):
                d = (5.0 * time_step if p else -5.0 * time_step) * rinv[h, a] * halo[p, h, i]
                change[h, i, p] = d
                vel[h, i, a] = vel[h, i, a] + d
            halo[0, h, 3 + i] = halo[0, h, 3 + i] + halo[0, h, 6] * stress_in[h, k, 0]
            halo[1, h, 3 + i] = halo[1, h, 3 + i] - halo[1, h, 6] * stress_in[h, k, 4]
    dst = flat(rows_out, 2250)

    def leave(first, k, field):
        for g in range(25):
            for h in range(2):
                dst[pl.ds(250 * (first + k) + 10 * g + h, 5, 2), :] = field[h, k, g // 5, g % 5, 0:5, :]
        there = pl.ds(125 * (first + k), 125)
        return pltpu.make_async_copy(rows_out.at[there], out.at[there], sems.at[first + k])

    def leave_all(first, count, field):
        def one(k, carry):
            leave(first, k, field).start()
            return carry

        lax.fori_loop(0, count, one, 0)

    leave_all(0, 3, vel)
    plane_changes(change, turn, perms, zj)

    def read(h, a):
        at = [early[h, k, a] for k in range(9)]
        low, high = float(D_LIFT[a, 0]), float(D_LIFT[a, 4])
        for i in range(3):
            if low:
                at[i] = at[i] + low * change[h, i, 0]
            if high:
                at[i] = at[i] + high * change[h, i, 1]
            if a in (0, 4):
                at[i] = at[i] + (5.0 if a else -5.0) * halo[a // 4, h, 3 + i]
                for k in (3, 6):
                    at[k + i] = at[k + i] + turn[h, k - 3 + i, a // 4]
        return at

    update_stress(stress_in, stress, read, lam, mu)
    leave_all(3, 6, stress)
    for k in range(9):
        there = pl.ds(125 * k, 125)
        pltpu.make_async_copy(rows_out.at[there], out.at[there], sems.at[k]).wait()


def last_image_kernel(acc, early, adj_vel, end_grads, first, rinv, near, far, keep, send, halo, change, turn, dense):
    load_halo(halo, flat(near, 150), flat(far, 150), None, None, 3)
    along = Along(D_PLAIN)
    for h in range(2):
        for i in range(3):
            for side, a in ((0, 0), (1, 4)):
                d = (5.0 if side else -5.0) * rinv[h, a] * halo[side, h, i]
                change[side, h, i] = d
                ys = derive_rows([time_step * d[b] for b in range(5)], D_PLAIN)
                for b in range(5):
                    turn[side, h, i, b] = ys[b]
                    turn[side, h, 3 + i, b] = along(time_step * d[b])

    def f_read(h, a, b):
        out = [early[h, k, a, b] for k in range(9)]
        low, high = float(time_step * D_PLAIN[a, 0]), float(time_step * D_PLAIN[a, 4])
        for i in range(3):
            out[i] = out[i] + (low * change[0, h, i, b] + high * change[1, h, i, b])
        if a in (0, 4):
            for k in range(6):
                out[3 + k] = out[3 + k] + turn[a // 4, h, k, b]
        return out

    def acc_read(h, a, b):
        if a in (0, 4):
            return [acc[h, i, a, b] + change[a // 4, h, i, b] for i in range(3)]
        return [acc[h, i, a, b] for i in range(3)]

    for h in range(2):
        dense[h, 368:384, :] = jnp.zeros((16, 128), f32)
    image(f_read, reader(end_grads, 9), acc_read, adj_vel, dense, first)
    core = lax.rem(lax.axis_index("shot"), 2)
    turned = [dense[h].T for h in range(2)]
    for parity, (mine, other) in ((0, (keep, send)), (1, (send, keep))):

        @pl.when(core == parity)
        def _():
            for s in range(16):
                piece = turned[s // 8][16 * (s % 8) : 16 * (s % 8) + 16]
                (mine if s % 2 == 0 else other)[s // 2] = piece


V = pl.BlockSpec(memory_space=pltpu.VMEM)
S = pl.BlockSpec(memory_space=pltpu.SMEM)


def shape(*dims):
    return jax.ShapeDtypeStruct(dims, f32)


def field(count):
    return shape(2, count, 5, 5, 8, 128)


ONE = shape(2, 5, 5, 8, 128)
PERMS = jax.ShapeDtypeStruct((4, N, N), bf16)


def sends(faces):
    return shape(faces * 25, 2, 128)


def scr(s):
    return pltpu.VMEM(s.shape, s.dtype)


JUMPS = [pltpu.VMEM((2, 2, 3, 5, 8, 128), f32), pltpu.VMEM((2, 3, 5, 5, 8, 128), f32)]
HALO = pltpu.VMEM((2, 2, 7, 5, 8, 128), f32)


def call(kernel, specs, outs, scratch, flops, moved, where=V):
    return pl.pallas_call(
        kernel,
        out_shape=outs,
        in_specs=specs,
        out_specs=jax.tree.map(lambda _: where, outs),
        scratch_shapes=scratch,
        compiler_params=pltpu.CompilerParams(vmem_limit_bytes=8 * 2**20),
        cost_estimate=pl.CostEstimate(flops=flops, bytes_accessed=moved, transcendentals=0),
    )


def both_ways(first, second):
    count = lax.axis_size("slab")
    near = [(i, i ^ 1) for i in range(count)]
    far = [(i, (i + (1 if i % 2 else -1)) % count) for i in range(count)]
    return lax.ppermute(first, "slab", near), lax.ppermute(second, "slab", far)


def core_sum_kernel(keep, got, mine, *others):
    line = lax.div(lax.axis_index("shot"), 4)
    for d, dst in zip((0, 2, 1, 3), (mine, *others)):
        to = lax.rem(line + d, 4)
        for high in range(2):
            dst[high] = keep[2 * to + high] + got[2 * to + high]


def line_sum_kernel(mine, one, two, three, held, keep, send):
    high = lax.rem(lax.div(lax.axis_index("shot"), 2), 2)
    for dst, k in ((keep, high), (send, 1 - high)):
        dst[...] = (mine[k] + one[k]) + (two[k] + three[k])


def last_sum_kernel(keep, got, out, rows):
    turned = (keep[...] + got[...]).T
    for t in range(3):
        rows[pl.ds(t, 125, 4), 0:16] = turned[125 * t : 125 * t + 125]
    out[...] = rows.reshape(125, 4, 128)[:, 0:3, 0:16]


def reduce_over_shots(keep, send, beside):
    hop = lambda v, to: lax.ppermute(v, "shot", [(i, to(i)) for i in range(16)])
    pair, chunk, hold = shape(2, 16, 384), shape(16, 384), pl.BlockSpec(memory_space=pl.ANY)
    mine, *others = call(core_sum_kernel, [V] * 2, (pair,) * 4, [], 1000, 1000)(keep, hop(send, lambda i: i ^ 1))
    got = [hop(x, lambda i: (i + 4 * d) % 16) for d, x in zip((2, 1, 3), others)]
    made = beside(mine)
    keep, send = call(line_sum_kernel, [V] * 4 + [hold], (chunk,) * 2, [], 1000, 1000)(mine, *got, made[0])
    result = call(last_sum_kernel, [V] * 2, shape(125, 3, 16), [scr(shape(500, 128))], 1000, 1000)(
        keep, hop(send, lambda i: i ^ 2)
    )
    return result, made


def body(fwd, adj, materials, nbr, source_element, pulse, receivers, residuals):
    receivers = receivers.reshape(1, N)
    fwd, adj = (x.reshape(1125, 2, 128) for x in (fwd, adj))
    mat = materials.transpose(1, 2, 3, 0, 4).reshape(125, 3, N)
    nbr = nbr.T
    residuals = residuals.transpose(0, 2, 1, 3).reshape(3, 2, N)

    f_one, f_two, f_acc, f_vel, f_stress, rinv, perms = call(
        forward_start_kernel,
        [pl.BlockSpec(memory_space=pltpu.HBM)] * 3,
        (sends(7), sends(7), field(3), field(3), field(6), ONE, PERMS),
        JUMPS + [scr(shape(1125, 2, 128)), scr(shape(125, 3, N)), pltpu.VMEM((4, N), jnp.int32), pltpu.SemaphoreType.DMA((3,))],
        10**8, 4 * 10**6,
    )(*(pltpu.with_memory_space_constraint(x, pltpu.HBM) for x in (fwd, mat, nbr)))
    f_near, f_far = both_ways(f_one, f_two)
    a_one, a_two, a_acc, a_vel, a_stress, lam, mu, end_grads, injected = call(
        adjoint_start_kernel,
        [V] * 6,
        (sends(6), sends(6), field(3), field(3), field(6), ONE, ONE, field(9), shape(16, N)),
        JUMPS,
        10**8, 4 * 10**6,
    )(adj, mat, rinv, perms, receivers, residuals)
    a_near, a_far = both_ways(a_one, a_two)
    adj_vel_end = a_vel

    f_one, f_two, f_vel1, f_acc1, f_plain, f_stress1 = call(
        forward_middle_kernel,
        [V] * 7 + [S] * 2 + [V] * 2,
        (sends(3), sends(3), field(3), field(3), field(9), field(6)),
        [HALO, scr(field(9))] + JUMPS,
        2 * 10**8, 8 * 10**6,
    )(f_vel, f_stress, f_acc, lam, mu, rinv, perms, source_element, pulse, f_near, f_far)
    f_near2, f_far2 = both_ways(f_one, f_two)
    a_one, a_two, a_vel1, a_stress1, a_acc2, first, f_acc2, f_early = call(
        adjoint_middle_kernel,
        [V] * 16 + [S] * 2,
        (sends(6), sends(6), field(3), field(6), field(3), shape(2, 384, 128), field(3), field(9)),
        [scr(field(3)), scr(field(9)), HALO, scr(field(9))] + JUMPS,
        2 * 10**8, 8 * 10**6,
    )(a_vel, a_stress, a_acc, lam, mu, rinv, perms, injected, a_near, a_far, f_near, f_far, f_plain, f_acc1, f_stress1, f_vel1, source_element, pulse)
    a_near2, a_far2 = both_ways(a_one, a_two)
    keep, send = call(
        last_image_kernel,
        [V] * 8,
        (shape(8, 16, 384), shape(8, 16, 384)),
        [HALO, pltpu.VMEM((2, 2, 3, 5, 8, 128), f32), pltpu.VMEM((2, 2, 6, 5, 8, 128), f32), scr(shape(2, 384, 128))],
        1000, 1000,
    )(f_acc2, f_early, adj_vel_end, end_grads, first, rinv, f_near2, f_far2)
    early_step = call(
        early_kernel,
        [V] * 4 + [pl.BlockSpec(memory_space=pl.ANY)],
        (field(3), field(9)),
        JUMPS,
        10**8, 8 * 10**6,
    )
    gradient, (early_vel, early) = reduce_over_shots(
        keep, send, lambda held: early_step(a_vel1, a_acc2, perms, injected, held)
    )
    adjoint_end = call(
        last_kernel,
        [V] * 11,
        shape(1125, 2, 128),
        [scr(field(3)), scr(field(6)), HALO]
        + [pltpu.VMEM((2, k, 2, 5, 8, 128), f32) for k in (3, 6, 3)]
        + [scr(shape(1125, 2, 128)), pltpu.SemaphoreType.DMA((9,))],
        10**8, 8 * 10**6,
        pl.BlockSpec(memory_space=pltpu.HBM),
    )(early_vel, early, a_stress1, lam, mu, rinv, perms, a_near2, a_far2, f_near, f_far)
    return gradient.reshape(5, 5, 5, 3, 16).transpose(3, 0, 1, 2, 4), adjoint_end.reshape(1, 9, 5, 5, 5, N)


def solution(mesh):
    return jax.shard_map(
        body,
        mesh=mesh,
        in_specs=(
            P("shot", None, None, None, None, "slab"),
            P("shot", None, None, None, None, "slab"),
            P(None, None, None, None, "slab"),
            P(),
            P("shot"),
            P("shot", None, None),
            P(),
            P("shot", None, None, None),
        ),
        out_specs=(
            P(None, None, None, None, ("slab", "shot")),
            P("shot", None, None, None, None, "slab"),
        ),
        check_vma=False,
    )
```
